32 devices in a mesh: dp: 4 (over y, core), expert: 8 (over z, x).
Axes of the slice: x: 2, y: 2, z: 4, core: 2. Of those that a mesh axis runs over, the one named last changes fastest.
Arguments:
- x_in: bfloat16 [12608, 512], P(('dp', 'expert')), may hold values from -6 to 6
- norm_gains: bfloat16 [2, 2, 512], P(None, None, ('dp', 'expert')), may hold values from 0.099609375 to 1.8984375
- norm_biases: bfloat16 [2, 2, 512], P(None, None, ('dp', 'expert')), may hold values from -3 to 3
- w_qkv: bfloat16 [2, 512, 1536], P(None, ('dp', 'expert')), may hold values from -0.375 to 0.375
- w_o: bfloat16 [2, 512, 512], P(None, ('dp', 'expert')), may hold values from -1 to 1
- w_router: bfloat16 [2, 512, 8], P(None, ('dp', 'expert')), may hold values from -0.5 to 0.5
- w_in: bfloat16 [2, 8, 512, 2048], P(None, 'expert'), may hold values from -0.25 to 0.25
- w_out: bfloat16 [2, 8, 2048, 512], P(None, 'expert'), may hold values from -0.1875 to 0.1875
- routes: int32 [2, 12608, 2], P(None, ('dp', 'expert')), may hold values from 0 to 7, all different within a row; in each aligned block of 394 rows (0 to 393, 394 to 787, ..., all dimensions but the last counted through in order) at most 197 rows name the same one
- threshold: float32 [2, 8], replicated, may hold values from 4 to 20
- cotangent: bfloat16 [12608, 512], P(('dp', 'expert')), may hold values from -6 to 6
Outputs:
- out_act: float32 [12608, 512], P(('dp', 'expert'))
- grad_x: float32 [12608, 512], P(('dp', 'expert'))
- grad_norm_gains: float32 [2, 2, 512], P(None, None, ('dp', 'expert'))
- grad_norm_biases: float32 [2, 2, 512], P(None, None, ('dp', 'expert'))
- grad_w_qkv: float32 [2, 512, 1536], P(None, ('dp', 'expert'))
- grad_w_o: float32 [2, 512, 512], P(None, ('dp', 'expert'))
- grad_w_router: float32 [2, 512, 8], P(None, ('dp', 'expert'))
- grad_w_in: float32 [2, 8, 512, 2048], P(None, 'expert', None, 'dp')
- grad_w_out: float32 [2, 8, 2048, 512], P(None, 'expert', 'dp')
- head_max: float32 [2, 8], replicated
- clipped_qk: float32 [2, 512, 1024], P(None, ('dp', 'expert'))
- grad_second_biases: float32 [2, 512], P(None, ('dp', 'expert'))
The draws below stay inside these ranges and needn't reach their ends.
Inputs may be any that keep to these rules, and one draw needn't show every extreme that they name: `routes`: each row names 2 different experts. In each layer no expert is named by more than 197 of the rows of one device, and on some device some expert is named by exactly 197 of them.
All inputs are finite; a program needn't handle non-finite values.
Results may differ from the reference program's by a relative error of at most 0.024.
Values may be sent and summed in bfloat16 or wider, within the bound.
No kernel may reach another device: no remote copies, remote signals or barrier semaphores. Data moves between devices by JAX's collectives and lax.ppermute only.
A program may use at most 192 MiB of HBM per device.

```python
import math
import jax
import jax.numpy as jnp
import numpy as np
from jax import lax

D = 512
HEADS = 8
HEAD_DIM = 64
FF = 2048
SEQ = 197
TOP = 2
LAYERS = 2
IMG_DEV = 2
TOK_DEV = 394
TOKENS = 12608
EXPERTS = 8
CAP = 197
N_DP = 4
N_EXPERT = 8


def block_levels(key, shape, pieces, least, largest):
    factor_of, own = 1.0, jax.random.fold_in(key, 6)
    for position, shards_of in pieces:
        heights = jnp.exp(jax.random.uniform(jax.random.fold_in(own, position), (shards_of,), jnp.float32, least / len(pieces), largest / len(pieces)))
        factor_of = factor_of * jnp.repeat(heights, shape[position] // shards_of).reshape([-1 if axis == position else 1 for axis in range(len(shape))])
    return factor_of


def assign_block(own_key, own, number, rows, number_of, top, reach, slope):
    order = jax.random.permutation(own_key, number_of)
    crowded, common = shares(number_of, rows * top, reach, slope, True), shares(number_of, rows * top, reach, slope, False)
    places = jnp.arange(number_of)

    def named(tallies, rotation):
        used = int((tallies > 0).sum())
        fixed = max(1, used // 4)
        passed = fixed + (places - fixed + rotation * (used - fixed)) % max(1, number_of - fixed)
        return jnp.zeros((number_of,), jnp.int32).at[order[jnp.where(places < fixed, places, passed)]].set(jnp.asarray(tallies, jnp.int32))

    tallies = jnp.where(number % 4 == 0, named(crowded, number // 4), named(common, number - number // 4 - 1))
    mixed = jax.random.permutation(jax.random.fold_in(own, 3), number_of)
    source_of, receiver = mixed[0:number_of // 2 * 2:2], mixed[1:number_of // 2 * 2:2]
    slack = jnp.minimum(tallies[source_of] - 1, reach - tallies[receiver]) // 2
    slack = jnp.where((source_of == order[0]) | (receiver == order[0]) | (tallies[receiver] == 0), 0, jnp.maximum(slack, 0))
    passed = jax.random.randint(jax.random.fold_in(own, 4), (number_of // 2,), 0, 1 << 20) % (slack + 1)
    tallies = tallies.at[source_of].add(-passed).at[receiver].add(passed)
    labels = jnp.searchsorted(jnp.cumsum(tallies), jnp.arange(rows * top), side="right").astype(jnp.int32)
    listing = labels.reshape(top, rows).T
    listing = listing[jax.random.permutation(jax.random.fold_in(own, 1), rows)]
    rotation = jax.random.randint(jax.random.fold_in(own, 2), (rows, 1), 0, top)
    return jnp.take_along_axis(listing, (jnp.arange(top)[None, :] + rotation) % top, axis=1)


def shares(number_of, total, bound, slope, full):
    weights = [(1 << 20) // math.isqrt(standing ** slope) + 1 for standing in range(1, number_of + 1)]
    largest = bound if full else min(bound, max(-(-total // number_of), total * weights[0] // sum(weights)))
    least = 1 if total - largest >= number_of - 1 else 0
    given, spare = [largest] + [least] * (number_of - 1), total - largest - least * (number_of - 1)
    while spare > 0:
        movable = [i for i in range(1, number_of) if given[i] < largest] or [i for i in range(1, number_of) if given[i] < bound]
        whole, budget = sum([weights[i] for i in movable]), spare
        for i in movable:
            addition = min(bound - given[i], max(1, budget * weights[i] // whole), spare)
            given[i] = given[i] + addition
            spare = spare - addition
    return np.array(given)


def normal_values(stream_key, extent, width, reach, split=(), held_as=jnp.bfloat16):
    gain = block_levels(stream_key, extent, split, -0.22, 0.18) if split else 1.0
    values = jax.random.normal(stream_key, extent, jnp.float32) * width * gain
    return jnp.minimum(jnp.maximum(values, -reach), reach).astype(held_as)


def setup_inputs(seed: int = 0) -> dict:
    seeds = jax.random.split(jax.random.key(seed), 12)
    x_in = normal_values(seeds[0], (TOKENS, D), 1.0, 6.0, ((0, 32),))
    norm_gains = jnp.clip(1.0 + 0.18 * jax.random.normal(seeds[1], (LAYERS, 2, D), jnp.float32), 0.099609375, 1.8984375).astype(jnp.bfloat16)
    norm_biases = normal_values(seeds[2], (LAYERS, 2, D), 0.5, 3.0, ((2, 32),))
    w_qkv = normal_values(seeds[3], (LAYERS, D, 3 * D), (D // 2) ** -0.5, 0.375, ((1, 32),))
    w_o = normal_values(seeds[4], (LAYERS, D, D), (D // 16) ** -0.5, 1.0, ((1, 32),))
    w_router = normal_values(seeds[5], (LAYERS, D, EXPERTS), (D // 4) ** -0.5, 0.5, ((1, 32),))
    w_in = normal_values(seeds[6], (LAYERS, EXPERTS, D, FF), D ** -0.5, 0.25, ((1, 8),))
    w_out = normal_values(seeds[7], (LAYERS, EXPERTS, FF, D), (FF // 2) ** -0.5, 0.1875, ((1, 8),))
    routes_keys = jax.random.split(jax.random.fold_in(seeds[8], 1), LAYERS * TOKENS // TOK_DEV)
    routes_turns = jax.random.permutation(jax.random.fold_in(seeds[8], 3), LAYERS * TOKENS // TOK_DEV)
    routes = jax.vmap(lambda own, number: assign_block(jax.random.fold_in(seeds[8], 2), own, number, TOK_DEV, EXPERTS, TOP, CAP, 2))(routes_keys, routes_turns).reshape((LAYERS, TOKENS, TOP))
    threshold = jnp.clip(jnp.exp(jax.random.uniform(seeds[9], (LAYERS, HEADS), jnp.float32, math.log(4.0), math.log(20.0))), 4.0, 20.0)
    cotangent = normal_values(seeds[10], (TOKENS, D), 1.0, 6.0, ((0, 32),))
    return dict(x_in=x_in, norm_gains=norm_gains, norm_biases=norm_biases, w_qkv=w_qkv, w_o=w_o, w_router=w_router, w_in=w_in, w_out=w_out, routes=routes, threshold=threshold, cotangent=cotangent)


HIGHEST = lax.Precision.HIGHEST

@jax.custom_vjp
def low(v):
    return lax.optimization_barrier(v.astype(jnp.bfloat16)).astype(jnp.float32)

@jax.custom_vjp
def low_back(v):
    return v

def low_keep(v):
    return (low(v), None)

def low_pass(kept, grad):
    return (grad,)

def back_keep(v):
    return (v, None)

def back_low(kept, grad):
    return (low(grad),)
low.defvjp(low_keep, low_pass)
low_back.defvjp(back_keep, back_low)

def layer_norm(values, gain_row, shift_row):
    center = values - lax.optimization_barrier(jnp.mean(values, axis=-1, keepdims=True))
    spread = lax.optimization_barrier(jnp.mean(center * center, axis=-1, keepdims=True))
    return center * lax.rsqrt(spread + 1e-06) * gain_row + shift_row

def slot_places(route_rows):
    matches = (route_rows[:, None] == jnp.arange(EXPERTS, dtype=jnp.int32)[None, :]).astype(jnp.int32)
    before = jnp.cumsum(matches, axis=0) - matches
    return lax.optimization_barrier(jnp.sum(before * matches, axis=1)).astype(jnp.int32)

def attend_block(packed):
    by_head = packed.reshape(IMG_DEV, SEQ, 3, HEADS, HEAD_DIM)
    queries = by_head[:, :, 0]
    keys_in = by_head[:, :, 1]
    values_in = by_head[:, :, 2]
    scores = low_back(jnp.einsum('bqhd,bkhd->bhqk', queries, keys_in, precision=HIGHEST) * HEAD_DIM ** (-0.5))
    head_top = lax.optimization_barrier(jnp.max(scores, axis=(0, 2, 3)))
    router_probs = low(jax.nn.softmax(scores, axis=-1))
    mixed_rows = jnp.einsum('bhqk,bkhd->bqhd', router_probs, values_in, precision=HIGHEST)
    return (mixed_rows.reshape(IMG_DEV * SEQ, HEADS * HEAD_DIM), head_top)

def expert_apply(members):
    rows_in, weight_in, weight_out = members
    hidden = low_back(jnp.dot(rows_in, weight_in, precision=HIGHEST))
    active = low(jax.nn.gelu(hidden))
    return low(low_back(jnp.dot(active, weight_out, precision=HIGHEST)))

def layer_forward(values, gain_rows, biases, weight_qkv, weight_o, weight_router, weight_in, weight_out, route_rows, places):
    devices = N_DP * N_EXPERT
    normed_one = low(layer_norm(values, gain_rows[0], biases[0]))
    packed = low(low_back(jnp.dot(normed_one, weight_qkv, precision=HIGHEST)))
    blocks = packed.reshape(devices, IMG_DEV * SEQ, 3 * D)
    mixed_rows, head_tops = lax.map(jax.checkpoint(attend_block), blocks)
    mixed_rows = low(low_back(mixed_rows.reshape(TOKENS, D)))
    middle = values + low_back(jnp.dot(mixed_rows, weight_o, precision=HIGHEST))
    normed_two = low(layer_norm(middle, gain_rows[1], biases[1]))
    logits = low_back(jnp.dot(normed_two, weight_router, precision=HIGHEST))
    router_probs = jax.nn.softmax(logits, axis=-1)
    picked = jnp.take_along_axis(router_probs, route_rows, axis=1)
    gate_values = picked / lax.optimization_barrier(jnp.sum(picked, axis=1, keepdims=True))
    copies = low_back(jnp.repeat(normed_two, TOP, axis=0))
    buffer = jnp.zeros((EXPERTS * devices * CAP, D), jnp.float32).at[places].set(copies)
    produced = lax.map(jax.checkpoint(expert_apply), (buffer.reshape(EXPERTS, devices * CAP, D), weight_in, weight_out))
    routed = produced.reshape(EXPERTS * devices * CAP, D)[places].reshape(TOKENS, TOP, D)
    return (middle + lax.optimization_barrier(jnp.sum(gate_values[:, :, None] * routed, axis=1)), lax.optimization_barrier(jnp.max(head_tops, axis=0)))

def reference(x_in, norm_gains, norm_biases, w_qkv, w_o, w_router, w_in, w_out, routes, threshold, cotangent):
    devices = N_DP * N_EXPERT
    blocks = routes.reshape(LAYERS, devices, TOK_DEV * TOP)
    slot_rows = jax.vmap(jax.vmap(slot_places))(blocks)
    owners = jnp.arange(devices, dtype=jnp.int32)[None, :, None]
    places = ((blocks * devices + owners) * CAP + slot_rows).reshape(LAYERS, TOKENS * TOP).astype(jnp.int32)

    def forward(values, gain_rows, biases, weight_qkv, weight_o, weight_router, weight_in, weight_out):
        head_tops = []
        for layer_at in range(LAYERS):
            values, head_top = layer_forward(values, gain_rows[layer_at], biases[layer_at], weight_qkv[layer_at], weight_o[layer_at], weight_router[layer_at], weight_in[layer_at], weight_out[layer_at], routes[layer_at], places[layer_at])
            head_tops.append(head_top)
        return (values, jnp.stack(head_tops))
    primals = tuple((member.astype(jnp.float32) for member in (x_in, norm_gains, norm_biases, w_qkv, w_o, w_router, w_in, w_out)))
    out_act, pull_back, head_max = jax.vjp(forward, *primals, has_aux=True)
    gradients = pull_back(cotangent.astype(jnp.float32))
    factor = jnp.sqrt(threshold / jnp.maximum(head_max, threshold))
    columns = jnp.repeat(factor, HEAD_DIM, axis=1)
    clipped_qk = primals[3][:, :, :2 * D] * jnp.concatenate([columns, columns], axis=1)[:, None, :]
    grad_second_biases = gradients[2][:, 1]
    return (out_act, gradients[0], gradients[1], gradients[2], gradients[3], gradients[4], gradients[5], gradients[6], gradients[7], head_max, clipped_qk, grad_second_biases)
```

```python
import functools

import jax
import jax.numpy as jnp
import numpy as np
from jax import lax
from jax.experimental import pallas as pl
from jax.experimental.pallas import tpu as pltpu
from jax.sharding import Mesh
from jax.sharding import PartitionSpec as P

HEADS = 8
HEAD_DIM = 64
SEQ = 197
TOP = 2
LAYERS = 2
EPSILON = 1e-06
BF = jnp.bfloat16
F32 = jnp.float32
LANES = 128
PIECES = 4
VMEM = 50 * 1024 * 1024


def up16(size):
    return -(-size // 16) * 16


def dot(a, b):
    return jnp.dot(a, b, preferred_element_type=F32)


def dot_last(a, b):
    return lax.dot_general(a, b, (((1,), (1,)), ((), ())), preferred_element_type=F32)


def dot_first(a, b):
    return lax.dot_general(a, b, (((0,), (0,)), ((), ())), preferred_element_type=F32)


def lane_of(rows, lanes=LANES):
    return lax.broadcasted_iota(jnp.int32, (rows, lanes), 1)


def row_of(rows, lanes=LANES):
    return lax.broadcasted_iota(jnp.int32, (rows, lanes), 0)


def normalize(values):
    center = values - jnp.mean(values, axis=-1, keepdims=True)
    inverse = lax.rsqrt(jnp.mean(center * center, axis=-1, keepdims=True) + EPSILON)
    return center * inverse, inverse


def norm_backward(upstream, normed, inverse, gain_row):
    scaled = upstream * gain_row
    mean_plain = jnp.mean(scaled, axis=-1, keepdims=True)
    mean_normed = jnp.mean(scaled * normed, axis=-1, keepdims=True)
    return inverse * (scaled - mean_plain - normed * mean_normed)


def norm_rows(tail, experts):
    picks = (lane_of(8) == row_of(8) + experts).astype(F32).astype(BF)
    return dot_last(picks, tail)


def places_kernel(experts, capacity, cols_ref, rows_ref, *out_refs):
    tokens = cols_ref.shape[1]
    slots = experts * capacity
    square_row = lax.broadcasted_iota(jnp.int32, (tokens, tokens), 0)
    square_col = lax.broadcasted_iota(jnp.int32, (tokens, tokens), 1)
    earlier = (square_col < square_row).astype(F32).astype(BF)
    later = (square_row < square_col).astype(F32).astype(BF)
    wide = max(16, experts)
    for layer_at in range(LAYERS):
        to_tokens, to_slots = out_refs[4 * layer_at : 4 * layer_at + 2], out_refs[
            4 * layer_at + 2 : 4 * layer_at + 4
        ]
        cols = cols_ref[layer_at]
        first, second = cols[:, 0:1], cols[:, 1:2]
        lane = lane_of(tokens)
        matches = jnp.where((lane == first) | (lane == second), 1.0, 0.0)
        before = dot(earlier, matches.astype(BF))
        slot_lane = lax.broadcasted_iota(jnp.int32, (tokens, slots), 1)
        for chosen, out_ref in zip((first, second), to_tokens):
            rank = jnp.sum(jnp.where(lane == chosen, before, 0.0), axis=1, keepdims=True)
            slot = chosen * capacity + rank.astype(jnp.int32)
            out_ref[...] = jnp.where(slot_lane == slot, 1.0, 0.0).astype(BF)
        rows = rows_ref[layer_at]
        first, second = rows[0:1], rows[1:2]
        which = lax.broadcasted_iota(jnp.int32, (wide, tokens), 0)
        matches = jnp.where((which == first) | (which == second), 1.0, 0.0)
        before = dot(matches.astype(BF), later)
        slot_row = lax.broadcasted_iota(jnp.int32, (slots, tokens), 0)
        for chosen, out_ref in zip((first, second), to_slots):
            rank = jnp.sum(jnp.where(which == chosen, before, 0.0), axis=0, keepdims=True)
            slot = chosen * capacity + rank.astype(jnp.int32)
            out_ref[...] = jnp.where(slot_row == slot, 1.0, 0.0).astype(BF)


def call(kernel, out_shapes, args, flops, scratch=()):
    moved = sum(a.size * a.dtype.itemsize for a in args) + sum(
        int(np.prod(o.shape)) * o.dtype.itemsize for o in out_shapes
    )
    return pl.pallas_call(
        kernel,
        out_shape=out_shapes,
        scratch_shapes=list(scratch),
        compiler_params=pltpu.CompilerParams(vmem_limit_bytes=VMEM),
        cost_estimate=pl.CostEstimate(
            flops=int(flops), bytes_accessed=int(moved), transcendentals=0
        ),
    )(*args)


def shape(dims, dtype):
    return jax.ShapeDtypeStruct(dims, dtype)


def half_masks():
    lane = lane_of(1)
    return (
        jnp.where(lane < HEAD_DIM, 1.0, 0.0).astype(BF),
        jnp.where(lane < HEAD_DIM, 0.0, 1.0).astype(BF),
    )


def dense_forward_kernel(experts, images, combine, last, *refs):
    refs = list(refs)
    take = lambda: refs.pop(0)
    x_ref = take()
    if combine:
        back_ref, take_first, take_second, gates_before = take(), take(), take(), take()
    full_ref, to_first, to_second, cols_ref = take(), take(), take(), take()
    if last:
        cot_ref = take()
    if combine:
        x_out, first_out, second_out = take(), take(), take()
    x1_out, qkv_out, mixed_out, lse_out, probs_out, gates_out, send_out, top_out = (
        take() for _ in range(8)
    )
    if last:
        send_grad_out = take()
    tokens, width = x_ref.shape
    rows_of = tokens // images
    x = x_ref[...]
    if combine:
        back = back_ref[...]
        first = dot(take_first[...], back)
        second = dot(take_second[...], back)
        gates = gates_before[...]
        x = x + (gates[:, 0:1] * first + gates[:, 1:2] * second)
        x_out[...] = x
        first_out[...] = first.astype(BF)
        second_out[...] = second.astype(BF)
    tail = full_ref[:, 4 * width :]
    norms = norm_rows(tail, experts)
    unit, _ = normalize(x)
    n1 = (unit * norms[0:1] + norms[2:3]).astype(BF)
    qkv_out[...] = dot(n1, full_ref[:, : 3 * width]).astype(BF)
    masks = half_masks()
    key_at = lax.broadcasted_iota(jnp.int32, (rows_of, rows_of), 1)
    query_at = lax.broadcasted_iota(jnp.int32, (rows_of, 1), 0)
    lane = lane_of(rows_of)
    top_lane = lane_of(8)
    tops = jnp.full((8, LANES), -jnp.inf, F32)
    scale = HEAD_DIM**-0.5
    for image in range(images):
        rows = slice(image * rows_of, (image + 1) * rows_of)
        lse = jnp.zeros((rows_of, LANES), F32)
        for pair in range(HEADS // 2):
            at = pair * LANES
            q = qkv_out[rows, at : at + LANES]
            k = qkv_out[rows, width + at : width + at + LANES]
            v = qkv_out[rows, 2 * width + at : 2 * width + at + LANES]
            mixed = None
            for half in range(2):
                scores = dot_last(q * masks[half], k) * scale
                scores = jnp.where(key_at < SEQ, scores, -jnp.inf)
                highest = jnp.max(scores, axis=-1, keepdims=True)
                top = jnp.max(
                    jnp.where(query_at < SEQ, highest, -jnp.inf), axis=0, keepdims=True
                )
                weights = jnp.exp(scores - highest)
                total = jnp.sum(weights, axis=-1, keepdims=True)
                weights = (weights * (1.0 / total)).astype(BF)
                part = dot(weights, v * masks[half])
                mixed = part if mixed is None else mixed + part
                head = 2 * pair + half
                lse = jnp.where(lane == head, highest + jnp.log(total), lse)
                tops = jnp.where(top_lane == head, jnp.maximum(tops, top), tops)
            mixed_out[rows, at : at + LANES] = mixed.astype(BF)
        lse_out[rows, :] = lse
    top_out[...] = tops
    x1 = x + dot(mixed_out[...], full_ref[:, 3 * width : 4 * width])
    x1_out[...] = x1
    unit, _ = normalize(x1)
    n2 = (unit * norms[1:2] + norms[3:4]).astype(BF)
    lane = lane_of(tokens)
    logits = jnp.where(lane < experts, dot(n2, tail), -jnp.inf)
    probs = jnp.exp(logits - jnp.max(logits, axis=-1, keepdims=True))
    probs = probs / jnp.sum(probs, axis=-1, keepdims=True)
    probs_out[...] = probs
    first, second = cols_ref[:, 0:1], cols_ref[:, 1:2]
    picked = [
        jnp.sum(jnp.where(lane == chosen, probs, 0.0), axis=1, keepdims=True)
        for chosen in (first, second)
    ]
    total = jnp.where(first >= 0, picked[0] + picked[1], 1.0)
    gates = [one / total for one in picked]
    packed = jnp.zeros((tokens, LANES), F32)
    for at, column in enumerate((gates[0], gates[1], total, picked[0], picked[1])):
        packed = jnp.where(lane == at, column, packed)
    gates_out[...] = packed
    send_out[...] = (dot(to_first[...], n2) + dot(to_second[...], n2)).astype(BF)
    if last:
        cot = cot_ref[...]
        send_grad_out[...] = (
            dot(to_first[...], (gates[0] * cot).astype(BF))
            + dot(to_second[...], (gates[1] * cot).astype(BF))
        ).astype(BF)


def expert_forward_kernel(rows_ref, win_ref, wout_ref, active_out, slope_out, out_ref, sums):
    at = pl.program_id(0)
    chunk = rows_ref.shape[0] // 4
    factor = (2.0 / np.pi) ** 0.5

    @pl.loop(0, 4)
    def _(step):
        rows = pl.ds(pl.multiple_of(step * chunk, 16), chunk)
        hidden = dot(rows_ref[rows, :], win_ref[...])
        square = hidden * hidden
        bend = jnp.tanh(factor * hidden * (1.0 + 0.044715 * square))
        half = 0.5 * (1.0 + bend)
        active = (hidden * half).astype(BF)
        active_out[rows, :] = active
        slope_out[rows, :] = (
            half
            + (0.5 * factor)
            * hidden
            * (1.0 - bend * bend)
            * (1.0 + (3 * 0.044715) * square)
        ).astype(BF)
        part = dot(active, wout_ref[...])

        @pl.when(at == 0)
        def _():
            sums[rows, :] = part

        @pl.when(at > 0)
        def _():
            sums[rows, :] += part

        @pl.when(at == PIECES - 1)
        def _():
            out_ref[rows, :] = sums[rows, :].astype(BF)


def expert_forward(rows_in, weight_in, weight_out):
    slots, width = rows_in.shape
    hidden_units = weight_in.shape[1]
    block = hidden_units // PIECES
    return pl.pallas_call(
        expert_forward_kernel,
        grid=(PIECES,),
        in_specs=[
            pl.BlockSpec((slots, width), lambda i: (0, 0)),
            pl.BlockSpec((width, block), lambda i: (0, i)),
            pl.BlockSpec((block, width), lambda i: (i, 0)),
        ],
        out_specs=[
            pl.BlockSpec((slots, block), lambda i: (0, i)),
            pl.BlockSpec((slots, block), lambda i: (0, i)),
            pl.BlockSpec((slots, width), lambda i: (0, 0)),
        ],
        out_shape=[
            shape((slots, hidden_units), BF),
            shape((slots, hidden_units), BF),
            shape((slots, width), BF),
        ],
        scratch_shapes=[pltpu.VMEM((slots, width), F32)],
        compiler_params=pltpu.CompilerParams(vmem_limit_bytes=VMEM),
        cost_estimate=pl.CostEstimate(
            flops=4 * slots * width * hidden_units,
            bytes_accessed=slots * (hidden_units * 4 + width * 4) + 4 * width * hidden_units,
            transcendentals=slots * hidden_units,
        ),
    )(rows_in, weight_in, weight_out)


def expert_backward_kernel(grad_ref, slope_ref, win_ref, wout_ref, hidden_out, out_ref, sums):
    at = pl.program_id(0)
    chunk = grad_ref.shape[0] // 4

    @pl.loop(0, 4)
    def _(step):
        rows = pl.ds(pl.multiple_of(step * chunk, 16), chunk)
        grad_active = dot_last(grad_ref[rows, :], wout_ref[...])
        grad_hidden = (grad_active * slope_ref[rows, :].astype(F32)).astype(BF)
        hidden_out[rows, :] = grad_hidden
        part = dot_last(grad_hidden, win_ref[...])

        @pl.when(at == 0)
        def _():
            sums[rows, :] = part

        @pl.when(at > 0)
        def _():
            sums[rows, :] += part

        @pl.when(at == PIECES - 1)
        def _():
            out_ref[rows, :] = sums[rows, :].astype(BF)


def expert_backward(grad_rows, slope, weight_in, weight_out):
    slots, width = grad_rows.shape
    hidden_units = weight_in.shape[1]
    block = hidden_units // PIECES
    return pl.pallas_call(
        expert_backward_kernel,
        grid=(PIECES,),
        in_specs=[
            pl.BlockSpec((slots, width), lambda i: (0, 0)),
            pl.BlockSpec((slots, block), lambda i: (0, i)),
            pl.BlockSpec((width, block), lambda i: (0, i)),
            pl.BlockSpec((block, width), lambda i: (i, 0)),
        ],
        out_specs=[
            pl.BlockSpec((slots, block), lambda i: (0, i)),
            pl.BlockSpec((slots, width), lambda i: (0, 0)),
        ],
        out_shape=[shape((slots, hidden_units), BF), shape((slots, width), BF)],
        scratch_shapes=[pltpu.VMEM((slots, width), F32)],
        compiler_params=pltpu.CompilerParams(vmem_limit_bytes=VMEM),
        cost_estimate=pl.CostEstimate(
            flops=4 * slots * width * hidden_units,
            bytes_accessed=slots * (hidden_units * 4 + width * 4) + 4 * width * hidden_units,
            transcendentals=0,
        ),
    )(grad_rows, slope, weight_in, weight_out)


def expert_weights_kernel(rows_ref, hidden_ref, active_ref, grad_ref, in_out, out_out):
    in_out[0] = dot_first(rows_ref[...], hidden_ref[...]).astype(BF)
    out_out[0] = dot_first(active_ref[...], grad_ref[...]).astype(BF)


def expert_weights(rows_in, grad_hidden, active, grad_rows, pieces):
    slots, width = rows_in.shape
    hidden_units = active.shape[1]
    block = hidden_units // pieces
    return pl.pallas_call(
        expert_weights_kernel,
        grid=(pieces,),
        in_specs=[
            pl.BlockSpec((slots, width), lambda i: (0, 0)),
            pl.BlockSpec((slots, block), lambda i: (0, i)),
            pl.BlockSpec((slots, block), lambda i: (0, i)),
            pl.BlockSpec((slots, width), lambda i: (0, 0)),
        ],
        out_specs=[
            pl.BlockSpec((1, width, block), lambda i: (i, 0, 0)),
            pl.BlockSpec((1, block, width), lambda i: (i, 0, 0)),
        ],
        out_shape=[shape((pieces, width, block), BF), shape((pieces, block, width), BF)],
        compiler_params=pltpu.CompilerParams(vmem_limit_bytes=VMEM),
        cost_estimate=pl.CostEstimate(
            flops=4 * slots * width * hidden_units,
            bytes_accessed=slots * (hidden_units * 4 + width * 4) + 4 * width * hidden_units,
            transcendentals=0,
        ),
    )(rows_in, grad_hidden, active, grad_rows)


def dense_backward_kernel(experts, images, last, first_layer, *refs):
    refs = list(refs)
    take = lambda: refs.pop(0)
    g_ref, rows_ref, take_first, take_second = take(), take(), take(), take()
    if last:
        out_rows_ref = take()
    else:
        first_ref, second_ref = take(), take()
    probs_ref, gates_ref, cols_ref, x_ref, x1_ref = (take() for _ in range(5))
    full_ref, qkv_ref, mixed_ref, lse_ref = (take() for _ in range(4))
    if not first_layer:
        to_first, to_second, gates_below = take(), take(), take()
    g_out, weights_out = take(), take()
    if not first_layer:
        send_out = take()
    if last:
        act_out = take()
    grad_qkv = take()
    tokens, width = g_ref.shape
    rows_of = tokens // images
    g = g_ref[...]
    gates = gates_ref[...]
    x1 = x1_ref[...]
    if last:
        out_rows = out_rows_ref[...]
        first = dot(take_first[...], out_rows)
        second = dot(take_second[...], out_rows)
        act_out[...] = x1 + (gates[:, 0:1] * first + gates[:, 1:2] * second)
    else:
        first = first_ref[...].astype(F32)
        second = second_ref[...].astype(F32)
    grad_gates = [jnp.sum(g * one, axis=1, keepdims=True) for one in (first, second)]
    weighted = grad_gates[0] * gates[:, 0:1] + grad_gates[1] * gates[:, 1:2]
    amounts = [
        (grad_gates[at] - weighted) / gates[:, 2:3] * gates[:, 3 + at : 4 + at]
        for at in range(TOP)
    ]
    lane = lane_of(tokens)
    chosen = [jnp.where(lane == cols_ref[:, at : at + 1], amounts[at], 0.0) for at in range(TOP)]
    grad_logits = (
        (chosen[0] + chosen[1]) - probs_ref[...] * (amounts[0] + amounts[1])
    ).astype(BF)
    tail = full_ref[:, 4 * width :]
    norms = norm_rows(tail, experts)
    rows = rows_ref[...]
    grad_n2 = (
        dot(take_first[...], rows) + dot(take_second[...], rows) + dot_last(grad_logits, tail)
    )
    unit2, inverse2 = normalize(x1)
    n2 = (unit2 * norms[1:2] + norms[3:4]).astype(BF)
    grad_x1 = g + norm_backward(grad_n2, unit2, inverse2, norms[1:2])
    grad_attn = grad_x1.astype(BF)
    grad_mixed = dot_last(grad_attn, full_ref[:, 3 * width : 4 * width]).astype(BF)
    masks = half_masks()
    key_at = lax.broadcasted_iota(jnp.int32, (rows_of, rows_of), 1)
    scale = HEAD_DIM**-0.5
    for image in range(images):
        rows = slice(image * rows_of, (image + 1) * rows_of)
        for pair in range(HEADS // 2):
            at = pair * LANES
            q = qkv_ref[rows, at : at + LANES]
            k = qkv_ref[rows, width + at : width + at + LANES]
            v = qkv_ref[rows, 2 * width + at : 2 * width + at + LANES]
            gm = grad_mixed[rows, at : at + LANES]
            sums = [None] * 3
            for half in range(2):
                head = 2 * pair + half
                mask = masks[half]
                scores = dot_last(q * mask, k) * scale
                weights = jnp.exp(scores - lse_ref[rows, head : head + 1])
                weights = jnp.where(key_at < SEQ, weights, 0.0)
                grad_weights = dot_last(gm * mask, v)
                inner = jnp.sum(grad_weights * weights, axis=-1, keepdims=True)
                grad_scores = (weights * (grad_weights - inner)).astype(BF)
                parts = (
                    dot(grad_scores, k * mask),
                    dot_first(grad_scores, q * mask),
                    dot_first(weights.astype(BF), gm * mask),
                )
                sums = [b if a is None else a + b for a, b in zip(sums, parts)]
            grad_qkv[rows, at : at + LANES] = (sums[0] * scale).astype(BF)
            grad_qkv[rows, width + at : width + at + LANES] = (sums[1] * scale).astype(BF)
            grad_qkv[rows, 2 * width + at : 2 * width + at + LANES] = sums[2].astype(BF)
    unit1, inverse1 = normalize(x_ref[...])
    n1 = (unit1 * norms[0:1] + norms[2:3]).astype(BF)
    grad_n1 = dot_last(grad_qkv[...], full_ref[:, : 3 * width])
    g_below = grad_x1 + norm_backward(grad_n1, unit1, inverse1, norms[0:1])
    g_out[...] = g_below
    if not first_layer:
        gates = gates_below[...]
        send_out[...] = (
            dot(to_first[...], (gates[:, 0:1] * g_below).astype(BF))
            + dot(to_second[...], (gates[:, 1:2] * g_below).astype(BF))
        ).astype(BF)
    weights_out[:, : 3 * width] = dot_first(n1, grad_qkv[...]).astype(BF)
    weights_out[:, 3 * width : 4 * width] = dot_first(mixed_ref[...], grad_attn).astype(BF)
    row = lax.broadcasted_iota(jnp.int32, (8, width), 0)
    norm_grads = jnp.zeros((8, width), F32)
    for at, total in enumerate((grad_n1 * unit1, grad_n2 * unit2, grad_n1, grad_n2)):
        norm_grads = jnp.where(row == at, jnp.sum(total, axis=0, keepdims=True), norm_grads)
    picks = (lane_of(8) == row_of(8) + experts).astype(F32).astype(BF)
    weights_out[:, 4 * width :] = (
        dot_first(n2, grad_logits) + dot_first(norm_grads.astype(BF), picks)
    ).astype(BF)


def other(values, axis):
    return lax.ppermute(values, axis, [(0, 1), (1, 0)])


def across(values, core_axis, axis):
    if axis < core_axis:
        return lax.ppermute(values, (axis, core_axis), [(1, 3), (3, 1)])
    return lax.ppermute(values, (core_axis, axis), [(2, 3), (3, 2)])


def expert_moved(weight, split_at, dp_axes, ex_axes):
    row_axes, core_axis = dp_axes[:-1], dp_axes[-1]
    count = 2 ** len(row_axes)
    size = weight.shape[split_at] // count
    place = lax.axis_index(row_axes) if row_axes else 0
    own = [
        lax.dynamic_slice_in_dim(weight, (place ^ p) * size, size, split_at)
        for p in range(count)
    ]
    first = lax.axis_index(core_axis) == 0
    got = [across(own[0], core_axis, ex_axes[0])]
    for axis in row_axes[::-1]:
        got = got + [across(one, core_axis, axis) for one in got]
    return jnp.concatenate(
        [jnp.where(first, a, b) for a, b in zip(own, got)], axis=split_at
    )


def expert_returned(pieces, dp_axes, ex_axes):
    row_axes, core_axis = dp_axes[:-1], dp_axes[-1]
    pieces = pieces.reshape((2,) * len(row_axes) + (2,) + pieces.shape[1:])
    for axis in row_axes:
        pieces = add_low(pieces[0], other(pieces[1], axis))
    moved = across(pieces, core_axis, ex_axes[0])
    core = lax.axis_index(core_axis)
    mine = jnp.where(core == 0, pieces, moved)
    keep = lax.dynamic_index_in_dim(mine, core, 0, keepdims=False)
    send = lax.dynamic_index_in_dim(mine, 1 - core, 0, keepdims=False)
    return keep.astype(F32) + other(send, core_axis).astype(F32)


def add_low(a, b):
    return (a.astype(F32) + b.astype(F32)).astype(BF)


def gather_all(shard, axes, order):
    whole = shard[None]
    for axis in order:
        theirs = other(whole, axis)
        mine_first = lax.axis_index(axis) == 0
        whole = jnp.stack(
            [jnp.where(mine_first, whole, theirs), jnp.where(mine_first, theirs, whole)]
        )
    whole = whole.reshape((2,) * len(axes) + shard.shape)
    places = tuple(order[::-1].index(axis) for axis in axes)
    whole = whole.transpose(places + tuple(range(len(axes), whole.ndim)))
    return whole.reshape((-1,) + shard.shape[1:])


def scatter_sum(values, axes, order):
    left = list(axes)
    values = values.reshape((2,) * len(axes) + (-1,) + values.shape[1:])
    for axis in order:
        at = left.index(axis)
        mine = lax.axis_index(axis)
        keep = lax.dynamic_index_in_dim(values, mine, at, keepdims=False)
        send = lax.dynamic_index_in_dim(values, 1 - mine, at, keepdims=False)
        values = keep.astype(F32) + other(send, axis).astype(F32)
        left.remove(axis)
        if left:
            values = values.astype(BF)
    return values


def body(
    dp_axes,
    ex_axes,
    x_in,
    norm_gains,
    norm_biases,
    w_qkv,
    w_o,
    w_router,
    w_in,
    w_out,
    routes,
    threshold,
    cotangent,
):
    axes = dp_axes + ex_axes
    group = dp_axes[-1:] + ex_axes[1:]
    order_out = ex_axes[::-1][1:] + ex_axes[-1:] + dp_axes
    order_in = dp_axes[::-1] + ex_axes[::-1]
    experts = 2 ** len(ex_axes)
    parts = 2 ** len(dp_axes)
    tokens, width = x_in.shape
    images = tokens // SEQ
    padded = up16(SEQ)
    capacity = up16(4 * tokens // experts)
    slots = experts * capacity
    total = images * padded

    def pad(values, fill=0):
        values = values.reshape((images, SEQ) + values.shape[1:])
        values = jnp.pad(
            values, ((0, 0), (0, padded - SEQ), (0, 0)), constant_values=fill
        )
        return values.reshape((total,) + values.shape[2:])

    def unpad(values):
        return values.reshape(images, padded, -1)[:, :SEQ].reshape(tokens, -1)

    shards = [
        jnp.concatenate(
            [
                w_qkv[at],
                w_o[at],
                w_router[at],
                norm_gains[at].T,
                norm_biases[at].T,
                jnp.zeros((w_o.shape[1], LANES - experts - 4), BF),
            ],
            axis=1,
        )
        for at in range(LAYERS)
    ]
    full = [gather_all(shards[0], axes, order_out)] + [
        lax.all_gather(shards[at], axes, axis=0, tiled=True) for at in range(1, LAYERS)
    ]
    cols = [pad(routes[at], -1) for at in range(LAYERS)]
    shift = lax.axis_index(ex_axes[0]) * (experts // 2)
    route_cols = jnp.stack(
        [pad((routes[at] + shift) % experts, -1) for at in range(LAYERS)]
    )
    weights_in, weights_out = [], []
    for at in range(LAYERS):
        weights_in.append(expert_moved(w_in[at, 0], 1, dp_axes, ex_axes))
        weights_out.append(expert_moved(w_out[at, 0], 0, dp_axes, ex_axes))
    to_and_from = call(
        functools.partial(places_kernel, experts, capacity),
        [shape(s, BF) for s in ((total, slots),) * 2 + ((slots, total),) * 2] * LAYERS,
        (route_cols, route_cols.transpose(0, 2, 1)),
        LAYERS * 4 * total * total * LANES,
    )
    collect = [to_and_from[4 * at : 4 * at + 2] for at in range(LAYERS)]
    spread = [to_and_from[4 * at + 2 : 4 * at + 4] for at in range(LAYERS)]
    cot = pad(cotangent.astype(F32))
    current = pad(x_in.astype(F32))

    def exchange(rows):
        return lax.all_to_all(rows, group, split_axis=0, concat_axis=0, tiled=True)

    dense_flops = 2 * total * width * (4 * width) + 6 * total * slots * width
    kept = []
    tops = []
    back = gates = None
    for at in range(LAYERS):
        combine, last = at > 0, at == LAYERS - 1
        args = [current]
        outs = []
        if combine:
            args += [back, *collect[at - 1], gates]
            outs += [shape((total, width), F32), shape((total, width), BF), shape((total, width), BF)]
        args += [full[at], *spread[at], cols[at]]
        if last:
            args.append(cot)
        outs += [
            shape((total, width), F32),
            shape((total, 3 * width), BF),
            shape((total, width), BF),
            shape((total, LANES), F32),
            shape((total, LANES), F32),
            shape((total, LANES), F32),
            shape((slots, width), BF),
            shape((8, LANES), F32),
        ]
        if last:
            outs.append(shape((slots, width), BF))
        made = list(
            call(
                functools.partial(dense_forward_kernel, experts, images, combine, last),
                outs,
                args,
                dense_flops,
            )
        )
        if combine:
            current, first, second = made[:3]
            made = made[3:]
            kept[-1]["routed"] = (first, second)
        x1, qkv, mixed, lse, probs, gates, send, top = made[:8]
        tops.append(top[0, :HEADS])
        rows = exchange(send)
        if last:
            grad_rows = exchange(made[8])
        active, slope, out_rows = expert_forward(rows, weights_in[at], weights_out[at])
        back = exchange(out_rows)
        kept.append(
            dict(
                x=current,
                x1=x1,
                qkv=qkv,
                mixed=mixed,
                lse=lse,
                probs=probs,
                gates=gates,
                rows=rows,
                active=active,
                slope=slope,
            )
        )
        current = x1
    tops = jnp.pad(jnp.concatenate(tops), (0, LANES - LAYERS * HEADS))
    everyone = 2 ** len(axes)
    tops = lax.all_to_all(
        jnp.broadcast_to(tops, (everyone, LANES)), axes, split_axis=0, concat_axis=0, tiled=True
    )
    head_max = jnp.max(tops, axis=0)[: LAYERS * HEADS].reshape(LAYERS, HEADS)
    upstream = cot
    expert_grads = [None] * LAYERS
    dense_grads = [None] * LAYERS
    for at in reversed(range(LAYERS)):
        own = kept[at]
        last, first_layer = at == LAYERS - 1, at == 0
        grad_hidden, grad_back = expert_backward(
            grad_rows, own["slope"], weights_in[at], weights_out[at]
        )
        grad_back = exchange(grad_back)
        expert_grads[at] = [
            expert_returned(one, dp_axes, ex_axes)
            for one in expert_weights(
                own["rows"], grad_hidden, own["active"], grad_rows, parts
            )
        ]
        args = [upstream, grad_back, *collect[at]]
        if last:
            args.append(back)
        else:
            args += own["routed"]
        args += [own["probs"], own["gates"], cols[at], own["x"], own["x1"]]
        args += [full[at], own["qkv"], own["mixed"], own["lse"]]
        outs = [shape((total, width), F32), shape((width, 4 * width + LANES), BF)]
        if not first_layer:
            args += [*spread[at - 1], kept[at - 1]["gates"]]
            outs.append(shape((slots, width), BF))
        if last:
            outs.append(shape((total, width), F32))
        made = list(
            call(
                functools.partial(dense_backward_kernel, experts, images, last, first_layer),
                outs,
                args,
                2 * dense_flops,
                [pltpu.VMEM((total, 3 * width), BF)],
            )
        )
        upstream, weight_grads = made[:2]
        if not first_layer:
            grad_rows = exchange(made[2])
        if last:
            out_act = made[-1]
        dense_grads[at] = scatter_sum(weight_grads, axes, order_in)
    dense = jnp.stack(dense_grads)
    tail = dense[:, :, 4 * width :]
    grad_norm_gains = tail[:, :, experts : experts + 2].transpose(0, 2, 1)
    grad_norm_biases = tail[:, :, experts + 2 : experts + 4].transpose(0, 2, 1)
    grad_in, grad_out = (
        jnp.stack([expert_grads[at][which] for at in range(LAYERS)])[:, None] for which in range(2)
    )
    factor = jnp.sqrt(threshold / jnp.maximum(head_max, threshold))
    columns = jnp.repeat(factor, HEAD_DIM, axis=1)
    clipped_qk = (
        w_qkv[:, :, : 2 * width].astype(F32)
        * jnp.concatenate([columns, columns], axis=1)[:, None, :]
    )
    return (
        unpad(out_act),
        unpad(upstream),
        grad_norm_gains,
        grad_norm_biases,
        dense[:, :, : 3 * width],
        dense[:, :, 3 * width : 4 * width],
        tail[:, :, :experts],
        grad_in,
        grad_out,
        head_max,
        clipped_qk,
        grad_norm_biases[:, 1],
    )


def solution(mesh):
    dp_bits = int(mesh.shape["dp"]).bit_length() - 1
    ex_bits = int(mesh.shape["expert"]).bit_length() - 1
    dp_axes = tuple(f"d{at}" for at in range(dp_bits))
    ex_axes = tuple(f"e{at}" for at in range(ex_bits))
    split = Mesh(mesh.devices.reshape((2,) * (dp_bits + ex_bits)), dp_axes + ex_axes)
    both = dp_axes + ex_axes
    in_specs = (
        P(both, None),
        P(None, None, both),
        P(None, None, both),
        P(None, both, None),
        P(None, both, None),
        P(None, both, None),
        P(None, ex_axes, None, None),
        P(None, ex_axes, None, None),
        P(None, both, None),
        P(),
        P(both, None),
    )
    out_specs = (
        P(both, None),
        P(both, None),
        P(None, None, both),
        P(None, None, both),
        P(None, both, None),
        P(None, both, None),
        P(None, both, None),
        P(None, ex_axes, None, dp_axes),
        P(None, ex_axes, dp_axes, None),
        P(),
        P(None, both, None),
        P(None, both),
    )
    return jax.shard_map(
        functools.partial(body, dp_axes, ex_axes),
        mesh=split,
        in_specs=in_specs,
        out_specs=out_specs,
        check_vma=False,
    )
```

```python
import functools

import jax
import jax.numpy as jnp
import numpy as np
from jax import lax
from jax.experimental import pallas as pl
from jax.experimental.pallas import tpu as pltpu
from jax.sharding import Mesh
from jax.sharding import PartitionSpec as P

HEADS = 8
HEAD_DIM = 64
SEQ = 197
TOP = 2
LAYERS = 2
EPSILON = 1e-06
BF = jnp.bfloat16
F32 = jnp.float32
LANES = 128
PIECES = 4
VMEM = 56 * 1024 * 1024
MOVED = (False, True)


def up16(size):
    return -(-size // 16) * 16


def dot(a, b):
    return jnp.dot(a, b, preferred_element_type=F32)


def dot_last(a, b):
    return lax.dot_general(a, b, (((1,), (1,)), ((), ())), preferred_element_type=F32)


def dot_first(a, b):
    return lax.dot_general(a, b, (((0,), (0,)), ((), ())), preferred_element_type=F32)


def lane_of(rows, lanes=LANES):
    return lax.broadcasted_iota(jnp.int32, (rows, lanes), 1)


def row_of(rows, lanes=LANES):
    return lax.broadcasted_iota(jnp.int32, (rows, lanes), 0)


def normalize(values):
    center = values - jnp.mean(values, axis=-1, keepdims=True)
    inverse = lax.rsqrt(jnp.mean(center * center, axis=-1, keepdims=True) + EPSILON)
    return center * inverse, inverse


def norm_backward(upstream, normed, inverse, gain_row):
    scaled = upstream * gain_row
    mean_plain = jnp.mean(scaled, axis=-1, keepdims=True)
    mean_normed = jnp.mean(scaled * normed, axis=-1, keepdims=True)
    return inverse * (scaled - mean_plain - normed * mean_normed)


def norm_rows(tail, experts):
    picks = (lane_of(8) == row_of(8) + experts).astype(F32).astype(BF)
    return dot_last(picks, tail)


def places_kernel(experts, capacity, cols_ref, rows_ref, cot_ref, *out_refs):
    tokens = cols_ref.shape[1]
    slots = experts * capacity
    square_row = lax.broadcasted_iota(jnp.int32, (tokens, tokens), 0)
    square_col = lax.broadcasted_iota(jnp.int32, (tokens, tokens), 1)
    earlier = (square_col < square_row).astype(F32).astype(BF)
    later = (square_row < square_col).astype(F32).astype(BF)
    wide = max(16, experts)
    for layer_at in range(LAYERS):
        to_tokens, to_slots = out_refs[4 * layer_at : 4 * layer_at + 2], out_refs[
            4 * layer_at + 2 : 4 * layer_at + 4
        ]
        cols = cols_ref[layer_at]
        first, second = cols[:, 0:1], cols[:, 1:2]
        lane = lane_of(tokens)
        matches = jnp.where((lane == first) | (lane == second), 1.0, 0.0)
        before = dot(earlier, matches.astype(BF))
        slot_lane = lax.broadcasted_iota(jnp.int32, (tokens, slots), 1)
        for chosen, out_ref in zip((first, second), to_tokens):
            rank = jnp.sum(jnp.where(lane == chosen, before, 0.0), axis=1, keepdims=True)
            slot = chosen * capacity + rank.astype(jnp.int32)
            out_ref[...] = jnp.where(slot_lane == slot, 1.0, 0.0).astype(BF)
        rows = rows_ref[layer_at]
        first, second = rows[0:1], rows[1:2]
        which = lax.broadcasted_iota(jnp.int32, (wide, tokens), 0)
        matches = jnp.where((which == first) | (which == second), 1.0, 0.0)
        before = dot(matches.astype(BF), later)
        slot_row = lax.broadcasted_iota(jnp.int32, (slots, tokens), 0)
        for chosen, out_ref in zip((first, second), to_slots):
            rank = jnp.sum(jnp.where(which == chosen, before, 0.0), axis=0, keepdims=True)
            slot = chosen * capacity + rank.astype(jnp.int32)
            out_ref[...] = jnp.where(slot_row == slot, 1.0, 0.0).astype(BF)
    for at, out_ref in enumerate(out_refs[4 * LAYERS :]):
        columns = out_ref.shape[1]
        cot = cot_ref[:, at * columns : (at + 1) * columns]
        out_ref[...] = (dot(to_slots[0][...], cot) + dot(to_slots[1][...], cot)).astype(BF)


def two_parts(values):
    high = values.astype(BF)
    return high, (values - high.astype(F32)).astype(BF)


def two_lanes(values):
    high, low = two_parts(values)
    lane = lane_of(values.shape[0])
    high, low = high.astype(F32), low.astype(F32)
    return jnp.where(lane == 0, high, jnp.where(lane == 1, low, 0.0)).astype(BF)


def from_lanes(parts):
    return parts[:, 0:1] + parts[:, 1:2]


def behind(kernel, operands, *refs):
    return kernel(*refs[operands:])


def call(kernel, out_shapes, args, flops, scratch=(), after=()):
    moved = sum(a.size * a.dtype.itemsize for a in args) + sum(
        int(np.prod(o.shape)) * o.dtype.itemsize for o in out_shapes
    )
    whole = pl.BlockSpec(memory_space=pltpu.VMEM)
    return pl.pallas_call(
        functools.partial(behind, kernel, len(after)),
        in_specs=[pl.BlockSpec(memory_space=pl.ANY)] * len(after) + [whole] * len(args),
        out_shape=out_shapes,
        scratch_shapes=list(scratch),
        compiler_params=pltpu.CompilerParams(vmem_limit_bytes=VMEM),
        cost_estimate=pl.CostEstimate(
            flops=int(flops), bytes_accessed=int(moved), transcendentals=0
        ),
    )(*after, *args)


def shape(dims, dtype):
    return jax.ShapeDtypeStruct(dims, dtype)


def half_masks():
    lane = lane_of(1)
    return (
        jnp.where(lane < HEAD_DIM, 1.0, 0.0).astype(BF),
        jnp.where(lane < HEAD_DIM, 0.0, 1.0).astype(BF),
    )


def dense_forward_kernel(experts, images, combine, last, *refs):
    refs = list(refs)
    take = lambda: refs.pop(0)
    x_ref = take()
    if combine:
        back_ref, take_first, take_second, gates_before = take(), take(), take(), take()
    full_ref, to_first, to_second, cols_ref = take(), take(), take(), take()
    if combine:
        x_out, first_out, second_out = take(), take(), take()
    x1_out, qkv_out, mixed_out, lse_out, probs_out, gates_out, send_out, top_out = (
        take() for _ in range(8)
    )
    if last:
        send_gates_out = take()
    tokens, width = x_ref.shape
    rows_of = tokens // images
    x = x_ref[...]
    if combine:
        back = back_ref[...]
        first = dot(take_first[...], back)
        second = dot(take_second[...], back)
        gates = gates_before[...]
        x = x + (gates[:, 0:1] * first + gates[:, 1:2] * second)
        x_out[...] = x
        first_out[...] = first.astype(BF)
        second_out[...] = second.astype(BF)
    tail = full_ref[:, 4 * width :]
    norms = norm_rows(tail, experts)
    unit, _ = normalize(x)
    n1 = (unit * norms[0:1] + norms[2:3]).astype(BF)
    qkv_out[...] = dot(n1, full_ref[:, : 3 * width]).astype(BF)
    masks = half_masks()
    key_at = lax.broadcasted_iota(jnp.int32, (rows_of, rows_of), 1)
    query_at = lax.broadcasted_iota(jnp.int32, (rows_of, 1), 0)
    lane = lane_of(rows_of)
    top_lane = lane_of(8)
    tops = jnp.full((8, LANES), -jnp.inf, F32)
    scale = HEAD_DIM**-0.5
    for image in range(images):
        rows = slice(image * rows_of, (image + 1) * rows_of)
        lse = jnp.zeros((rows_of, LANES), F32)
        for pair in range(HEADS // 2):
            at = pair * LANES
            q = qkv_out[rows, at : at + LANES]
            k = qkv_out[rows, width + at : width + at + LANES]
            v = qkv_out[rows, 2 * width + at : 2 * width + at + LANES]
            mixed = None
            for half in range(2):
                scores = dot_last(q * masks[half], k) * scale
                scores = jnp.where(key_at < SEQ, scores, -jnp.inf)
                highest = jnp.max(scores, axis=-1, keepdims=True)
                top = jnp.max(
                    jnp.where(query_at < SEQ, highest, -jnp.inf), axis=0, keepdims=True
                )
                weights = jnp.exp(scores - highest)
                total = jnp.sum(weights, axis=-1, keepdims=True)
                weights = (weights * (1.0 / total)).astype(BF)
                part = dot(weights, v * masks[half])
                mixed = part if mixed is None else mixed + part
                head = 2 * pair + half
                lse = jnp.where(lane == head, highest + jnp.log(total), lse)
                tops = jnp.where(top_lane == head, jnp.maximum(tops, top), tops)
            mixed_out[rows, at : at + LANES] = mixed.astype(BF)
        lse_out[rows, :] = lse
    top_out[...] = tops
    x1 = x + dot(mixed_out[...], full_ref[:, 3 * width : 4 * width])
    x1_out[...] = x1
    unit, _ = normalize(x1)
    n2 = (unit * norms[1:2] + norms[3:4]).astype(BF)
    lane = lane_of(tokens)
    logits = jnp.where(lane < experts, dot(n2, tail), -jnp.inf)
    probs = jnp.exp(logits - jnp.max(logits, axis=-1, keepdims=True))
    probs = probs / jnp.sum(probs, axis=-1, keepdims=True)
    probs_out[...] = probs
    first, second = cols_ref[:, 0:1], cols_ref[:, 1:2]
    picked = [
        jnp.sum(jnp.where(lane == chosen, probs, 0.0), axis=1, keepdims=True)
        for chosen in (first, second)
    ]
    total = jnp.where(first >= 0, picked[0] + picked[1], 1.0)
    gates = [one / total for one in picked]
    packed = jnp.zeros((tokens, LANES), F32)
    for at, column in enumerate((gates[0], gates[1], total, picked[0], picked[1])):
        packed = jnp.where(lane == at, column, packed)
    gates_out[...] = packed
    send_out[...] = (dot(to_first[...], n2) + dot(to_second[...], n2)).astype(BF)
    if last:
        send_gates_out[...] = (
            dot(to_first[...], two_lanes(gates[0])) + dot(to_second[...], two_lanes(gates[1]))
        ).astype(BF)


def expert_forward_kernel(last, *refs):
    refs = list(refs)
    if last:
        grad_refs, inner_out = (refs.pop(0), refs.pop(0)), refs.pop()
    rows_ref, win_ref, wout_ref, active_out, slope_out, out_ref = refs
    units = win_ref.shape[1] // 2
    factor = (2.0 / np.pi) ** 0.5
    rows = rows_ref[...]
    hidden = dot(rows, win_ref[:, :units])
    total = before = None
    for piece in range(2):
        at = slice(piece * units, (piece + 1) * units)
        later = dot(rows, win_ref[:, units:]) if piece == 0 else None
        square = hidden * hidden
        gate = 0.5 + 0.5 * jnp.tanh(hidden * (factor + (0.044715 * factor) * square))
        active = hidden * gate
        slope = active * (2 * factor + (6 * 0.044715 * factor) * square)
        slope_out[:, at] = (gate + slope * (1.0 - gate)).astype(BF)
        active = active.astype(BF)
        active_out[:, at] = active
        if piece == 1:
            total = dot(before, wout_ref[:units, :]) + dot(active, wout_ref[units:, :])
        before, hidden = active, later
    total = total.astype(BF)
    out_ref[...] = total
    if last:
        half = total.shape[1] // 2
        inner_out[...] = two_lanes(
            jnp.sum(
                total[:, :half].astype(F32) * grad_refs[0][...].astype(F32)
                + total[:, half:].astype(F32) * grad_refs[1][...].astype(F32),
                axis=1,
                keepdims=True,
            )
        )


def weight_spec(weight, layer_at):
    if weight.ndim == 4:
        return pl.BlockSpec((None, None) + weight.shape[2:], lambda i: (layer_at, 0, 0, 0))
    return pl.BlockSpec(weight.shape, lambda i: (0, 0))


def expert_forward(layer_at, grads, rows_in, weight_in, weight_out, after=()):
    last = len(grads) > 0
    slots, width = rows_in.shape
    hidden_units = weight_in.shape[-1]
    chunk = slots // 4
    return pl.pallas_call(
        functools.partial(behind, functools.partial(expert_forward_kernel, last), len(after)),
        grid=(4,),
        in_specs=[pl.BlockSpec(memory_space=pl.ANY)] * len(after)
        + [pl.BlockSpec((chunk, width // 2), lambda i: (i, 0))] * len(grads)
        + [
            pl.BlockSpec((chunk, width), lambda i: (i, 0)),
            weight_spec(weight_in, layer_at),
            weight_spec(weight_out, layer_at),
        ],
        out_specs=[
            pl.BlockSpec((chunk, hidden_units), lambda i: (i, 0)),
            pl.BlockSpec((chunk, hidden_units), lambda i: (i, 0)),
            pl.BlockSpec((chunk, width), lambda i: (i, 0)),
        ]
        + [pl.BlockSpec((chunk, LANES), lambda i: (i, 0))] * last,
        out_shape=[
            shape((slots, hidden_units), BF),
            shape((slots, hidden_units), BF),
            shape((slots, width), BF),
        ]
        + [shape((slots, LANES), BF)] * last,
        compiler_params=pltpu.CompilerParams(vmem_limit_bytes=VMEM),
        cost_estimate=pl.CostEstimate(
            flops=4 * slots * width * hidden_units,
            bytes_accessed=slots * (hidden_units * 4 + width * 4) + 4 * width * hidden_units,
            transcendentals=slots * hidden_units,
        ),
    )(*after, *grads, rows_in, weight_in, weight_out)


def expert_backward_kernel(gated, *refs):
    refs = list(refs)
    grad_ref = refs.pop(0)
    if gated:
        second_ref, gates_ref, scaled = refs.pop(0), refs.pop(0), refs.pop()
        gates = from_lanes(gates_ref[...].astype(F32))
        half = grad_ref.shape[1]
        scaled[:, :half] = (gates * grad_ref[...].astype(F32)).astype(BF)
        scaled[:, half:] = (gates * second_ref[...].astype(F32)).astype(BF)
        grad_ref = scaled
    slope_ref, win_ref, wout_ref, hidden_out, out_ref = refs
    units = win_ref.shape[1] // PIECES
    for piece in range(PIECES):
        at = slice(piece * units, (piece + 1) * units)
        grad_active = dot_last(grad_ref[...], wout_ref[at, :])
        hidden_out[:, at] = (grad_active * slope_ref[:, at].astype(F32)).astype(BF)
    out_ref[...] = dot_last(hidden_out[...], win_ref[...]).astype(BF)


def expert_backward(layer_at, grads, gates, slope, weight_in, weight_out):
    slots, width = grads[0].shape[0], weight_in.shape[-2]
    hidden_units = weight_in.shape[-1]
    chunk = slots // 4
    gated = len(gates)
    rows_spec = lambda lanes: pl.BlockSpec((chunk, lanes), lambda i: (i, 0))
    return pl.pallas_call(
        functools.partial(expert_backward_kernel, gated),
        grid=(4,),
        in_specs=[rows_spec(one.shape[1]) for one in grads]
        + [rows_spec(LANES)] * gated
        + [
            rows_spec(hidden_units),
            weight_spec(weight_in, layer_at),
            weight_spec(weight_out, layer_at),
        ],
        out_specs=[rows_spec(hidden_units), rows_spec(width)] + [rows_spec(width)] * gated,
        out_shape=[shape((slots, hidden_units), BF), shape((slots, width), BF)]
        + [shape((slots, width), BF)] * gated,
        compiler_params=pltpu.CompilerParams(vmem_limit_bytes=VMEM),
        cost_estimate=pl.CostEstimate(
            flops=4 * slots * width * hidden_units,
            bytes_accessed=slots * (hidden_units * 4 + width * 4) + 4 * width * hidden_units,
            transcendentals=0,
        ),
    )(*grads, *gates, slope, weight_in, weight_out)


def expert_weights_kernel(rows_ref, hidden_ref, active_ref, grad_ref, in_out, out_out):
    in_out[0] = dot_first(rows_ref[...], hidden_ref[...]).astype(BF)
    out_out[0] = dot_first(active_ref[...], grad_ref[...]).astype(BF)


def expert_weights(rows_in, grad_hidden, active, grad_rows, pieces):
    slots, width = rows_in.shape
    hidden_units = active.shape[1]
    block = hidden_units // pieces
    return pl.pallas_call(
        expert_weights_kernel,
        grid=(pieces,),
        in_specs=[
            pl.BlockSpec((slots, width), lambda i: (0, 0)),
            pl.BlockSpec((slots, block), lambda i: (0, i)),
            pl.BlockSpec((slots, block), lambda i: (0, i)),
            pl.BlockSpec((slots, width), lambda i: (0, 0)),
        ],
        out_specs=[
            pl.BlockSpec((1, width, block), lambda i: (i, 0, 0)),
            pl.BlockSpec((1, block, width), lambda i: (i, 0, 0)),
        ],
        out_shape=[shape((pieces, width, block), BF), shape((pieces, block, width), BF)],
        compiler_params=pltpu.CompilerParams(vmem_limit_bytes=VMEM),
        cost_estimate=pl.CostEstimate(
            flops=4 * slots * width * hidden_units,
            bytes_accessed=slots * (hidden_units * 4 + width * 4) + 4 * width * hidden_units,
            transcendentals=0,
        ),
    )(rows_in, grad_hidden, active, grad_rows)


def dense_backward_kernel(experts, images, last, first_layer, *refs):
    refs = list(refs)
    take = lambda: refs.pop(0)
    g_ref, rows_ref, take_first, take_second = take(), take(), take(), take()
    if last:
        inner_ref = take()
    else:
        first_ref, second_ref = take(), take()
    probs_ref, gates_ref, cols_ref, x_ref, x1_ref = (take() for _ in range(5))
    full_ref, qkv_ref, mixed_ref, lse_ref = (take() for _ in range(4))
    if not first_layer:
        to_first, to_second, gates_below = take(), take(), take()
    g_out, weights_out = take(), take()
    if not first_layer:
        send_out = take()
    grad_qkv = take()
    tokens, width = g_ref.shape
    rows_of = tokens // images
    g = g_ref[...]
    gates = gates_ref[...]
    x1 = x1_ref[...]
    if last:
        inner = inner_ref[...]
        grad_gates = [from_lanes(dot(one[...], inner)) for one in (take_first, take_second)]
    else:
        grad_gates = [
            jnp.sum(g * one[...].astype(F32), axis=1, keepdims=True)
            for one in (first_ref, second_ref)
        ]
    weighted = grad_gates[0] * gates[:, 0:1] + grad_gates[1] * gates[:, 1:2]
    amounts = [
        (grad_gates[at] - weighted) / gates[:, 2:3] * gates[:, 3 + at : 4 + at]
        for at in range(TOP)
    ]
    lane = lane_of(tokens)
    chosen = [jnp.where(lane == cols_ref[:, at : at + 1], amounts[at], 0.0) for at in range(TOP)]
    grad_logits = (
        (chosen[0] + chosen[1]) - probs_ref[...] * (amounts[0] + amounts[1])
    ).astype(BF)
    tail = full_ref[:, 4 * width :]
    norms = norm_rows(tail, experts)
    rows = rows_ref[...]
    grad_n2 = (
        dot(take_first[...], rows) + dot(take_second[...], rows) + dot_last(grad_logits, tail)
    )
    unit2, inverse2 = normalize(x1)
    n2 = (unit2 * norms[1:2] + norms[3:4]).astype(BF)
    grad_x1 = g + norm_backward(grad_n2, unit2, inverse2, norms[1:2])
    grad_attn = grad_x1.astype(BF)
    grad_mixed = dot_last(grad_attn, full_ref[:, 3 * width : 4 * width]).astype(BF)
    masks = half_masks()
    key_at = lax.broadcasted_iota(jnp.int32, (rows_of, rows_of), 1)
    scale = HEAD_DIM**-0.5
    for image in range(images):
        rows = slice(image * rows_of, (image + 1) * rows_of)
        for pair in range(HEADS // 2):
            at = pair * LANES
            q = qkv_ref[rows, at : at + LANES]
            k = qkv_ref[rows, width + at : width + at + LANES]
            v = qkv_ref[rows, 2 * width + at : 2 * width + at + LANES]
            gm = grad_mixed[rows, at : at + LANES]
            sums = [None] * 3
            for half in range(2):
                head = 2 * pair + half
                mask = masks[half]
                scores = dot_last(q * mask, k) * scale
                weights = jnp.exp(scores - lse_ref[rows, head : head + 1])
                weights = jnp.where(key_at < SEQ, weights, 0.0)
                grad_weights = dot_last(gm * mask, v)
                inner = jnp.sum(grad_weights * weights, axis=-1, keepdims=True)
                grad_scores = (weights * (grad_weights - inner)).astype(BF)
                parts = (
                    dot(grad_scores, k * mask),
                    dot_first(grad_scores, q * mask),
                    dot_first(weights.astype(BF), gm * mask),
                )
                sums = [b if a is None else a + b for a, b in zip(sums, parts)]
            grad_qkv[rows, at : at + LANES] = (sums[0] * scale).astype(BF)
            grad_qkv[rows, width + at : width + at + LANES] = (sums[1] * scale).astype(BF)
            grad_qkv[rows, 2 * width + at : 2 * width + at + LANES] = sums[2].astype(BF)
    unit1, inverse1 = normalize(x_ref[...])
    n1 = (unit1 * norms[0:1] + norms[2:3]).astype(BF)
    grad_n1 = dot_last(grad_qkv[...], full_ref[:, : 3 * width])
    g_below = grad_x1 + norm_backward(grad_n1, unit1, inverse1, norms[0:1])
    g_out[...] = g_below
    if not first_layer:
        gates = gates_below[...]
        send_out[...] = (
            dot(to_first[...], (gates[:, 0:1] * g_below).astype(BF))
            + dot(to_second[...], (gates[:, 1:2] * g_below).astype(BF))
        ).astype(BF)
    weights_out[:, : 3 * width] = dot_first(n1, grad_qkv[...]).astype(BF)
    weights_out[:, 3 * width : 4 * width] = dot_first(mixed_ref[...], grad_attn).astype(BF)
    row = lax.broadcasted_iota(jnp.int32, (8, width), 0)
    norm_grads = jnp.zeros((8, width), F32)
    for at, total in enumerate((grad_n1 * unit1, grad_n2 * unit2, grad_n1, grad_n2)):
        norm_grads = jnp.where(row == at, jnp.sum(total, axis=0, keepdims=True), norm_grads)
    picks = (lane_of(8) == row_of(8) + experts).astype(F32).astype(BF)
    weights_out[:, 4 * width :] = (
        dot_first(n2, grad_logits) + dot_first(norm_grads.astype(BF), picks)
    ).astype(BF)


def combine_kernel(images, x1_ref, gates_ref, take_first, take_second, back_ref, out_ref):
    back = back_ref[...]
    gates = gates_ref[...]
    out = x1_ref[...] + (
        gates[:, 0:1] * dot(take_first[...], back) + gates[:, 1:2] * dot(take_second[...], back)
    )
    out_ref[...] = out


def pack_kernel(experts, qkv_ref, o_ref, router_ref, gains_ref, biases_ref, *out_refs):
    width = o_ref.shape[2]
    router_lanes = (lane_of(experts) == row_of(experts)).astype(F32).astype(BF)
    gains_lanes = (lane_of(2) == row_of(2) + experts).astype(F32).astype(BF)
    biases_lanes = (lane_of(2) == row_of(2) + experts + 2).astype(F32).astype(BF)
    for at, out_ref in enumerate(out_refs):
        out_ref[:, : 3 * width] = qkv_ref[at]
        out_ref[:, 3 * width : 4 * width] = o_ref[at]
        out_ref[:, 4 * width :] = (
            dot(router_ref[at], router_lanes)
            + dot_first(gains_ref[at], gains_lanes)
            + dot_first(biases_ref[at], biases_lanes)
        ).astype(BF)


def finish_kernel(experts, *refs):
    sums, outs = refs[:8], refs[8:]
    keep_ref, more_ref = sums[:2]
    qkv_out, o_out, router_out, gains_out, biases_out, second_out, in_out, wout_out = outs
    width = o_out.shape[2]
    picks = jnp.where(lane_of(8) == row_of(8) + experts, 1.0, 0.0)
    for at in range(LAYERS):
        dense = keep_ref[at].astype(F32) + more_ref[at].astype(F32)
        qkv_out[at] = dense[:, : 3 * width]
        o_out[at] = dense[:, 3 * width : 4 * width]
        tail = dense[:, 4 * width :]
        router_out[at] = tail[:, :experts]
        norms = lax.dot_general(
            picks, tail, (((1,), (1,)), ((), ())), precision=lax.Precision.HIGHEST
        )
        gains_out[at] = norms[0:2]
        biases_out[at] = norms[2:4]
        second_out[at : at + 1] = norms[3:4]
    for whole, keep, more, out_ref in zip(sums[2:4], sums[4:6], sums[6:8], (in_out, wout_out)):
        out_ref[0, 0] = whole[...].astype(F32)
        out_ref[1, 0] = keep[...].astype(F32) + more[...].astype(F32)


def other(values, axis):
    return lax.ppermute(values, axis, [(0, 1), (1, 0)])


def across(values, core_axis, axis):
    if axis < core_axis:
        return lax.ppermute(values, (axis, core_axis), [(1, 3), (3, 1)])
    return lax.ppermute(values, (core_axis, axis), [(2, 3), (3, 2)])


def expert_sent(weight, split_at, dp_axes, ex_axes):
    row_axes = dp_axes[:-1]
    size = weight.shape[split_at] // 2 ** len(row_axes)
    place = lax.axis_index(row_axes) if row_axes else 0
    own = lax.dynamic_slice_in_dim(weight, place * size, size, split_at)
    return across(own, dp_axes[-1], ex_axes[0])


def expert_others(got, dp_axes):
    got = [got]
    for axis in dp_axes[:-1][::-1]:
        got = got + [across(one, dp_axes[-1], axis) for one in got]
    return got


def expert_joined(weight, got, split_at, dp_axes):
    row_axes = dp_axes[:-1]
    place = lax.axis_index(row_axes) if row_axes else 0
    first = lax.axis_index(dp_axes[-1]) == 0
    size = weight.shape[split_at] // len(got)
    blocks = []
    for at in range(len(got)):
        theirs = got[at]
        for p, one in enumerate(got):
            theirs = jnp.where(place == at ^ p, one, theirs)
        own = lax.slice_in_dim(weight, at * size, (at + 1) * size, axis=split_at)
        blocks.append(jnp.where(first, own, theirs))
    return jnp.concatenate(blocks, axis=split_at)


def returned_rows(pieces, dp_axes):
    row_axes = dp_axes[:-1]
    pieces = pieces.reshape((-1,) + pieces.shape[2:])
    pieces = lax.psum_scatter(pieces, row_axes, scatter_dimension=0, tiled=True)
    return pieces.reshape((2, -1) + pieces.shape[1:])


def returned_home(pieces, moved, core_axis):
    core = lax.axis_index(core_axis)
    mine = jnp.where(core == 0, pieces, moved)
    keep = lax.dynamic_index_in_dim(mine, core, 0, keepdims=False)
    send = lax.dynamic_index_in_dim(mine, 1 - core, 0, keepdims=False)
    return keep, other(send, core_axis)


def add_low(a, b):
    return (a.astype(F32) + b.astype(F32)).astype(BF)


def gather_step(whole, axis, milestone=None):
    theirs = other(whole, axis)
    if milestone is not None:
        theirs = tie(theirs, milestone)
    mine_first = lax.axis_index(axis) == 0
    return jnp.stack([jnp.where(mine_first, whole, theirs), jnp.where(mine_first, theirs, whole)])


def gathered(whole, axes, order):
    rows, columns = whole.shape[-2:]
    whole = whole.reshape((2,) * len(axes) + (rows, columns))
    places = tuple(order[::-1].index(axis) for axis in axes)
    whole = whole.transpose(places + (len(axes), len(axes) + 1))
    return whole.reshape(-1, columns)


def tie(values, milestone):
    return lax.optimization_barrier((values, milestone))[0]


def halves(values, left, axis, milestone=None):
    at = left.index(axis)
    mine = lax.axis_index(axis)
    keep = lax.dynamic_index_in_dim(values, mine, at, keepdims=False)
    theirs = other(lax.dynamic_index_in_dim(values, 1 - mine, at, keepdims=False), axis)
    if milestone is not None:
        theirs = tie(theirs, milestone)
    left.remove(axis)
    return keep, theirs


def halve(values, left, axis, milestone=None):
    return add_low(*halves(values, left, axis, milestone))


def body(
    dp_axes,
    ex_axes,
    x_in,
    norm_gains,
    norm_biases,
    w_qkv,
    w_o,
    w_router,
    w_in,
    w_out,
    routes,
    threshold,
    cotangent,
):
    axes = dp_axes + ex_axes
    group = dp_axes[-1:] + ex_axes[1:]
    order_out = ex_axes[::-1][1:] + ex_axes[-1:] + dp_axes
    order_in = dp_axes[-1:] + ex_axes[1:][::-1] + dp_axes[:-1][::-1] + ex_axes[:1]
    experts = 2 ** len(ex_axes)
    parts = 2 ** len(dp_axes)
    tokens, width = x_in.shape
    images = tokens // SEQ
    padded = up16(SEQ)
    capacity = up16(4 * tokens // experts)
    slots = experts * capacity
    total = images * padded

    def pad(values, fill=0):
        values = values.reshape((images, SEQ) + values.shape[1:])
        values = jnp.pad(
            values, ((0, 0), (0, padded - SEQ), (0, 0)), constant_values=fill
        )
        return values.reshape((total,) + values.shape[2:])

    def unpad(values):
        return values.reshape(images, padded, -1)[:, :SEQ].reshape(tokens, -1)

    shards = call(
        functools.partial(pack_kernel, experts),
        [shape((w_o.shape[1], 4 * width + LANES), BF)] * LAYERS,
        (w_qkv, w_o, w_router, norm_gains, norm_biases),
        1000,
    )
    def exchange(rows, at):
        over = group if MOVED[at] else ex_axes
        return lax.all_to_all(rows, over, split_axis=0, concat_axis=0, tiled=True)

    cols = [pad(routes[at], -1) for at in range(LAYERS)]
    half_away = lax.axis_index(ex_axes[0]) * (experts // 2)
    route_cols = jnp.stack(
        [
            pad((routes[at] + half_away) % experts if MOVED[at] else routes[at], -1)
            for at in range(LAYERS)
        ]
    )
    to_and_from = call(
        functools.partial(places_kernel, experts, capacity),
        [shape(s, BF) for s in ((total, slots),) * 2 + ((slots, total),) * 2] * LAYERS
        + [shape((slots, width // 2), BF)] * 2,
        (route_cols, route_cols.transpose(0, 2, 1), pad(cotangent)),
        LAYERS * 4 * total * total * LANES,
    )
    collect = [to_and_from[4 * at : 4 * at + 2] for at in range(LAYERS)]
    spread = [to_and_from[4 * at + 2 : 4 * at + 4] for at in range(LAYERS)]
    moved_at = LAYERS - 1
    whole = shards[0][None]
    for step, axis in enumerate(order_out):
        milestone = None if step < 2 else {2: (to_and_from, sent[0]), 3: sent[1]}.get(step)
        whole = gather_step(whole, axis, milestone)
        if step == 1:
            sent = [
                expert_sent(tie(one[moved_at, 0], whole), split_at, dp_axes, ex_axes)
                for one, split_at in ((w_in, 1), (w_out, 0))
            ]
    full = [gathered(whole, axes, order_out)]
    weights = [(w_in, w_out)] * LAYERS
    cot = pad(cotangent.astype(F32))
    current = pad(x_in.astype(F32))

    dense_flops = 2 * total * width * (4 * width) + 6 * total * slots * width
    kept = []
    tops = []
    back = gates = None
    for at in range(LAYERS):
        combine, last = at > 0, at == LAYERS - 1
        args = [current]
        outs = []
        if combine:
            args += [back, *collect[at - 1], gates]
            outs += [shape((total, width), F32), shape((total, width), BF), shape((total, width), BF)]
        args += [full[at], *spread[at], cols[at]]
        outs += [
            shape((total, width), F32),
            shape((total, 3 * width), BF),
            shape((total, width), BF),
            shape((total, LANES), F32),
            shape((total, LANES), F32),
            shape((total, LANES), F32),
            shape((slots, width), BF),
            shape((8, LANES), F32),
        ]
        if last:
            outs.append(shape((slots, LANES), BF))
        made = list(
            call(
                functools.partial(dense_forward_kernel, experts, images, combine, last),
                outs,
                args,
                dense_flops,
            )
        )
        if combine:
            current, first, second = made[:3]
            made = made[3:]
            kept[-1]["routed"] = (first, second)
        x1, qkv, mixed, lse, probs, gates, send, top = made[:8]
        tops.append(top[0, :HEADS])
        rows = exchange(send if at == 0 else tie(send, cot_rows[1]), at)
        if at == 0:
            others = [expert_others(tie(one, send), dp_axes) for one in sent]
            ahead = [one for got in others for one in got]
            whole = tie(shards[1], whole)[None]
            for axis in order_out[:-1]:
                whole = gather_step(whole, axis)
            ahead.append(whole)
        if last:
            gate_rows = exchange(tie(made[8], rows), at)
            active, slope, out_rows, inner = expert_forward(at, cot_rows, rows, *weights[at])
        else:
            active, slope, out_rows = expert_forward(at, [], rows, *weights[at], ahead)
            cot_rows = [exchange(tie(to_and_from[-2], rows), LAYERS - 1)]
            back = exchange(tie(out_rows, cot_rows[0]), at)
            cot_rows.append(exchange(tie(to_and_from[-1], back), LAYERS - 1))
            full.append(
                gathered(gather_step(tie(whole, out_rows), order_out[-1]), axes, order_out)
            )
            weights[moved_at] = [
                expert_joined(one[moved_at, 0], tie(got, out_rows), split_at, dp_axes)
                for one, got, split_at in zip((w_in, w_out), others, (1, 0))
            ]
        kept.append(
            dict(
                x=current,
                x1=x1,
                qkv=qkv,
                mixed=mixed,
                lse=lse,
                probs=probs,
                gates=gates,
                rows=rows,
                active=active,
                slope=slope,
            )
        )
        current = x1
    tops = jnp.pad(jnp.concatenate(tops), (0, LANES - LAYERS * HEADS))
    upstream = cot
    expert_grads = [None] * LAYERS
    dense_grads = [None] * LAYERS
    for at in reversed(range(LAYERS)):
        own = kept[at]
        last, first_layer = at == LAYERS - 1, at == 0
        if last:
            inner = exchange(inner, at)
            grad_hidden, grad_back, grad_rows = expert_backward(
                at, cot_rows, [gate_rows], own["slope"], *weights[at]
            )
            grad_back = tie(grad_back, inner)
        else:
            grad_hidden, grad_back = expert_backward(
                at, [grad_rows], [], own["slope"], *weights[at]
            )
            grad_back = tie(grad_back, head_max)
        grad_back = exchange(grad_back, at)
        pieces = expert_weights(own["rows"], grad_hidden, own["active"], grad_rows, parts)
        if MOVED[at]:
            moved_pieces = [returned_rows(one, dp_axes) for one in pieces]
            out_rows = tie(out_rows, (grad_back, pieces))
        else:
            expert_grads[at] = [
                lax.psum_scatter(
                    one.reshape((-1,) + one.shape[2:]), dp_axes, scatter_dimension=0, tiled=True
                )
                for one in pieces
            ]
        if first_layer:
            moved_pieces = [tie(one, (grad_back, pieces)) for one in moved_pieces]
            crossed = [across(one, dp_axes[-1], ex_axes[0]) for one in moved_pieces]
        args = [upstream, grad_back, *collect[at]]
        if last:
            args.append(inner)
        else:
            args += own["routed"]
        args += [own["probs"], own["gates"], cols[at], own["x"], own["x1"]]
        args += [full[at], own["qkv"], own["mixed"], own["lse"]]
        outs = [shape((total, width), F32), shape((width, 4 * width + LANES), BF)]
        if not first_layer:
            args += [*spread[at - 1], kept[at - 1]["gates"]]
            outs.append(shape((slots, width), BF))
        made = list(
            call(
                functools.partial(dense_backward_kernel, experts, images, last, first_layer),
                outs,
                args,
                2 * dense_flops,
                [pltpu.VMEM((total, 3 * width), BF)],
                pieces,
            )
        )
        upstream, weight_grads = made[:2]
        if not first_layer:
            back = exchange(out_rows, at)
            grad_rows = exchange(tie(made[2], back), at - 1)
        weight_grads = weight_grads.reshape((2,) * len(axes) + (-1,) + weight_grads.shape[1:])
        if first_layer:
            first_left = list(axes)
            weight_grads = tie(weight_grads, crossed[0])
            weight_grads = halve(weight_grads, first_left, order_in[0])
            weight_grads = halve(weight_grads, first_left, order_in[1])
            both = jnp.stack([weight_grads, sums], axis=-3)
            both = tie(halve(both, first_left, order_in[2]), crossed[1])
            for axis in order_in[3:-1]:
                both = halve(both, first_left, axis)
            dense = [
                one.reshape(LAYERS, -1, one.shape[-1])
                for one in halves(both, first_left, order_in[-1])
            ]
        else:
            left = list(axes)
            sums = halve(weight_grads, left, order_in[0])
            sums = halve(sums, left, order_in[1], grad_rows)
            [out_act] = call(
                functools.partial(combine_kernel, images),
                [shape((total, width), F32)],
                [own["x1"], own["gates"], *collect[at], back],
                4 * total * slots * width,
            )
            grad_rows = tie(grad_rows, (out_act, sums))
            everyone = 2 ** len(axes)
            tops = lax.all_to_all(
                jnp.broadcast_to(tie(tops, grad_rows), (everyone, LANES)),
                axes,
                split_axis=0,
                concat_axis=0,
                tiled=True,
            )
            head_max = jnp.max(tops, axis=0)[: LAYERS * HEADS].reshape(LAYERS, HEADS)
    home = [
        returned_home(one, tie(moved, both), dp_axes[-1])
        for one, moved in zip(moved_pieces, crossed)
    ]
    rows = w_o.shape[1]
    finished = call(
        functools.partial(finish_kernel, experts),
        [
            shape((LAYERS, rows, 3 * width), F32),
            shape((LAYERS, rows, width), F32),
            shape((LAYERS, rows, experts), F32),
            shape((LAYERS, 2, rows), F32),
            shape((LAYERS, 2, rows), F32),
            shape((LAYERS, rows), F32),
        ]
        + [shape((LAYERS, 1) + one.shape, F32) for one, _ in home],
        [*dense, *expert_grads[0], home[0][0], home[1][0], home[0][1], home[1][1]],
        1000,
    )
    grad_qkv, grad_o, grad_router, grad_gains, grad_biases, second, grad_in, grad_out = finished
    factor = jnp.sqrt(threshold / jnp.maximum(head_max, threshold))
    columns = jnp.repeat(factor, HEAD_DIM, axis=1)
    clipped_qk = (
        w_qkv[:, :, : 2 * width].astype(F32)
        * jnp.concatenate([columns, columns], axis=1)[:, None, :]
    )
    return (
        unpad(out_act),
        unpad(upstream),
        grad_gains,
        grad_biases,
        grad_qkv,
        grad_o,
        grad_router,
        grad_in,
        grad_out,
        head_max,
        clipped_qk,
        second,
    )


def solution(mesh):
    dp_bits = int(mesh.shape["dp"]).bit_length() - 1
    ex_bits = int(mesh.shape["expert"]).bit_length() - 1
    dp_axes = tuple(f"d{at}" for at in range(dp_bits))
    ex_axes = tuple(f"e{at}" for at in range(ex_bits))
    split = Mesh(mesh.devices.reshape((2,) * (dp_bits + ex_bits)), dp_axes + ex_axes)
    both = dp_axes + ex_axes
    in_specs = (
        P(both, None),
        P(None, None, both),
        P(None, None, both),
        P(None, both, None),
        P(None, both, None),
        P(None, both, None),
        P(None, ex_axes, None, None),
        P(None, ex_axes, None, None),
        P(None, both, None),
        P(),
        P(both, None),
    )
    out_specs = (
        P(both, None),
        P(both, None),
        P(None, None, both),
        P(None, None, both),
        P(None, both, None),
        P(None, both, None),
        P(None, both, None),
        P(None, ex_axes, None, dp_axes),
        P(None, ex_axes, dp_axes, None),
        P(),
        P(None, both, None),
        P(None, both),
    )
    return jax.shard_map(
        functools.partial(body, dp_axes, ex_axes),
        mesh=split,
        in_specs=in_specs,
        out_specs=out_specs,
        check_vma=False,
    )
```

```python
import functools

import jax
import jax.numpy as jnp
import numpy as np
from jax import lax
from jax.experimental import pallas as pl
from jax.experimental.pallas import tpu as pltpu
from jax.sharding import Mesh
from jax.sharding import PartitionSpec as P

HEADS = 8
HEAD_DIM = 64
SEQ = 197
TOP = 2
LAYERS = 2
EPSILON = 1e-06
BF = jnp.bfloat16
F32 = jnp.float32
LANES = 128
PIECES = 4
VMEM = 56 * 1024 * 1024
MOVED = (False, True)


def up16(size):
    return -(-size // 16) * 16


def dot(a, b):
    return jnp.dot(a, b, preferred_element_type=F32)


def dot_last(a, b):
    return lax.dot_general(a, b, (((1,), (1,)), ((), ())), preferred_element_type=F32)


def dot_first(a, b):
    return lax.dot_general(a, b, (((0,), (0,)), ((), ())), preferred_element_type=F32)


def lane_of(rows, lanes=LANES):
    return lax.broadcasted_iota(jnp.int32, (rows, lanes), 1)


def row_of(rows, lanes=LANES):
    return lax.broadcasted_iota(jnp.int32, (rows, lanes), 0)


def normalize(values):
    center = values - jnp.mean(values, axis=-1, keepdims=True)
    inverse = lax.rsqrt(jnp.mean(center * center, axis=-1, keepdims=True) + EPSILON)
    return center * inverse, inverse


def norm_backward(upstream, normed, inverse, gain_row):
    scaled = upstream * gain_row
    mean_plain = jnp.mean(scaled, axis=-1, keepdims=True)
    mean_normed = jnp.mean(scaled * normed, axis=-1, keepdims=True)
    return inverse * (scaled - mean_plain - normed * mean_normed)


def norm_rows(tail, experts):
    picks = (lane_of(8) == row_of(8) + experts).astype(F32).astype(BF)
    return dot_last(picks, tail)


def places_kernel(experts, capacity, cols_ref, rows_ref, cot_ref, *out_refs):
    tokens = cols_ref.shape[1]
    slots = experts * capacity
    square_row = lax.broadcasted_iota(jnp.int32, (tokens, tokens), 0)
    square_col = lax.broadcasted_iota(jnp.int32, (tokens, tokens), 1)
    earlier = (square_col < square_row).astype(F32).astype(BF)
    later = (square_row < square_col).astype(F32).astype(BF)
    wide = max(16, experts)
    for layer_at in range(LAYERS):
        to_tokens, to_slots = out_refs[4 * layer_at : 4 * layer_at + 2], out_refs[
            4 * layer_at + 2 : 4 * layer_at + 4
        ]
        cols = cols_ref[layer_at]
        first, second = cols[:, 0:1], cols[:, 1:2]
        lane = lane_of(tokens)
        matches = jnp.where((lane == first) | (lane == second), 1.0, 0.0)
        before = dot(earlier, matches.astype(BF))
        slot_lane = lax.broadcasted_iota(jnp.int32, (tokens, slots), 1)
        for chosen, out_ref in zip((first, second), to_tokens):
            rank = jnp.sum(jnp.where(lane == chosen, before, 0.0), axis=1, keepdims=True)
            slot = chosen * capacity + rank.astype(jnp.int32)
            out_ref[...] = jnp.where(slot_lane == slot, 1.0, 0.0).astype(BF)
        rows = rows_ref[layer_at]
        first, second = rows[0:1], rows[1:2]
        which = lax.broadcasted_iota(jnp.int32, (wide, tokens), 0)
        matches = jnp.where((which == first) | (which == second), 1.0, 0.0)
        before = dot(matches.astype(BF), later)
        slot_row = lax.broadcasted_iota(jnp.int32, (slots, tokens), 0)
        for chosen, out_ref in zip((first, second), to_slots):
            rank = jnp.sum(jnp.where(which == chosen, before, 0.0), axis=0, keepdims=True)
            slot = chosen * capacity + rank.astype(jnp.int32)
            out_ref[...] = jnp.where(slot_row == slot, 1.0, 0.0).astype(BF)
    for at, out_ref in enumerate(out_refs[4 * LAYERS :]):
        columns = out_ref.shape[1]
        cot = cot_ref[:, at * columns : (at + 1) * columns]
        out_ref[...] = (dot(to_slots[0][...], cot) + dot(to_slots[1][...], cot)).astype(BF)


def two_parts(values):
    high = values.astype(BF)
    return high, (values - high.astype(F32)).astype(BF)


def two_lanes(values):
    high, low = two_parts(values)
    lane = lane_of(values.shape[0])
    high, low = high.astype(F32), low.astype(F32)
    return jnp.where(lane == 0, high, jnp.where(lane == 1, low, 0.0)).astype(BF)


def from_lanes(parts):
    return parts[:, 0:1] + parts[:, 1:2]


def behind(kernel, operands, *refs):
    return kernel(*refs[operands:])


def call(kernel, out_shapes, args, flops, scratch=(), after=()):
    moved = sum(a.size * a.dtype.itemsize for a in args) + sum(
        int(np.prod(o.shape)) * o.dtype.itemsize for o in out_shapes
    )
    whole = pl.BlockSpec(memory_space=pltpu.VMEM)
    return pl.pallas_call(
        functools.partial(behind, kernel, len(after)),
        in_specs=[pl.BlockSpec(memory_space=pl.ANY)] * len(after) + [whole] * len(args),
        out_shape=out_shapes,
        scratch_shapes=list(scratch),
        compiler_params=pltpu.CompilerParams(vmem_limit_bytes=VMEM),
        cost_estimate=pl.CostEstimate(
            flops=int(flops), bytes_accessed=int(moved), transcendentals=0
        ),
    )(*after, *args)


def shape(dims, dtype):
    return jax.ShapeDtypeStruct(dims, dtype)


def half_masks():
    lane = lane_of(1)
    return (
        jnp.where(lane < HEAD_DIM, 1.0, 0.0).astype(BF),
        jnp.where(lane < HEAD_DIM, 0.0, 1.0).astype(BF),
    )


def dense_forward_kernel(experts, images, combine, last, *refs):
    refs = list(refs)
    take = lambda: refs.pop(0)
    x_ref = take()
    if combine:
        back_ref, take_first, take_second, gates_before = take(), take(), take(), take()
    full_ref, to_first, to_second, cols_ref = take(), take(), take(), take()
    if combine:
        x_out, first_out, second_out = take(), take(), take()
    x1_out, qkv_out, mixed_out, lse_out, probs_out, gates_out, send_out, top_out = (
        take() for _ in range(8)
    )
    if last:
        send_gates_out = take()
    tokens, width = x_ref.shape
    rows_of = tokens // images
    x = x_ref[...]
    if combine:
        back = back_ref[...]
        first = dot(take_first[...], back)
        second = dot(take_second[...], back)
        gates = gates_before[...]
        x = x + (gates[:, 0:1] * first + gates[:, 1:2] * second)
        x_out[...] = x
        first_out[...] = first.astype(BF)
        second_out[...] = second.astype(BF)
    tail = full_ref[:, 4 * width :]
    norms = norm_rows(tail, experts)
    unit, _ = normalize(x)
    n1 = (unit * norms[0:1] + norms[2:3]).astype(BF)
    qkv_out[...] = dot(n1, full_ref[:, : 3 * width]).astype(BF)
    masks = half_masks()
    key_at = lax.broadcasted_iota(jnp.int32, (rows_of, rows_of), 1)
    query_at = lax.broadcasted_iota(jnp.int32, (rows_of, 1), 0)
    lane = lane_of(rows_of)
    top_lane = lane_of(8)
    tops = jnp.full((8, LANES), -jnp.inf, F32)
    scale = HEAD_DIM**-0.5
    for image in range(images):
        rows = slice(image * rows_of, (image + 1) * rows_of)
        lse = jnp.zeros((rows_of, LANES), F32)
        for pair in range(HEADS // 2):
            at = pair * LANES
            q = qkv_out[rows, at : at + LANES]
            k = qkv_out[rows, width + at : width + at + LANES]
            v = qkv_out[rows, 2 * width + at : 2 * width + at + LANES]
            mixed = None
            for half in range(2):
                scores = dot_last(q * masks[half], k) * scale
                scores = jnp.where(key_at < SEQ, scores, -jnp.inf)
                highest = jnp.max(scores, axis=-1, keepdims=True)
                top = jnp.max(
                    jnp.where(query_at < SEQ, highest, -jnp.inf), axis=0, keepdims=True
                )
                weights = jnp.exp(scores - highest)
                total = jnp.sum(weights, axis=-1, keepdims=True)
                weights = (weights * (1.0 / total)).astype(BF)
                part = dot(weights, v * masks[half])
                mixed = part if mixed is None else mixed + part
                head = 2 * pair + half
                lse = jnp.where(lane == head, highest + jnp.log(total), lse)
                tops = jnp.where(top_lane == head, jnp.maximum(tops, top), tops)
            mixed_out[rows, at : at + LANES] = mixed.astype(BF)
        lse_out[rows, :] = lse
    top_out[...] = tops
    x1 = x + dot(mixed_out[...], full_ref[:, 3 * width : 4 * width])
    x1_out[...] = x1
    unit, _ = normalize(x1)
    n2 = (unit * norms[1:2] + norms[3:4]).astype(BF)
    lane = lane_of(tokens)
    logits = jnp.where(lane < experts, dot(n2, tail), -jnp.inf)
    probs = jnp.exp(logits - jnp.max(logits, axis=-1, keepdims=True))
    probs = probs / jnp.sum(probs, axis=-1, keepdims=True)
    probs_out[...] = probs
    first, second = cols_ref[:, 0:1], cols_ref[:, 1:2]
    picked = [
        jnp.sum(jnp.where(lane == chosen, probs, 0.0), axis=1, keepdims=True)
        for chosen in (first, second)
    ]
    total = jnp.where(first >= 0, picked[0] + picked[1], 1.0)
    gates = [one / total for one in picked]
    packed = jnp.zeros((tokens, LANES), F32)
    for at, column in enumerate((gates[0], gates[1], total, picked[0], picked[1])):
        packed = jnp.where(lane == at, column, packed)
    gates_out[...] = packed
    send_out[...] = dot(to_first[...] + to_second[...], n2).astype(BF)
    if last:
        send_gates_out[...] = (
            dot(to_first[...], two_lanes(gates[0])) + dot(to_second[...], two_lanes(gates[1]))
        ).astype(BF)


def expert_forward_kernel(last, *refs):
    refs = list(refs)
    if last:
        grad_refs, inner_out = (refs.pop(0), refs.pop(0)), refs.pop()
    rows_ref, win_ref, wout_ref, active_out, slope_out, out_ref = refs
    units = win_ref.shape[1] // 2
    factor = (2.0 / np.pi) ** 0.5
    rows = rows_ref[...]
    hidden = dot(rows, win_ref[:, :units])
    total = before = None
    for piece in range(2):
        at = slice(piece * units, (piece + 1) * units)
        later = dot(rows, win_ref[:, units:]) if piece == 0 else None
        square = hidden * hidden
        gate = 0.5 + 0.5 * jnp.tanh(hidden * (factor + (0.044715 * factor) * square))
        active = hidden * gate
        slope = active * (2 * factor + (6 * 0.044715 * factor) * square)
        slope_out[:, at] = (gate + slope * (1.0 - gate)).astype(BF)
        active = active.astype(BF)
        active_out[:, at] = active
        if piece == 1:
            total = dot(before, wout_ref[:units, :]) + dot(active, wout_ref[units:, :])
        before, hidden = active, later
    total = total.astype(BF)
    out_ref[...] = total
    if last:
        half = total.shape[1] // 2
        inner_out[...] = two_lanes(
            jnp.sum(
                total[:, :half].astype(F32) * grad_refs[0][...].astype(F32)
                + total[:, half:].astype(F32) * grad_refs[1][...].astype(F32),
                axis=1,
                keepdims=True,
            )
        )


def weight_spec(weight, layer_at):
    if weight.ndim == 4:
        return pl.BlockSpec((None, None) + weight.shape[2:], lambda i: (layer_at, 0, 0, 0))
    return pl.BlockSpec(weight.shape, lambda i: (0, 0))


def expert_forward(layer_at, grads, rows_in, weight_in, weight_out, after=()):
    last = len(grads) > 0
    slots, width = rows_in.shape
    hidden_units = weight_in.shape[-1]
    chunk = slots // 4
    return pl.pallas_call(
        functools.partial(behind, functools.partial(expert_forward_kernel, last), len(after)),
        grid=(4,),
        in_specs=[pl.BlockSpec(memory_space=pl.ANY)] * len(after)
        + [pl.BlockSpec((chunk, width // 2), lambda i: (i, 0))] * len(grads)
        + [
            pl.BlockSpec((chunk, width), lambda i: (i, 0)),
            weight_spec(weight_in, layer_at),
            weight_spec(weight_out, layer_at),
        ],
        out_specs=[
            pl.BlockSpec((chunk, hidden_units), lambda i: (i, 0)),
            pl.BlockSpec((chunk, hidden_units), lambda i: (i, 0)),
            pl.BlockSpec((chunk, width), lambda i: (i, 0)),
        ]
        + [pl.BlockSpec((chunk, LANES), lambda i: (i, 0))] * last,
        out_shape=[
            shape((slots, hidden_units), BF),
            shape((slots, hidden_units), BF),
            shape((slots, width), BF),
        ]
        + [shape((slots, LANES), BF)] * last,
        compiler_params=pltpu.CompilerParams(vmem_limit_bytes=VMEM),
        cost_estimate=pl.CostEstimate(
            flops=4 * slots * width * hidden_units,
            bytes_accessed=slots * (hidden_units * 4 + width * 4) + 4 * width * hidden_units,
            transcendentals=slots * hidden_units,
        ),
    )(*after, *grads, rows_in, weight_in, weight_out)


def expert_backward_kernel(gated, *refs):
    refs = list(refs)
    grad_ref = refs.pop(0)
    if gated:
        second_ref, gates_ref, scaled = refs.pop(0), refs.pop(0), refs.pop()
        gates = from_lanes(gates_ref[...].astype(F32))
        half = grad_ref.shape[1]
        scaled[:, :half] = (gates * grad_ref[...].astype(F32)).astype(BF)
        scaled[:, half:] = (gates * second_ref[...].astype(F32)).astype(BF)
        grad_ref = scaled
    slope_ref, win_ref, wout_ref, hidden_out, out_ref = refs
    units = win_ref.shape[1] // PIECES
    for piece in range(PIECES):
        at = slice(piece * units, (piece + 1) * units)
        grad_active = dot_last(grad_ref[...], wout_ref[at, :])
        hidden_out[:, at] = (grad_active * slope_ref[:, at].astype(F32)).astype(BF)
    out_ref[...] = dot_last(hidden_out[...], win_ref[...]).astype(BF)


def expert_backward(layer_at, grads, gates, slope, weight_in, weight_out):
    slots, width = grads[0].shape[0], weight_in.shape[-2]
    hidden_units = weight_in.shape[-1]
    chunk = slots // 4
    gated = len(gates)
    rows_spec = lambda lanes: pl.BlockSpec((chunk, lanes), lambda i: (i, 0))
    return pl.pallas_call(
        functools.partial(expert_backward_kernel, gated),
        grid=(4,),
        in_specs=[rows_spec(one.shape[1]) for one in grads]
        + [rows_spec(LANES)] * gated
        + [
            rows_spec(hidden_units),
            weight_spec(weight_in, layer_at),
            weight_spec(weight_out, layer_at),
        ],
        out_specs=[rows_spec(hidden_units), rows_spec(width)] + [rows_spec(width)] * gated,
        out_shape=[shape((slots, hidden_units), BF), shape((slots, width), BF)]
        + [shape((slots, width), BF)] * gated,
        compiler_params=pltpu.CompilerParams(vmem_limit_bytes=VMEM),
        cost_estimate=pl.CostEstimate(
            flops=4 * slots * width * hidden_units,
            bytes_accessed=slots * (hidden_units * 4 + width * 4) + 4 * width * hidden_units,
            transcendentals=0,
        ),
    )(*grads, *gates, slope, weight_in, weight_out)


def expert_weights_kernel(rows_ref, hidden_ref, active_ref, grad_ref, in_out, out_out):
    in_out[0] = dot_first(rows_ref[...], hidden_ref[...]).astype(BF)
    out_out[0] = dot_first(active_ref[...], grad_ref[...]).astype(BF)


def expert_weights(rows_in, grad_hidden, active, grad_rows, pieces):
    slots, width = rows_in.shape
    hidden_units = active.shape[1]
    block = hidden_units // pieces
    return pl.pallas_call(
        expert_weights_kernel,
        grid=(pieces,),
        in_specs=[
            pl.BlockSpec((slots, width), lambda i: (0, 0)),
            pl.BlockSpec((slots, block), lambda i: (0, i)),
            pl.BlockSpec((slots, block), lambda i: (0, i)),
            pl.BlockSpec((slots, width), lambda i: (0, 0)),
        ],
        out_specs=[
            pl.BlockSpec((1, width, block), lambda i: (i, 0, 0)),
            pl.BlockSpec((1, block, width), lambda i: (i, 0, 0)),
        ],
        out_shape=[shape((pieces, width, block), BF), shape((pieces, block, width), BF)],
        compiler_params=pltpu.CompilerParams(vmem_limit_bytes=VMEM),
        cost_estimate=pl.CostEstimate(
            flops=4 * slots * width * hidden_units,
            bytes_accessed=slots * (hidden_units * 4 + width * 4) + 4 * width * hidden_units,
            transcendentals=0,
        ),
    )(rows_in, grad_hidden, active, grad_rows)


def dense_backward_kernel(experts, images, last, first_layer, *refs):
    refs = list(refs)
    take = lambda: refs.pop(0)
    g_ref, rows_ref, take_first, take_second = take(), take(), take(), take()
    if last:
        inner_ref = take()
    else:
        first_ref, second_ref = take(), take()
    probs_ref, gates_ref, cols_ref, x_ref, x1_ref = (take() for _ in range(5))
    full_ref, qkv_ref, mixed_ref, lse_ref = (take() for _ in range(4))
    if not first_layer:
        to_first, to_second, gates_below = take(), take(), take()
    g_out, weights_out = take(), take()
    if not first_layer:
        send_out = take()
    grad_qkv = take()
    tokens, width = g_ref.shape
    rows_of = tokens // images
    g = g_ref[...]
    gates = gates_ref[...]
    x1 = x1_ref[...]
    if last:
        inner = inner_ref[...]
        grad_gates = [from_lanes(dot(one[...], inner)) for one in (take_first, take_second)]
    else:
        grad_gates = [
            jnp.sum(g * one[...].astype(F32), axis=1, keepdims=True)
            for one in (first_ref, second_ref)
        ]
    weighted = grad_gates[0] * gates[:, 0:1] + grad_gates[1] * gates[:, 1:2]
    amounts = [
        (grad_gates[at] - weighted) / gates[:, 2:3] * gates[:, 3 + at : 4 + at]
        for at in range(TOP)
    ]
    lane = lane_of(tokens)
    chosen = [jnp.where(lane == cols_ref[:, at : at + 1], amounts[at], 0.0) for at in range(TOP)]
    grad_logits = (
        (chosen[0] + chosen[1]) - probs_ref[...] * (amounts[0] + amounts[1])
    ).astype(BF)
    tail = full_ref[:, 4 * width :]
    norms = norm_rows(tail, experts)
    rows = rows_ref[...]
    grad_n2 = dot(take_first[...] + take_second[...], rows) + dot_last(grad_logits, tail)
    unit2, inverse2 = normalize(x1)
    n2 = (unit2 * norms[1:2] + norms[3:4]).astype(BF)
    grad_x1 = g + norm_backward(grad_n2, unit2, inverse2, norms[1:2])
    grad_attn = grad_x1.astype(BF)
    grad_mixed = dot_last(grad_attn, full_ref[:, 3 * width : 4 * width]).astype(BF)
    masks = half_masks()
    key_at = lax.broadcasted_iota(jnp.int32, (rows_of, rows_of), 1)
    scale = HEAD_DIM**-0.5
    for image in range(images):
        rows = slice(image * rows_of, (image + 1) * rows_of)
        for pair in range(HEADS // 2):
            at = pair * LANES
            q = qkv_ref[rows, at : at + LANES]
            k = qkv_ref[rows, width + at : width + at + LANES]
            v = qkv_ref[rows, 2 * width + at : 2 * width + at + LANES]
            gm = grad_mixed[rows, at : at + LANES]
            sums = [None] * 3
            for half in range(2):
                head = 2 * pair + half
                mask = masks[half]
                scores = dot_last(q * mask, k) * scale
                weights = jnp.exp(scores - lse_ref[rows, head : head + 1])
                weights = jnp.where(key_at < SEQ, weights, 0.0)
                grad_weights = dot_last(gm * mask, v)
                inner = jnp.sum(grad_weights * weights, axis=-1, keepdims=True)
                grad_scores = (weights * (grad_weights - inner)).astype(BF)
                parts = (
                    dot(grad_scores, k * mask),
                    dot_first(grad_scores, q * mask),
                    dot_first(weights.astype(BF), gm * mask),
                )
                sums = [b if a is None else a + b for a, b in zip(sums, parts)]
            grad_qkv[rows, at : at + LANES] = (sums[0] * scale).astype(BF)
            grad_qkv[rows, width + at : width + at + LANES] = (sums[1] * scale).astype(BF)
            grad_qkv[rows, 2 * width + at : 2 * width + at + LANES] = sums[2].astype(BF)
    unit1, inverse1 = normalize(x_ref[...])
    n1 = (unit1 * norms[0:1] + norms[2:3]).astype(BF)
    grad_n1 = dot_last(grad_qkv[...], full_ref[:, : 3 * width])
    g_below = grad_x1 + norm_backward(grad_n1, unit1, inverse1, norms[0:1])
    g_out[...] = g_below
    if not first_layer:
        gates = gates_below[...]
        send_out[...] = (
            dot(to_first[...], (gates[:, 0:1] * g_below).astype(BF))
            + dot(to_second[...], (gates[:, 1:2] * g_below).astype(BF))
        ).astype(BF)
    weights_out[:, : 3 * width] = dot_first(n1, grad_qkv[...]).astype(BF)
    weights_out[:, 3 * width : 4 * width] = dot_first(mixed_ref[...], grad_attn).astype(BF)
    row = lax.broadcasted_iota(jnp.int32, (8, width), 0)
    norm_grads = jnp.zeros((8, width), F32)
    for at, total in enumerate((grad_n1 * unit1, grad_n2 * unit2, grad_n1, grad_n2)):
        norm_grads = jnp.where(row == at, jnp.sum(total, axis=0, keepdims=True), norm_grads)
    picks = (lane_of(8) == row_of(8) + experts).astype(F32).astype(BF)
    weights_out[:, 4 * width :] = (
        dot_first(n2, grad_logits) + dot_first(norm_grads.astype(BF), picks)
    ).astype(BF)


def combine_kernel(images, x1_ref, gates_ref, take_first, take_second, back_ref, out_ref):
    back = back_ref[...]
    gates = gates_ref[...]
    out = x1_ref[...] + (
        gates[:, 0:1] * dot(take_first[...], back) + gates[:, 1:2] * dot(take_second[...], back)
    )
    out_ref[...] = out


def pack_kernel(experts, qkv_ref, o_ref, router_ref, gains_ref, biases_ref, *out_refs):
    width = o_ref.shape[2]
    router_lanes = (lane_of(experts) == row_of(experts)).astype(F32).astype(BF)
    gains_lanes = (lane_of(2) == row_of(2) + experts).astype(F32).astype(BF)
    biases_lanes = (lane_of(2) == row_of(2) + experts + 2).astype(F32).astype(BF)
    for at, out_ref in enumerate(out_refs):
        out_ref[:, : 3 * width] = qkv_ref[at]
        out_ref[:, 3 * width : 4 * width] = o_ref[at]
        out_ref[:, 4 * width :] = (
            dot(router_ref[at], router_lanes)
            + dot_first(gains_ref[at], gains_lanes)
            + dot_first(biases_ref[at], biases_lanes)
        ).astype(BF)


def finish_kernel(experts, *refs):
    sums, outs = refs[:8], refs[8:]
    keep_ref, more_ref = sums[:2]
    qkv_out, o_out, router_out, gains_out, biases_out, second_out, in_out, wout_out = outs
    width = o_out.shape[2]
    picks = jnp.where(lane_of(8) == row_of(8) + experts, 1.0, 0.0)
    for at in range(LAYERS):
        dense = keep_ref[at].astype(F32) + more_ref[at].astype(F32)
        qkv_out[at] = dense[:, : 3 * width]
        o_out[at] = dense[:, 3 * width : 4 * width]
        tail = dense[:, 4 * width :]
        router_out[at] = tail[:, :experts]
        norms = lax.dot_general(
            picks, tail, (((1,), (1,)), ((), ())), precision=lax.Precision.HIGHEST
        )
        gains_out[at] = norms[0:2]
        biases_out[at] = norms[2:4]
        second_out[at : at + 1] = norms[3:4]
    for whole, keep, more, out_ref in zip(sums[2:4], sums[4:6], sums[6:8], (in_out, wout_out)):
        out_ref[0, 0] = whole[...].astype(F32)
        out_ref[1, 0] = keep[...].astype(F32) + more[...].astype(F32)


def other(values, axis):
    return lax.ppermute(values, axis, [(0, 1), (1, 0)])


def across(values, core_axis, axis):
    if axis < core_axis:
        return lax.ppermute(values, (axis, core_axis), [(1, 3), (3, 1)])
    return lax.ppermute(values, (core_axis, axis), [(2, 3), (3, 2)])


def expert_sent(weight, split_at, dp_axes, ex_axes):
    row_axes = dp_axes[:-1]
    size = weight.shape[split_at] // 2 ** len(row_axes)
    place = lax.axis_index(row_axes) if row_axes else 0
    own = lax.dynamic_slice_in_dim(weight, place * size, size, split_at)
    return across(own, dp_axes[-1], ex_axes[0])


def expert_others(got, dp_axes):
    got = [got]
    for axis in dp_axes[:-1][::-1]:
        got = got + [across(one, dp_axes[-1], axis) for one in got]
    return got


def expert_joined(weight, got, split_at, dp_axes):
    row_axes = dp_axes[:-1]
    place = lax.axis_index(row_axes) if row_axes else 0
    first = lax.axis_index(dp_axes[-1]) == 0
    size = weight.shape[split_at] // len(got)
    blocks = []
    for at in range(len(got)):
        theirs = got[at]
        for p, one in enumerate(got):
            theirs = jnp.where(place == at ^ p, one, theirs)
        own = lax.slice_in_dim(weight, at * size, (at + 1) * size, axis=split_at)
        blocks.append(jnp.where(first, own, theirs))
    return jnp.concatenate(blocks, axis=split_at)


def returned_rows(pieces, dp_axes):
    row_axes = dp_axes[:-1]
    pieces = pieces.reshape((-1,) + pieces.shape[2:])
    pieces = lax.psum_scatter(pieces, row_axes, scatter_dimension=0, tiled=True)
    return pieces.reshape((2, -1) + pieces.shape[1:])


def returned_home(pieces, moved, core_axis):
    core = lax.axis_index(core_axis)
    mine = jnp.where(core == 0, pieces, moved)
    keep = lax.dynamic_index_in_dim(mine, core, 0, keepdims=False)
    send = lax.dynamic_index_in_dim(mine, 1 - core, 0, keepdims=False)
    return keep, other(send, core_axis)


def add_low(a, b):
    return (a.astype(F32) + b.astype(F32)).astype(BF)


def gather_step(whole, axis, milestone=None):
    theirs = other(whole, axis)
    if milestone is not None:
        theirs = tie(theirs, milestone)
    mine_first = lax.axis_index(axis) == 0
    return jnp.stack([jnp.where(mine_first, whole, theirs), jnp.where(mine_first, theirs, whole)])


def gathered(whole, axes, order):
    rows, columns = whole.shape[-2:]
    whole = whole.reshape((2,) * len(axes) + (rows, columns))
    places = tuple(order[::-1].index(axis) for axis in axes)
    whole = whole.transpose(places + (len(axes), len(axes) + 1))
    return whole.reshape(-1, columns)


def tie(values, milestone):
    return lax.optimization_barrier((values, milestone))[0]


def halves(values, left, axis, milestone=None):
    at = left.index(axis)
    mine = lax.axis_index(axis)
    keep = lax.dynamic_index_in_dim(values, mine, at, keepdims=False)
    theirs = other(lax.dynamic_index_in_dim(values, 1 - mine, at, keepdims=False), axis)
    if milestone is not None:
        theirs = tie(theirs, milestone)
    left.remove(axis)
    return keep, theirs


def halve(values, left, axis, milestone=None):
    return add_low(*halves(values, left, axis, milestone))


def body(
    dp_axes,
    ex_axes,
    x_in,
    norm_gains,
    norm_biases,
    w_qkv,
    w_o,
    w_router,
    w_in,
    w_out,
    routes,
    threshold,
    cotangent,
):
    axes = dp_axes + ex_axes
    group = dp_axes[-1:] + ex_axes[1:]
    order_out = ex_axes[::-1][1:] + ex_axes[-1:] + dp_axes
    order_in = dp_axes[-1:] + ex_axes[1:][::-1] + dp_axes[:-1][::-1] + ex_axes[:1]
    experts = 2 ** len(ex_axes)
    parts = 2 ** len(dp_axes)
    tokens, width = x_in.shape
    images = tokens // SEQ
    padded = up16(SEQ)
    capacity = -(-(4 * tokens // experts) // 8) * 8
    slots = experts * capacity
    total = images * padded

    def pad(values, fill=0):
        values = values.reshape((images, SEQ) + values.shape[1:])
        values = jnp.pad(
            values, ((0, 0), (0, padded - SEQ), (0, 0)), constant_values=fill
        )
        return values.reshape((total,) + values.shape[2:])

    def unpad(values):
        return values.reshape(images, padded, -1)[:, :SEQ].reshape(tokens, -1)

    shards = call(
        functools.partial(pack_kernel, experts),
        [shape((w_o.shape[1], 4 * width + LANES), BF)] * LAYERS,
        (w_qkv, w_o, w_router, norm_gains, norm_biases),
        1000,
    )
    def exchange(rows, at):
        over = group if MOVED[at] else ex_axes
        return lax.all_to_all(rows, over, split_axis=0, concat_axis=0, tiled=True)

    cols = [pad(routes[at], -1) for at in range(LAYERS)]
    half_away = lax.axis_index(ex_axes[0]) * (experts // 2)
    route_cols = jnp.stack(
        [
            pad((routes[at] + half_away) % experts if MOVED[at] else routes[at], -1)
            for at in range(LAYERS)
        ]
    )
    to_and_from = call(
        functools.partial(places_kernel, experts, capacity),
        [shape(s, BF) for s in ((total, slots),) * 2 + ((slots, total),) * 2] * LAYERS
        + [shape((slots, width // 2), BF)] * 2,
        (route_cols, route_cols.transpose(0, 2, 1), pad(cotangent)),
        LAYERS * 4 * total * total * LANES,
    )
    collect = [to_and_from[4 * at : 4 * at + 2] for at in range(LAYERS)]
    spread = [to_and_from[4 * at + 2 : 4 * at + 4] for at in range(LAYERS)]
    moved_at = LAYERS - 1
    whole = shards[0][None]
    for step, axis in enumerate(order_out):
        milestone = None if step < 2 else {2: (to_and_from, sent[0]), 3: sent[1]}.get(step)
        whole = gather_step(whole, axis, milestone)
        if step == 1:
            sent = [
                expert_sent(tie(one[moved_at, 0], whole), split_at, dp_axes, ex_axes)
                for one, split_at in ((w_in, 1), (w_out, 0))
            ]
    full = [gathered(whole, axes, order_out)]
    weights = [(w_in, w_out)] * LAYERS
    cot = pad(cotangent.astype(F32))
    current = pad(x_in.astype(F32))

    dense_flops = 2 * total * width * (4 * width) + 6 * total * slots * width
    kept = []
    tops = []
    back = gates = None
    for at in range(LAYERS):
        combine, last = at > 0, at == LAYERS - 1
        args = [current]
        outs = []
        if combine:
            args += [back, *collect[at - 1], gates]
            outs += [shape((total, width), F32), shape((total, width), BF), shape((total, width), BF)]
        args += [full[at], *spread[at], cols[at]]
        outs += [
            shape((total, width), F32),
            shape((total, 3 * width), BF),
            shape((total, width), BF),
            shape((total, LANES), F32),
            shape((total, LANES), F32),
            shape((total, LANES), F32),
            shape((slots, width), BF),
            shape((8, LANES), F32),
        ]
        if last:
            outs.append(shape((slots, LANES), BF))
        made = list(
            call(
                functools.partial(dense_forward_kernel, experts, images, combine, last),
                outs,
                args,
                dense_flops,
                after=weights[moved_at] if last else [],
            )
        )
        if combine:
            current, first, second = made[:3]
            made = made[3:]
            kept[-1]["routed"] = (first, second)
        x1, qkv, mixed, lse, probs, gates, send, top = made[:8]
        tops.append(top[0, :HEADS])
        rows = exchange(send if at == 0 else tie(send, cot_rows[1]), at)
        if at == 0:
            others = [expert_others(tie(one, send), dp_axes) for one in sent]
            ahead = [one for got in others for one in got]
            whole = tie(shards[1], whole)[None]
            for axis in order_out[:-1]:
                whole = gather_step(whole, axis)
            ahead.append(whole)
        if last:
            gate_rows = exchange(tie(made[8], rows), at)
            active, slope, out_rows, inner = expert_forward(at, cot_rows, rows, *weights[at])
        else:
            active, slope, out_rows = expert_forward(at, [], rows, *weights[at], ahead)
            cot_rows = [exchange(tie(to_and_from[-2], rows), LAYERS - 1)]
            back = exchange(tie(out_rows, cot_rows[0]), at)
            cot_rows.append(exchange(tie(to_and_from[-1], back), LAYERS - 1))
            full.append(
                gathered(gather_step(tie(whole, out_rows), order_out[-1]), axes, order_out)
            )
            weights[moved_at] = [
                expert_joined(one[moved_at, 0], tie(got, out_rows), split_at, dp_axes)
                for one, got, split_at in zip((w_in, w_out), others, (1, 0))
            ]
        kept.append(
            dict(
                x=current,
                x1=x1,
                qkv=qkv,
                mixed=mixed,
                lse=lse,
                probs=probs,
                gates=gates,
                rows=rows,
                active=active,
                slope=slope,
            )
        )
        current = x1
    tops = jnp.pad(jnp.concatenate(tops), (0, LANES - LAYERS * HEADS))
    upstream = cot
    expert_grads = [None] * LAYERS
    dense_grads = [None] * LAYERS
    for at in reversed(range(LAYERS)):
        own = kept[at]
        last, first_layer = at == LAYERS - 1, at == 0
        if last:
            inner = exchange(inner, at)
            grad_hidden, grad_back, grad_rows = expert_backward(
                at, cot_rows, [gate_rows], own["slope"], *weights[at]
            )
            grad_back = tie(grad_back, inner)
        else:
            grad_hidden, grad_back = expert_backward(
                at, [grad_rows], [], own["slope"], *weights[at]
            )
            grad_back = tie(grad_back, head_max)
        grad_back = exchange(grad_back, at)
        pieces = expert_weights(own["rows"], grad_hidden, own["active"], grad_rows, parts)
        if MOVED[at]:
            moved_pieces = [returned_rows(one, dp_axes) for one in pieces]
            out_rows = tie(out_rows, (grad_back, pieces))
        else:
            expert_grads[at] = [
                lax.psum_scatter(
                    one.reshape((-1,) + one.shape[2:]), dp_axes, scatter_dimension=0, tiled=True
                )
                for one in pieces
            ]
        if first_layer:
            moved_pieces = [tie(one, (grad_back, pieces)) for one in moved_pieces]
            crossed = [across(one, dp_axes[-1], ex_axes[0]) for one in moved_pieces]
        args = [upstream, grad_back, *collect[at]]
        if last:
            args.append(inner)
        else:
            args += own["routed"]
        args += [own["probs"], own["gates"], cols[at], own["x"], own["x1"]]
        args += [full[at], own["qkv"], own["mixed"], own["lse"]]
        outs = [shape((total, width), F32), shape((width, 4 * width + LANES), BF)]
        if not first_layer:
            args += [*spread[at - 1], kept[at - 1]["gates"]]
            outs.append(shape((slots, width), BF))
        made = list(
            call(
                functools.partial(dense_backward_kernel, experts, images, last, first_layer),
                outs,
                args,
                2 * dense_flops,
                [pltpu.VMEM((total, 3 * width), BF)],
                pieces,
            )
        )
        upstream, weight_grads = made[:2]
        if not first_layer:
            back = exchange(out_rows, at)
            grad_rows = exchange(tie(made[2], back), at - 1)
        weight_grads = weight_grads.reshape((2,) * len(axes) + (-1,) + weight_grads.shape[1:])
        if first_layer:
            first_left = list(axes)
            weight_grads = tie(weight_grads, crossed[0])
            weight_grads = halve(weight_grads, first_left, order_in[0])
            weight_grads = halve(weight_grads, first_left, order_in[1])
            both = jnp.stack([weight_grads, sums], axis=-3)
            both = tie(halve(both, first_left, order_in[2]), crossed[1])
            for axis in order_in[3:-1]:
                both = halve(both, first_left, axis)
            dense = [
                one.reshape(LAYERS, -1, one.shape[-1])
                for one in halves(both, first_left, order_in[-1])
            ]
        else:
            left = list(axes)
            sums = halve(weight_grads, left, order_in[0])
            sums = halve(sums, left, order_in[1], grad_rows)
            [out_act] = call(
                functools.partial(combine_kernel, images),
                [shape((total, width), F32)],
                [own["x1"], own["gates"], *collect[at], back],
                4 * total * slots * width,
            )
            grad_rows = tie(grad_rows, (out_act, sums))
            everyone = 2 ** len(axes)
            tops = lax.all_to_all(
                jnp.broadcast_to(tie(tops, grad_rows), (everyone, LANES)),
                axes,
                split_axis=0,
                concat_axis=0,
                tiled=True,
            )
            head_max = jnp.max(tops, axis=0)[: LAYERS * HEADS].reshape(LAYERS, HEADS)
    home = [
        returned_home(one, tie(moved, both), dp_axes[-1])
        for one, moved in zip(moved_pieces, crossed)
    ]
    rows = w_o.shape[1]
    finished = call(
        functools.partial(finish_kernel, experts),
        [
            shape((LAYERS, rows, 3 * width), F32),
            shape((LAYERS, rows, width), F32),
            shape((LAYERS, rows, experts), F32),
            shape((LAYERS, 2, rows), F32),
            shape((LAYERS, 2, rows), F32),
            shape((LAYERS, rows), F32),
        ]
        + [shape((LAYERS, 1) + one.shape, F32) for one, _ in home],
        [*dense, *expert_grads[0], home[0][0], home[1][0], home[0][1], home[1][1]],
        1000,
    )
    grad_qkv, grad_o, grad_router, grad_gains, grad_biases, second, grad_in, grad_out = finished
    factor = jnp.sqrt(threshold / jnp.maximum(head_max, threshold))
    columns = jnp.repeat(factor, HEAD_DIM, axis=1)
    clipped_qk = (
        w_qkv[:, :, : 2 * width].astype(F32)
        * jnp.concatenate([columns, columns], axis=1)[:, None, :]
    )
    return (
        unpad(out_act),
        unpad(upstream),
        grad_gains,
        grad_biases,
        grad_qkv,
        grad_o,
        grad_router,
        grad_in,
        grad_out,
        head_max,
        clipped_qk,
        second,
    )


def solution(mesh):
    dp_bits = int(mesh.shape["dp"]).bit_length() - 1
    ex_bits = int(mesh.shape["expert"]).bit_length() - 1
    dp_axes = tuple(f"d{at}" for at in range(dp_bits))
    ex_axes = tuple(f"e{at}" for at in range(ex_bits))
    split = Mesh(mesh.devices.reshape((2,) * (dp_bits + ex_bits)), dp_axes + ex_axes)
    both = dp_axes + ex_axes
    in_specs = (
        P(both, None),
        P(None, None, both),
        P(None, None, both),
        P(None, both, None),
        P(None, both, None),
        P(None, both, None),
        P(None, ex_axes, None, None),
        P(None, ex_axes, None, None),
        P(None, both, None),
        P(),
        P(both, None),
    )
    out_specs = (
        P(both, None),
        P(both, None),
        P(None, None, both),
        P(None, None, both),
        P(None, both, None),
        P(None, both, None),
        P(None, both, None),
        P(None, ex_axes, None, dp_axes),
        P(None, ex_axes, dp_axes, None),
        P(),
        P(None, both, None),
        P(None, both),
    )
    return jax.shard_map(
        functools.partial(body, dp_axes, ex_axes),
        mesh=split,
        in_specs=in_specs,
        out_specs=out_specs,
        check_vma=False,
    )
```

```python
import functools

import jax
import jax.numpy as jnp
import numpy as np
from jax import lax
from jax.experimental import pallas as pl
from jax.experimental.pallas import tpu as pltpu
from jax.sharding import Mesh
from jax.sharding import PartitionSpec as P

HEADS = 8
HEAD_DIM = 64
SEQ = 197
TOP = 2
LAYERS = 2
EPSILON = 1e-06
BF = jnp.bfloat16
F32 = jnp.float32
LANES = 128
PIECES = 4
VMEM = 56 * 1024 * 1024
MOVED = (False, True)


def up16(size):
    return -(-size // 16) * 16


def dot(a, b):
    return jnp.dot(a, b, preferred_element_type=F32)


def dot_last(a, b):
    return lax.dot_general(a, b, (((1,), (1,)), ((), ())), preferred_element_type=F32)


def dot_first(a, b):
    return lax.dot_general(a, b, (((0,), (0,)), ((), ())), preferred_element_type=F32)


def lane_of(rows, lanes=LANES):
    return lax.broadcasted_iota(jnp.int32, (rows, lanes), 1)


def row_of(rows, lanes=LANES):
    return lax.broadcasted_iota(jnp.int32, (rows, lanes), 0)


def normalize(values):
    center = values - jnp.mean(values, axis=-1, keepdims=True)
    inverse = lax.rsqrt(jnp.mean(center * center, axis=-1, keepdims=True) + EPSILON)
    return center * inverse, inverse


def norm_backward(upstream, normed, inverse, gain_row):
    scaled = upstream * gain_row
    mean_plain = jnp.mean(scaled, axis=-1, keepdims=True)
    mean_normed = jnp.mean(scaled * normed, axis=-1, keepdims=True)
    return inverse * (scaled - mean_plain - normed * mean_normed)


def norm_rows(tail, experts):
    picks = (lane_of(8) == row_of(8) + experts).astype(F32).astype(BF)
    return dot_last(picks, tail)


def places_kernel(experts, capacity, cols_ref, rows_ref, cot_ref, *out_refs):
    tokens = cols_ref.shape[1]
    slots = experts * capacity
    square_row = lax.broadcasted_iota(jnp.int32, (tokens, tokens), 0)
    square_col = lax.broadcasted_iota(jnp.int32, (tokens, tokens), 1)
    earlier = (square_col < square_row).astype(F32).astype(BF)
    later = (square_row < square_col).astype(F32).astype(BF)
    wide = max(16, experts)
    for layer_at in range(LAYERS):
        to_tokens, to_slots = out_refs[4 * layer_at : 4 * layer_at + 2], out_refs[
            4 * layer_at + 2 : 4 * layer_at + 4
        ]
        cols = cols_ref[layer_at]
        first, second = cols[:, 0:1], cols[:, 1:2]
        lane = lane_of(tokens)
        matches = jnp.where((lane == first) | (lane == second), 1.0, 0.0)
        before = dot(earlier, matches.astype(BF))
        slot_lane = lax.broadcasted_iota(jnp.int32, (tokens, slots), 1)
        for chosen, out_ref in zip((first, second), to_tokens):
            rank = jnp.sum(jnp.where(lane == chosen, before, 0.0), axis=1, keepdims=True)
            slot = chosen * capacity + rank.astype(jnp.int32)
            out_ref[...] = jnp.where(slot_lane == slot, 1.0, 0.0).astype(BF)
        rows = rows_ref[layer_at]
        first, second = rows[0:1], rows[1:2]
        which = lax.broadcasted_iota(jnp.int32, (wide, tokens), 0)
        matches = jnp.where((which == first) | (which == second), 1.0, 0.0)
        before = dot(matches.astype(BF), later)
        slot_row = lax.broadcasted_iota(jnp.int32, (slots, tokens), 0)
        for chosen, out_ref in zip((first, second), to_slots):
            rank = jnp.sum(jnp.where(which == chosen, before, 0.0), axis=0, keepdims=True)
            slot = chosen * capacity + rank.astype(jnp.int32)
            out_ref[...] = jnp.where(slot_row == slot, 1.0, 0.0).astype(BF)
    for at, out_ref in enumerate(out_refs[4 * LAYERS :]):
        columns = out_ref.shape[1]
        cot = cot_ref[:, at * columns : (at + 1) * columns]
        out_ref[...] = (dot(to_slots[0][...], cot) + dot(to_slots[1][...], cot)).astype(BF)


def two_parts(values):
    high = values.astype(BF)
    return high, (values - high.astype(F32)).astype(BF)


def two_lanes(values):
    high, low = two_parts(values)
    lane = lane_of(values.shape[0])
    high, low = high.astype(F32), low.astype(F32)
    return jnp.where(lane == 0, high, jnp.where(lane == 1, low, 0.0)).astype(BF)


def from_lanes(parts):
    return parts[:, 0:1] + parts[:, 1:2]


def behind(kernel, operands, *refs):
    return kernel(*refs[operands:])


def call(kernel, out_shapes, args, flops, scratch=(), after=()):
    moved = sum(a.size * a.dtype.itemsize for a in args) + sum(
        int(np.prod(o.shape)) * o.dtype.itemsize for o in out_shapes
    )
    whole = pl.BlockSpec(memory_space=pltpu.VMEM)
    return pl.pallas_call(
        functools.partial(behind, kernel, len(after)),
        in_specs=[pl.BlockSpec(memory_space=pl.ANY)] * len(after) + [whole] * len(args),
        out_shape=out_shapes,
        scratch_shapes=list(scratch),
        compiler_params=pltpu.CompilerParams(vmem_limit_bytes=VMEM),
        cost_estimate=pl.CostEstimate(
            flops=int(flops), bytes_accessed=int(moved), transcendentals=0
        ),
    )(*after, *args)


def shape(dims, dtype):
    return jax.ShapeDtypeStruct(dims, dtype)


def half_masks():
    lane = lane_of(1)
    return (
        jnp.where(lane < HEAD_DIM, 1.0, 0.0).astype(BF),
        jnp.where(lane < HEAD_DIM, 0.0, 1.0).astype(BF),
    )


def dense_forward_kernel(experts, images, combine, last, *refs):
    refs = list(refs)
    take = lambda: refs.pop(0)
    x_ref = take()
    if combine:
        back_ref, take_first, take_second, gates_before = take(), take(), take(), take()
    full_ref, to_first, to_second, cols_ref = take(), take(), take(), take()
    if combine:
        x_out, first_out, second_out = take(), take(), take()
    x1_out, qkv_out, mixed_out, lse_out, probs_out, gates_out, send_out, top_out = (
        take() for _ in range(8)
    )
    if last:
        send_gates_out = take()
    tokens, width = x_ref.shape
    rows_of = tokens // images
    x = x_ref[...]
    if combine:
        back = back_ref[...]
        first = dot(take_first[...], back)
        second = dot(take_second[...], back)
        gates = gates_before[...]
        x = x + (gates[:, 0:1] * first + gates[:, 1:2] * second)
        x_out[...] = x
        first_out[...] = first.astype(BF)
        second_out[...] = second.astype(BF)
    tail = full_ref[:, 4 * width :]
    norms = norm_rows(tail, experts)
    unit, _ = normalize(x)
    n1 = (unit * norms[0:1] + norms[2:3]).astype(BF)
    qkv_out[...] = dot(n1, full_ref[:, : 3 * width]).astype(BF)
    masks = half_masks()
    key_at = lax.broadcasted_iota(jnp.int32, (rows_of, rows_of), 1)
    query_at = lax.broadcasted_iota(jnp.int32, (rows_of, 1), 0)
    lane = lane_of(rows_of)
    top_lane = lane_of(8)
    tops = jnp.full((8, LANES), -jnp.inf, F32)
    scale = HEAD_DIM**-0.5
    for image in range(images):
        rows = slice(image * rows_of, (image + 1) * rows_of)
        lse = jnp.zeros((rows_of, LANES), F32)
        for pair in range(HEADS // 2):
            at = pair * LANES
            q = qkv_out[rows, at : at + LANES]
            k = qkv_out[rows, width + at : width + at + LANES]
            v = qkv_out[rows, 2 * width + at : 2 * width + at + LANES]
            mixed = None
            for half in range(2):
                scores = dot_last(q * masks[half], k) * scale
                scores = jnp.where(key_at < SEQ, scores, -jnp.inf)
                highest = jnp.max(scores, axis=-1, keepdims=True)
                top = jnp.max(
                    jnp.where(query_at < SEQ, highest, -jnp.inf), axis=0, keepdims=True
                )
                weights = jnp.exp(scores - highest)
                total = jnp.sum(weights, axis=-1, keepdims=True)
                weights = (weights * (1.0 / total)).astype(BF)
                part = dot(weights, v * masks[half])
                mixed = part if mixed is None else mixed + part
                head = 2 * pair + half
                lse = jnp.where(lane == head, highest + jnp.log(total), lse)
                tops = jnp.where(top_lane == head, jnp.maximum(tops, top), tops)
            mixed_out[rows, at : at + LANES] = mixed.astype(BF)
        lse_out[rows, :] = lse
    top_out[...] = tops
    x1 = x + dot(mixed_out[...], full_ref[:, 3 * width : 4 * width])
    x1_out[...] = x1
    unit, _ = normalize(x1)
    n2 = (unit * norms[1:2] + norms[3:4]).astype(BF)
    lane = lane_of(tokens)
    logits = jnp.where(lane < experts, dot(n2, tail), -jnp.inf)
    probs = jnp.exp(logits - jnp.max(logits, axis=-1, keepdims=True))
    probs = probs / jnp.sum(probs, axis=-1, keepdims=True)
    probs_out[...] = probs
    first, second = cols_ref[:, 0:1], cols_ref[:, 1:2]
    picked = [
        jnp.sum(jnp.where(lane == chosen, probs, 0.0), axis=1, keepdims=True)
        for chosen in (first, second)
    ]
    total = jnp.where(first >= 0, picked[0] + picked[1], 1.0)
    gates = [one / total for one in picked]
    packed = jnp.zeros((tokens, LANES), F32)
    for at, column in enumerate((gates[0], gates[1], total, picked[0], picked[1])):
        packed = jnp.where(lane == at, column, packed)
    gates_out[...] = packed
    send_out[...] = dot(to_first[...] + to_second[...], n2).astype(BF)
    if last:
        send_gates_out[...] = (
            dot(to_first[...], two_lanes(gates[0])) + dot(to_second[...], two_lanes(gates[1]))
        ).astype(BF)


def expert_forward_kernel(last, *refs):
    refs = list(refs)
    if last:
        grad_refs, inner_out = (refs.pop(0), refs.pop(0)), refs.pop()
    rows_ref, win_ref, wout_ref, active_out, slope_out, out_ref = refs
    units = win_ref.shape[1] // 2
    factor = (2.0 / np.pi) ** 0.5
    rows = rows_ref[...]
    hidden = dot(rows, win_ref[:, :units])
    total = before = None
    for piece in range(2):
        at = slice(piece * units, (piece + 1) * units)
        later = dot(rows, win_ref[:, units:]) if piece == 0 else None
        square = hidden * hidden
        gate = 0.5 + 0.5 * jnp.tanh(hidden * (factor + (0.044715 * factor) * square))
        active = hidden * gate
        slope = active * (2 * factor + (6 * 0.044715 * factor) * square)
        slope_out[:, at] = (gate + slope * (1.0 - gate)).astype(BF)
        active = active.astype(BF)
        active_out[:, at] = active
        if piece == 1:
            total = dot(before, wout_ref[:units, :]) + dot(active, wout_ref[units:, :])
        before, hidden = active, later
    total = total.astype(BF)
    out_ref[...] = total
    if last:
        half = total.shape[1] // 2
        inner_out[...] = two_lanes(
            jnp.sum(
                total[:, :half].astype(F32) * grad_refs[0][...].astype(F32)
                + total[:, half:].astype(F32) * grad_refs[1][...].astype(F32),
                axis=1,
                keepdims=True,
            )
        )


def weight_spec(weight, layer_at):
    if weight.ndim == 4:
        return pl.BlockSpec((None, None) + weight.shape[2:], lambda i: (layer_at, 0, 0, 0))
    return pl.BlockSpec(weight.shape, lambda i: (0, 0))


def expert_forward(layer_at, grads, rows_in, weight_in, weight_out, after=()):
    last = len(grads) > 0
    slots, width = rows_in.shape
    hidden_units = weight_in.shape[-1]
    chunk = slots // 4
    return pl.pallas_call(
        functools.partial(behind, functools.partial(expert_forward_kernel, last), len(after)),
        grid=(4,),
        in_specs=[pl.BlockSpec(memory_space=pl.ANY)] * len(after)
        + [pl.BlockSpec((chunk, width // 2), lambda i: (i, 0))] * len(grads)
        + [
            pl.BlockSpec((chunk, width), lambda i: (i, 0)),
            weight_spec(weight_in, layer_at),
            weight_spec(weight_out, layer_at),
        ],
        out_specs=[
            pl.BlockSpec((chunk, hidden_units), lambda i: (i, 0)),
            pl.BlockSpec((chunk, hidden_units), lambda i: (i, 0)),
            pl.BlockSpec((chunk, width), lambda i: (i, 0)),
        ]
        + [pl.BlockSpec((chunk, LANES), lambda i: (i, 0))] * last,
        out_shape=[
            shape((slots, hidden_units), BF),
            shape((slots, hidden_units), BF),
            shape((slots, width), BF),
        ]
        + [shape((slots, LANES), BF)] * last,
        compiler_params=pltpu.CompilerParams(vmem_limit_bytes=VMEM),
        cost_estimate=pl.CostEstimate(
            flops=4 * slots * width * hidden_units,
            bytes_accessed=slots * (hidden_units * 4 + width * 4) + 4 * width * hidden_units,
            transcendentals=slots * hidden_units,
        ),
    )(*after, *grads, rows_in, weight_in, weight_out)


def expert_backward_kernel(gated, *refs):
    refs = list(refs)
    grad_ref = refs.pop(0)
    if gated:
        second_ref, gates_ref, scaled = refs.pop(0), refs.pop(0), refs.pop()
        gates = from_lanes(gates_ref[...].astype(F32))
        half = grad_ref.shape[1]
        scaled[:, :half] = (gates * grad_ref[...].astype(F32)).astype(BF)
        scaled[:, half:] = (gates * second_ref[...].astype(F32)).astype(BF)
        grad_ref = scaled
    slope_ref, win_ref, wout_ref, hidden_out, out_ref = refs
    units = win_ref.shape[1] // PIECES
    for piece in range(PIECES):
        at = slice(piece * units, (piece + 1) * units)
        grad_active = dot_last(grad_ref[...], wout_ref[at, :])
        hidden_out[:, at] = (grad_active * slope_ref[:, at].astype(F32)).astype(BF)
    out_ref[...] = dot_last(hidden_out[...], win_ref[...]).astype(BF)


def expert_backward(layer_at, grads, gates, slope, weight_in, weight_out):
    slots, width = grads[0].shape[0], weight_in.shape[-2]
    hidden_units = weight_in.shape[-1]
    chunk = slots // 4
    gated = len(gates)
    rows_spec = lambda lanes: pl.BlockSpec((chunk, lanes), lambda i: (i, 0))
    return pl.pallas_call(
        functools.partial(expert_backward_kernel, gated),
        grid=(4,),
        in_specs=[rows_spec(one.shape[1]) for one in grads]
        + [rows_spec(LANES)] * gated
        + [
            rows_spec(hidden_units),
            weight_spec(weight_in, layer_at),
            weight_spec(weight_out, layer_at),
        ],
        out_specs=[rows_spec(hidden_units), rows_spec(width)] + [rows_spec(width)] * gated,
        out_shape=[shape((slots, hidden_units), BF), shape((slots, width), BF)]
        + [shape((slots, width), BF)] * gated,
        compiler_params=pltpu.CompilerParams(vmem_limit_bytes=VMEM),
        cost_estimate=pl.CostEstimate(
            flops=4 * slots * width * hidden_units,
            bytes_accessed=slots * (hidden_units * 4 + width * 4) + 4 * width * hidden_units,
            transcendentals=0,
        ),
    )(*grads, *gates, slope, weight_in, weight_out)


def expert_weights_kernel(rows_ref, hidden_ref, active_ref, grad_ref, in_out, out_out):
    in_out[0] = dot_first(rows_ref[...], hidden_ref[...]).astype(BF)
    out_out[0] = dot_first(active_ref[...], grad_ref[...]).astype(BF)


def expert_weights(rows_in, grad_hidden, active, grad_rows, pieces):
    slots, width = rows_in.shape
    hidden_units = active.shape[1]
    block = hidden_units // pieces
    return pl.pallas_call(
        expert_weights_kernel,
        grid=(pieces,),
        in_specs=[
            pl.BlockSpec((slots, width), lambda i: (0, 0)),
            pl.BlockSpec((slots, block), lambda i: (0, i)),
            pl.BlockSpec((slots, block), lambda i: (0, i)),
            pl.BlockSpec((slots, width), lambda i: (0, 0)),
        ],
        out_specs=[
            pl.BlockSpec((1, width, block), lambda i: (i, 0, 0)),
            pl.BlockSpec((1, block, width), lambda i: (i, 0, 0)),
        ],
        out_shape=[shape((pieces, width, block), BF), shape((pieces, block, width), BF)],
        compiler_params=pltpu.CompilerParams(vmem_limit_bytes=VMEM),
        cost_estimate=pl.CostEstimate(
            flops=4 * slots * width * hidden_units,
            bytes_accessed=slots * (hidden_units * 4 + width * 4) + 4 * width * hidden_units,
            transcendentals=0,
        ),
    )(rows_in, grad_hidden, active, grad_rows)


def dense_backward_kernel(experts, images, last, first_layer, *refs):
    refs = list(refs)
    take = lambda: refs.pop(0)
    g_ref, rows_ref, take_first, take_second = take(), take(), take(), take()
    if last:
        inner_ref = take()
    else:
        first_ref, second_ref = take(), take()
    probs_ref, gates_ref, cols_ref, x_ref, x1_ref = (take() for _ in range(5))
    full_ref, qkv_ref, mixed_ref, lse_ref = (take() for _ in range(4))
    if not first_layer:
        to_first, to_second, gates_below = take(), take(), take()
    g_out, weights_out = take(), take()
    if not first_layer:
        send_out = take()
    grad_qkv = take()
    tokens, width = g_ref.shape
    rows_of = tokens // images
    g = g_ref[...]
    gates = gates_ref[...]
    x1 = x1_ref[...]
    if last:
        inner = inner_ref[...]
        grad_gates = [from_lanes(dot(one[...], inner)) for one in (take_first, take_second)]
    else:
        grad_gates = [
            jnp.sum(g * one[...].astype(F32), axis=1, keepdims=True)
            for one in (first_ref, second_ref)
        ]
    weighted = grad_gates[0] * gates[:, 0:1] + grad_gates[1] * gates[:, 1:2]
    amounts = [
        (grad_gates[at] - weighted) / gates[:, 2:3] * gates[:, 3 + at : 4 + at]
        for at in range(TOP)
    ]
    lane = lane_of(tokens)
    chosen = [jnp.where(lane == cols_ref[:, at : at + 1], amounts[at], 0.0) for at in range(TOP)]
    grad_logits = (
        (chosen[0] + chosen[1]) - probs_ref[...] * (amounts[0] + amounts[1])
    ).astype(BF)
    tail = full_ref[:, 4 * width :]
    norms = norm_rows(tail, experts)
    rows = rows_ref[...]
    grad_n2 = dot(take_first[...] + take_second[...], rows) + dot_last(grad_logits, tail)
    unit2, inverse2 = normalize(x1)
    n2 = (unit2 * norms[1:2] + norms[3:4]).astype(BF)
    grad_x1 = g + norm_backward(grad_n2, unit2, inverse2, norms[1:2])
    grad_attn = grad_x1.astype(BF)
    grad_mixed = dot_last(grad_attn, full_ref[:, 3 * width : 4 * width]).astype(BF)
    masks = half_masks()
    key_at = lax.broadcasted_iota(jnp.int32, (rows_of, rows_of), 1)
    scale = HEAD_DIM**-0.5
    for image in range(images):
        rows = slice(image * rows_of, (image + 1) * rows_of)
        for pair in range(HEADS // 2):
            at = pair * LANES
            q = qkv_ref[rows, at : at + LANES]
            k = qkv_ref[rows, width + at : width + at + LANES]
            v = qkv_ref[rows, 2 * width + at : 2 * width + at + LANES]
            gm = grad_mixed[rows, at : at + LANES]
            sums = [None] * 3
            for half in range(2):
                head = 2 * pair + half
                mask = masks[half]
                scores = dot_last(q * mask, k) * scale
                weights = jnp.exp(scores - lse_ref[rows, head : head + 1])
                weights = jnp.where(key_at < SEQ, weights, 0.0)
                grad_weights = dot_last(gm * mask, v)
                inner = jnp.sum(grad_weights * weights, axis=-1, keepdims=True)
                grad_scores = (weights * (grad_weights - inner)).astype(BF)
                parts = (
                    dot(grad_scores, k * mask),
                    dot_first(grad_scores, q * mask),
                    dot_first(weights.astype(BF), gm * mask),
                )
                sums = [b if a is None else a + b for a, b in zip(sums, parts)]
            grad_qkv[rows, at : at + LANES] = (sums[0] * scale).astype(BF)
            grad_qkv[rows, width + at : width + at + LANES] = (sums[1] * scale).astype(BF)
            grad_qkv[rows, 2 * width + at : 2 * width + at + LANES] = sums[2].astype(BF)
    unit1, inverse1 = normalize(x_ref[...])
    n1 = (unit1 * norms[0:1] + norms[2:3]).astype(BF)
    grad_n1 = dot_last(grad_qkv[...], full_ref[:, : 3 * width])
    g_below = grad_x1 + norm_backward(grad_n1, unit1, inverse1, norms[0:1])
    g_out[...] = g_below
    if not first_layer:
        gates = gates_below[...]
        send_out[...] = (
            dot(to_first[...], (gates[:, 0:1] * g_below).astype(BF))
            + dot(to_second[...], (gates[:, 1:2] * g_below).astype(BF))
        ).astype(BF)
    weights_out[:, : 3 * width] = dot_first(n1, grad_qkv[...]).astype(BF)
    weights_out[:, 3 * width : 4 * width] = dot_first(mixed_ref[...], grad_attn).astype(BF)
    row = lax.broadcasted_iota(jnp.int32, (8, width), 0)
    norm_grads = jnp.zeros((8, width), F32)
    for at, total in enumerate((grad_n1 * unit1, grad_n2 * unit2, grad_n1, grad_n2)):
        norm_grads = jnp.where(row == at, jnp.sum(total, axis=0, keepdims=True), norm_grads)
    picks = (lane_of(8) == row_of(8) + experts).astype(F32).astype(BF)
    weights_out[:, 4 * width :] = (
        dot_first(n2, grad_logits) + dot_first(norm_grads.astype(BF), picks)
    ).astype(BF)


def combine_kernel(images, x1_ref, gates_ref, take_first, take_second, back_ref, out_ref):
    back = back_ref[...]
    gates = gates_ref[...]
    out = x1_ref[...] + (
        gates[:, 0:1] * dot(take_first[...], back) + gates[:, 1:2] * dot(take_second[...], back)
    )
    out_ref[...] = out


def pack_kernel(experts, qkv_ref, o_ref, router_ref, gains_ref, biases_ref, *out_refs):
    width = o_ref.shape[2]
    router_lanes = (lane_of(experts) == row_of(experts)).astype(F32).astype(BF)
    gains_lanes = (lane_of(2) == row_of(2) + experts).astype(F32).astype(BF)
    biases_lanes = (lane_of(2) == row_of(2) + experts + 2).astype(F32).astype(BF)
    for at, out_ref in enumerate(out_refs):
        out_ref[:, : 3 * width] = qkv_ref[at]
        out_ref[:, 3 * width : 4 * width] = o_ref[at]
        out_ref[:, 4 * width :] = (
            dot_first(router_ref[at], router_lanes)
            + dot_first(gains_ref[at], gains_lanes)
            + dot_first(biases_ref[at], biases_lanes)
        ).astype(BF)


def finish_kernel(experts, *refs):
    sums, outs = refs[:12], refs[12:]
    keep_ref, more_ref = sums[:2]
    qkv_out, o_out, router_out, gains_out, biases_out, second_out, in_out, wout_out = outs
    width = o_out.shape[2]
    picks = jnp.where(lane_of(8) == row_of(8) + experts, 1.0, 0.0)
    for at in range(LAYERS):
        dense = keep_ref[at].astype(F32) + more_ref[at].astype(F32)
        qkv_out[at] = dense[:, : 3 * width]
        o_out[at] = dense[:, 3 * width : 4 * width]
        tail = dense[:, 4 * width :]
        router_out[at] = tail[:, :experts]
        norms = lax.dot_general(
            picks, tail, (((1,), (1,)), ((), ())), precision=lax.Precision.HIGHEST
        )
        gains_out[at] = norms[0:2]
        biases_out[at] = norms[2:4]
        second_out[at : at + 1] = norms[3:4]
    for number, out_ref in enumerate((in_out, wout_out)):
        out_ref[0, 0] = sums[2 + number][...].astype(F32)
        for half in range(2):
            keep_ref, more_ref = sums[4 + 4 * number + 2 * half :][:2]
            rows = keep_ref.shape[0]
            at = slice(half * rows, (half + 1) * rows)
            out_ref[1, 0, at] = keep_ref[...].astype(F32) + more_ref[...].astype(F32)


def other(values, axis):
    return lax.ppermute(values, axis, [(0, 1), (1, 0)])


def across(values, core_axis, axis):
    if axis < core_axis:
        return lax.ppermute(values, (axis, core_axis), [(1, 3), (3, 1)])
    return lax.ppermute(values, (core_axis, axis), [(2, 3), (3, 2)])


def expert_sent(weight, split_at, dp_axes, ex_axes):
    row_axes = dp_axes[:-1]
    size = weight.shape[split_at] // 2 ** len(row_axes)
    place = lax.axis_index(row_axes) if row_axes else 0
    own = lax.dynamic_slice_in_dim(weight, place * size, size, split_at)
    return across(own, dp_axes[-1], ex_axes[0])


def expert_others(got, dp_axes):
    got = [got]
    for axis in dp_axes[:-1][::-1]:
        got = got + [across(one, dp_axes[-1], axis) for one in got]
    return got


def expert_joined(weight, got, split_at, dp_axes):
    row_axes = dp_axes[:-1]
    place = lax.axis_index(row_axes) if row_axes else 0
    first = lax.axis_index(dp_axes[-1]) == 0
    size = weight.shape[split_at] // len(got)
    blocks = []
    for at in range(len(got)):
        theirs = got[at]
        for p, one in enumerate(got):
            theirs = jnp.where(place == at ^ p, one, theirs)
        own = lax.slice_in_dim(weight, at * size, (at + 1) * size, axis=split_at)
        blocks.append(jnp.where(first, own, theirs))
    return jnp.concatenate(blocks, axis=split_at)


def returned_rows(pieces, dp_axes):
    row_axes = dp_axes[:-1]
    pieces = pieces.reshape((-1,) + pieces.shape[2:])
    pieces = lax.psum_scatter(pieces, row_axes, scatter_dimension=0, tiled=True)
    return pieces.reshape((2, -1) + pieces.shape[1:])


def returned_home(pieces, moved, core_axis):
    core = lax.axis_index(core_axis)
    mine = jnp.where(core == 0, pieces, moved)
    keep = lax.dynamic_index_in_dim(mine, core, 0, keepdims=False)
    send = lax.dynamic_index_in_dim(mine, 1 - core, 0, keepdims=False)
    return keep, other(send, core_axis)


def add_low(a, b):
    return (a.astype(F32) + b.astype(F32)).astype(BF)


def gather_step(whole, axis, milestone=None):
    theirs = other(whole, axis)
    if milestone is not None:
        theirs = tie(theirs, milestone)
    mine_first = lax.axis_index(axis) == 0
    return jnp.stack([jnp.where(mine_first, whole, theirs), jnp.where(mine_first, theirs, whole)])


def gathered(whole, axes, order):
    rows, columns = whole.shape[-2:]
    whole = whole.reshape((2,) * len(axes) + (rows, columns))
    places = tuple(order[::-1].index(axis) for axis in axes)
    whole = whole.transpose(places + (len(axes), len(axes) + 1))
    return whole.reshape(-1, columns)


def tie(values, milestone):
    return lax.optimization_barrier((values, milestone))[0]


def halves(values, left, axis, milestone=None):
    at = left.index(axis)
    mine = lax.axis_index(axis)
    keep = lax.dynamic_index_in_dim(values, mine, at, keepdims=False)
    theirs = other(lax.dynamic_index_in_dim(values, 1 - mine, at, keepdims=False), axis)
    if milestone is not None:
        theirs = tie(theirs, milestone)
    left.remove(axis)
    return keep, theirs


def halve(values, left, axis, milestone=None):
    return add_low(*halves(values, left, axis, milestone))


def body(
    dp_axes,
    ex_axes,
    x_in,
    norm_gains,
    norm_biases,
    w_qkv,
    w_o,
    w_router,
    w_in,
    w_out,
    routes,
    threshold,
    cotangent,
):
    axes = dp_axes + ex_axes
    group = dp_axes[-1:] + ex_axes[1:]
    order_out = ex_axes[::-1][1:] + ex_axes[-1:] + dp_axes
    order_in = dp_axes[-1:] + ex_axes[1:][::-1] + dp_axes[:-1][::-1] + ex_axes[:1]
    experts = 2 ** len(ex_axes)
    parts = 2 ** len(dp_axes)
    tokens, width = x_in.shape
    images = tokens // SEQ
    padded = up16(SEQ)
    capacity = -(-(4 * tokens // experts) // 8) * 8
    slots = experts * capacity
    total = images * padded

    def pad(values, fill=0):
        values = values.reshape((images, SEQ) + values.shape[1:])
        values = jnp.pad(
            values, ((0, 0), (0, padded - SEQ), (0, 0)), constant_values=fill
        )
        return values.reshape((total,) + values.shape[2:])

    def unpad(values):
        return values.reshape(images, padded, -1)[:, :SEQ].reshape(tokens, -1)

    shards = call(
        functools.partial(pack_kernel, experts),
        [shape((w_o.shape[1], 4 * width + LANES), BF)] * LAYERS,
        (w_qkv, w_o, w_router.transpose(0, 2, 1), norm_gains, norm_biases),
        1000,
    )
    def exchange(rows, at):
        over = group if MOVED[at] else ex_axes
        return lax.all_to_all(rows, over, split_axis=0, concat_axis=0, tiled=True)

    cols = [pad(routes[at], -1) for at in range(LAYERS)]
    half_away = lax.axis_index(ex_axes[0]) * (experts // 2)
    route_cols = jnp.stack(
        [
            pad((routes[at] + half_away) % experts if MOVED[at] else routes[at], -1)
            for at in range(LAYERS)
        ]
    )
    to_and_from = call(
        functools.partial(places_kernel, experts, capacity),
        [shape(s, BF) for s in ((total, slots),) * 2 + ((slots, total),) * 2] * LAYERS
        + [shape((slots, width // 2), BF)] * 2,
        (route_cols, route_cols.transpose(0, 2, 1), pad(cotangent)),
        LAYERS * 4 * total * total * LANES,
    )
    collect = [to_and_from[4 * at : 4 * at + 2] for at in range(LAYERS)]
    spread = [to_and_from[4 * at + 2 : 4 * at + 4] for at in range(LAYERS)]
    moved_at = LAYERS - 1
    whole = shards[0][None]
    for step, axis in enumerate(order_out):
        milestone = None if step < 2 else {2: (to_and_from, sent[0]), 3: sent[1]}.get(step)
        whole = gather_step(whole, axis, milestone)
        if step == 1:
            sent = [
                expert_sent(tie(one[moved_at, 0], whole), split_at, dp_axes, ex_axes)
                for one, split_at in ((w_in, 1), (w_out, 0))
            ]
    full = [gathered(whole, axes, order_out)]
    weights = [(w_in, w_out)] * LAYERS
    cot = pad(cotangent.astype(F32))
    current = pad(x_in.astype(F32))

    dense_flops = 2 * total * width * (4 * width) + 6 * total * slots * width
    kept = []
    tops = []
    back = gates = None
    for at in range(LAYERS):
        combine, last = at > 0, at == LAYERS - 1
        args = [current]
        outs = []
        if combine:
            args += [back, *collect[at - 1], gates]
            outs += [shape((total, width), F32), shape((total, width), BF), shape((total, width), BF)]
        args += [full[at], *spread[at], cols[at]]
        outs += [
            shape((total, width), F32),
            shape((total, 3 * width), BF),
            shape((total, width), BF),
            shape((total, LANES), F32),
            shape((total, LANES), F32),
            shape((total, LANES), F32),
            shape((slots, width), BF),
            shape((8, LANES), F32),
        ]
        if last:
            outs.append(shape((slots, LANES), BF))
        made = list(
            call(
                functools.partial(dense_forward_kernel, experts, images, combine, last),
                outs,
                args,
                dense_flops,
                after=weights[moved_at] if last else [],
            )
        )
        if combine:
            current, first, second = made[:3]
            made = made[3:]
            kept[-1]["routed"] = (first, second)
        x1, qkv, mixed, lse, probs, gates, send, top = made[:8]
        tops.append(top[0, :HEADS])
        rows = exchange(send if at == 0 else tie(send, cot_rows[1]), at)
        if at == 0:
            others = [expert_others(tie(one, send), dp_axes) for one in sent]
            ahead = [one for got in others for one in got]
            whole = tie(shards[1], whole)[None]
            for axis in order_out[:-1]:
                whole = gather_step(whole, axis)
            ahead.append(whole)
        if last:
            gate_rows = exchange(tie(made[8], rows), at)
            active, slope, out_rows, inner = expert_forward(at, cot_rows, rows, *weights[at])
        else:
            active, slope, out_rows = expert_forward(at, [], rows, *weights[at], ahead)
            cot_rows = [exchange(tie(to_and_from[-2], rows), LAYERS - 1)]
            back = exchange(tie(out_rows, cot_rows[0]), at)
            cot_rows.append(exchange(tie(to_and_from[-1], back), LAYERS - 1))
            full.append(
                gathered(gather_step(tie(whole, out_rows), order_out[-1]), axes, order_out)
            )
            weights[moved_at] = [
                expert_joined(one[moved_at, 0], tie(got, out_rows), split_at, dp_axes)
                for one, got, split_at in zip((w_in, w_out), others, (1, 0))
            ]
        kept.append(
            dict(
                x=current,
                x1=x1,
                qkv=qkv,
                mixed=mixed,
                lse=lse,
                probs=probs,
                gates=gates,
                rows=rows,
                active=active,
                slope=slope,
            )
        )
        current = x1
    tops = jnp.pad(jnp.concatenate(tops), (0, LANES - LAYERS * HEADS))
    upstream = cot
    expert_grads = [None] * LAYERS
    dense_grads = [None] * LAYERS
    for at in reversed(range(LAYERS)):
        own = kept[at]
        last, first_layer = at == LAYERS - 1, at == 0
        if last:
            inner = exchange(inner, at)
            grad_hidden, grad_back, grad_rows = expert_backward(
                at, cot_rows, [gate_rows], own["slope"], *weights[at]
            )
            grad_back = tie(grad_back, inner)
        else:
            grad_hidden, grad_back = expert_backward(
                at, [grad_rows], [], own["slope"], *weights[at]
            )
            grad_back = tie(grad_back, head_max)
        grad_back = exchange(grad_back, at)
        pieces = expert_weights(own["rows"], grad_hidden, own["active"], grad_rows, parts)
        if MOVED[at]:
            moved_pieces = [returned_rows(one, dp_axes) for one in pieces]
            moved_pieces = [half for one in moved_pieces for half in jnp.split(one, 2, axis=1)]
            out_rows = tie(out_rows, (grad_back, pieces))
        else:
            expert_grads[at] = [
                lax.psum_scatter(
                    one.reshape((-1,) + one.shape[2:]), dp_axes, scatter_dimension=0, tiled=True
                )
                for one in pieces
            ]
        if first_layer:
            moved_pieces = [tie(one, (grad_back, pieces)) for one in moved_pieces]
            crossed = [across(one, dp_axes[-1], ex_axes[0]) for one in moved_pieces]
        args = [upstream, grad_back, *collect[at]]
        if last:
            args.append(inner)
        else:
            args += own["routed"]
        args += [own["probs"], own["gates"], cols[at], own["x"], own["x1"]]
        args += [full[at], own["qkv"], own["mixed"], own["lse"]]
        outs = [shape((total, width), F32), shape((width, 4 * width + LANES), BF)]
        if not first_layer:
            args += [*spread[at - 1], kept[at - 1]["gates"]]
            outs.append(shape((slots, width), BF))
        made = list(
            call(
                functools.partial(dense_backward_kernel, experts, images, last, first_layer),
                outs,
                args,
                2 * dense_flops,
                [pltpu.VMEM((total, 3 * width), BF)],
                pieces,
            )
        )
        upstream, weight_grads = made[:2]
        if not first_layer:
            back = exchange(out_rows, at)
            grad_rows = exchange(tie(made[2], back), at - 1)
        weight_grads = weight_grads.reshape((2,) * len(axes) + (-1,) + weight_grads.shape[1:])
        if first_layer:
            first_left = list(axes)
            weight_grads = tie(weight_grads, crossed[0])
            weight_grads = halve(weight_grads, first_left, order_in[0])
            weight_grads = halve(weight_grads, first_left, order_in[1], crossed[1])
            both = jnp.stack([weight_grads, sums], axis=-3)
            both = halve(both, first_left, order_in[2], crossed[2])
            both = halve(both, first_left, order_in[3], crossed[3])
            for axis in order_in[4:-1]:
                both = halve(both, first_left, axis)
            dense = [
                one.reshape(LAYERS, -1, one.shape[-1])
                for one in halves(both, first_left, order_in[-1])
            ]
        else:
            left = list(axes)
            sums = halve(weight_grads, left, order_in[0])
            sums = halve(sums, left, order_in[1], grad_rows)
            [out_act] = call(
                functools.partial(combine_kernel, images),
                [shape((total, width), F32)],
                [own["x1"], own["gates"], *collect[at], back],
                4 * total * slots * width,
            )
            grad_rows = tie(grad_rows, (out_act, sums))
            everyone = 2 ** len(axes)
            tops = lax.all_to_all(
                jnp.broadcast_to(tie(tops, grad_rows), (everyone, LANES)),
                axes,
                split_axis=0,
                concat_axis=0,
                tiled=True,
            )
            head_max = jnp.max(tops, axis=0)[: LAYERS * HEADS].reshape(LAYERS, HEADS)
    home = [
        returned_home(one, tie(moved, both), dp_axes[-1])
        for one, moved in zip(moved_pieces, crossed)
    ]
    rows = w_o.shape[1]
    finished = call(
        functools.partial(finish_kernel, experts),
        [
            shape((LAYERS, rows, 3 * width), F32),
            shape((LAYERS, rows, width), F32),
            shape((LAYERS, rows, experts), F32),
            shape((LAYERS, 2, rows), F32),
            shape((LAYERS, 2, rows), F32),
            shape((LAYERS, rows), F32),
        ]
        + [shape((LAYERS, 1) + one.shape, F32) for one in expert_grads[0]],
        [*dense, *expert_grads[0], *(one for pair in home for one in pair)],
        1000,
    )
    grad_qkv, grad_o, grad_router, grad_gains, grad_biases, second, grad_in, grad_out = finished
    factor = jnp.sqrt(threshold / jnp.maximum(head_max, threshold))
    columns = jnp.repeat(factor, HEAD_DIM, axis=1)
    clipped_qk = (
        w_qkv[:, :, : 2 * width].astype(F32)
        * jnp.concatenate([columns, columns], axis=1)[:, None, :]
    )
    return (
        unpad(out_act),
        unpad(upstream),
        grad_gains,
        grad_biases,
        grad_qkv,
        grad_o,
        grad_router,
        grad_in,
        grad_out,
        head_max,
        clipped_qk,
        second,
    )


def solution(mesh):
    dp_bits = int(mesh.shape["dp"]).bit_length() - 1
    ex_bits = int(mesh.shape["expert"]).bit_length() - 1
    dp_axes = tuple(f"d{at}" for at in range(dp_bits))
    ex_axes = tuple(f"e{at}" for at in range(ex_bits))
    split = Mesh(mesh.devices.reshape((2,) * (dp_bits + ex_bits)), dp_axes + ex_axes)
    both = dp_axes + ex_axes
    in_specs = (
        P(both, None),
        P(None, None, both),
        P(None, None, both),
        P(None, both, None),
        P(None, both, None),
        P(None, both, None),
        P(None, ex_axes, None, None),
        P(None, ex_axes, None, None),
        P(None, both, None),
        P(),
        P(both, None),
    )
    out_specs = (
        P(both, None),
        P(both, None),
        P(None, None, both),
        P(None, None, both),
        P(None, both, None),
        P(None, both, None),
        P(None, both, None),
        P(None, ex_axes, None, dp_axes),
        P(None, ex_axes, dp_axes, None),
        P(),
        P(None, both, None),
        P(None, both),
    )
    return jax.shard_map(
        functools.partial(body, dp_axes, ex_axes),
        mesh=split,
        in_specs=in_specs,
        out_specs=out_specs,
        check_vma=False,
    )
```

```python
import functools

import jax
import jax.numpy as jnp
import numpy as np
from jax import lax
from jax.experimental import pallas as pl
from jax.experimental.pallas import tpu as pltpu
from jax.sharding import Mesh
from jax.sharding import PartitionSpec as P

HEADS = 8
HEAD_DIM = 64
SEQ = 197
TOP = 2
LAYERS = 2
EPSILON = 1e-06
BF = jnp.bfloat16
F32 = jnp.float32
LANES = 128
PIECES = 4
VMEM = 56 * 1024 * 1024
VMEM_EX = 47 * 1024 * 1024
MOVED = (False, True)


def up16(size):
    return -(-size // 16) * 16


def dot(a, b):
    return jnp.dot(a, b, preferred_element_type=F32)


def dot_last(a, b):
    return lax.dot_general(a, b, (((1,), (1,)), ((), ())), preferred_element_type=F32)


def dot_first(a, b):
    return lax.dot_general(a, b, (((0,), (0,)), ((), ())), preferred_element_type=F32)


def lane_of(rows, lanes=LANES):
    return lax.broadcasted_iota(jnp.int32, (rows, lanes), 1)


def row_of(rows, lanes=LANES):
    return lax.broadcasted_iota(jnp.int32, (rows, lanes), 0)


def normalize(values):
    center = values - jnp.mean(values, axis=-1, keepdims=True)
    inverse = lax.rsqrt(jnp.mean(center * center, axis=-1, keepdims=True) + EPSILON)
    return center * inverse, inverse


def norm_backward(upstream, normed, inverse, gain_row):
    scaled = upstream * gain_row
    mean_plain = jnp.mean(scaled, axis=-1, keepdims=True)
    mean_normed = jnp.mean(scaled * normed, axis=-1, keepdims=True)
    return inverse * (scaled - mean_plain - normed * mean_normed)


def norm_rows(tail, experts):
    picks = (lane_of(8) == row_of(8) + experts).astype(F32).astype(BF)
    return dot_last(picks, tail)


def places_kernel(experts, capacity, cols_ref, rows_ref, cot_ref, *out_refs):
    tokens = cols_ref.shape[1]
    slots = experts * capacity
    square_row = lax.broadcasted_iota(jnp.int32, (tokens, tokens), 0)
    square_col = lax.broadcasted_iota(jnp.int32, (tokens, tokens), 1)
    earlier = (square_col < square_row).astype(F32).astype(BF)
    later = (square_row < square_col).astype(F32).astype(BF)
    wide = max(16, experts)
    for layer_at in range(LAYERS):
        to_tokens, to_slots = out_refs[4 * layer_at : 4 * layer_at + 2], out_refs[
            4 * layer_at + 2 : 4 * layer_at + 4
        ]
        cols = cols_ref[layer_at]
        first, second = cols[:, 0:1], cols[:, 1:2]
        lane = lane_of(tokens)
        matches = jnp.where((lane == first) | (lane == second), 1.0, 0.0)
        before = dot(earlier, matches.astype(BF))
        slot_lane = lax.broadcasted_iota(jnp.int32, (tokens, slots), 1)
        for chosen, out_ref in zip((first, second), to_tokens):
            rank = jnp.sum(jnp.where(lane == chosen, before, 0.0), axis=1, keepdims=True)
            slot = chosen * capacity + rank.astype(jnp.int32)
            out_ref[...] = jnp.where(slot_lane == slot, 1.0, 0.0).astype(BF)
        rows = rows_ref[layer_at]
        first, second = rows[0:1], rows[1:2]
        which = lax.broadcasted_iota(jnp.int32, (wide, tokens), 0)
        matches = jnp.where((which == first) | (which == second), 1.0, 0.0)
        before = dot(matches.astype(BF), later)
        slot_row = lax.broadcasted_iota(jnp.int32, (slots, tokens), 0)
        for chosen, out_ref in zip((first, second), to_slots):
            rank = jnp.sum(jnp.where(which == chosen, before, 0.0), axis=0, keepdims=True)
            slot = chosen * capacity + rank.astype(jnp.int32)
            out_ref[...] = jnp.where(slot_row == slot, 1.0, 0.0).astype(BF)
    for at, out_ref in enumerate(out_refs[4 * LAYERS :]):
        columns = out_ref.shape[1]
        cot = cot_ref[:, at * columns : (at + 1) * columns]
        out_ref[...] = (dot(to_slots[0][...], cot) + dot(to_slots[1][...], cot)).astype(BF)


def two_parts(values):
    high = values.astype(BF)
    return high, (values - high.astype(F32)).astype(BF)


def two_lanes(values):
    high, low = two_parts(values)
    lane = lane_of(values.shape[0])
    high, low = high.astype(F32), low.astype(F32)
    return jnp.where(lane == 0, high, jnp.where(lane == 1, low, 0.0)).astype(BF)


def from_lanes(parts):
    return parts[:, 0:1] + parts[:, 1:2]


def behind(kernel, operands, *refs):
    return kernel(*refs[operands:])


def call(kernel, out_shapes, args, flops, scratch=(), after=()):
    moved = sum(a.size * a.dtype.itemsize for a in args) + sum(
        int(np.prod(o.shape)) * o.dtype.itemsize for o in out_shapes
    )
    whole = pl.BlockSpec(memory_space=pltpu.VMEM)
    return pl.pallas_call(
        functools.partial(behind, kernel, len(after)),
        in_specs=[pl.BlockSpec(memory_space=pl.ANY)] * len(after) + [whole] * len(args),
        out_shape=out_shapes,
        scratch_shapes=list(scratch),
        compiler_params=pltpu.CompilerParams(vmem_limit_bytes=VMEM),
        cost_estimate=pl.CostEstimate(
            flops=int(flops), bytes_accessed=int(moved), transcendentals=0
        ),
    )(*after, *args)


def shape(dims, dtype):
    return jax.ShapeDtypeStruct(dims, dtype)


def half_masks():
    lane = lane_of(1)
    return (
        jnp.where(lane < HEAD_DIM, 1.0, 0.0).astype(BF),
        jnp.where(lane < HEAD_DIM, 0.0, 1.0).astype(BF),
    )


def dense_forward_kernel(experts, images, combine, last, *refs):
    refs = list(refs)
    take = lambda: refs.pop(0)
    x_ref = take()
    if combine:
        back_ref, take_first, take_second, gates_before = take(), take(), take(), take()
    full_ref, to_first, to_second, cols_ref = take(), take(), take(), take()
    if combine:
        x_out, first_out, second_out = take(), take(), take()
    x1_out, qkv_out, mixed_out, lse_out, probs_out, gates_out, send_out, top_out = (
        take() for _ in range(8)
    )
    if last:
        send_gates_out = take()
    tokens, width = x_ref.shape
    rows_of = tokens // images
    x = x_ref[...]
    if combine:
        back = back_ref[...]
        first = dot(take_first[...], back)
        second = dot(take_second[...], back)
        gates = gates_before[...]
        x = x + (gates[:, 0:1] * first + gates[:, 1:2] * second)
        x_out[...] = x
        first_out[...] = first.astype(BF)
        second_out[...] = second.astype(BF)
    tail = full_ref[:, 4 * width :]
    norms = norm_rows(tail, experts)
    unit, _ = normalize(x)
    n1 = (unit * norms[0:1] + norms[2:3]).astype(BF)
    qkv_out[...] = dot(n1, full_ref[:, : 3 * width]).astype(BF)
    masks = half_masks()
    key_at = lax.broadcasted_iota(jnp.int32, (rows_of, rows_of), 1)
    query_at = lax.broadcasted_iota(jnp.int32, (rows_of, 1), 0)
    lane = lane_of(rows_of)
    top_lane = lane_of(8)
    tops = jnp.full((8, LANES), -jnp.inf, F32)
    scale = HEAD_DIM**-0.5
    for image in range(images):
        rows = slice(image * rows_of, (image + 1) * rows_of)
        lse = jnp.zeros((rows_of, LANES), F32)
        for pair in range(HEADS // 2):
            at = pair * LANES
            q = qkv_out[rows, at : at + LANES]
            k = qkv_out[rows, width + at : width + at + LANES]
            v = qkv_out[rows, 2 * width + at : 2 * width + at + LANES]
            mixed = None
            for half in range(2):
                scores = dot_last(q * masks[half], k) * scale
                scores = jnp.where(key_at < SEQ, scores, -jnp.inf)
                highest = jnp.max(scores, axis=-1, keepdims=True)
                top = jnp.max(
                    jnp.where(query_at < SEQ, highest, -jnp.inf), axis=0, keepdims=True
                )
                weights = jnp.exp(scores - highest)
                total = jnp.sum(weights, axis=-1, keepdims=True)
                weights = (weights * (1.0 / total)).astype(BF)
                part = dot(weights, v * masks[half])
                mixed = part if mixed is None else mixed + part
                head = 2 * pair + half
                lse = jnp.where(lane == head, highest + jnp.log(total), lse)
                tops = jnp.where(top_lane == head, jnp.maximum(tops, top), tops)
            mixed_out[rows, at : at + LANES] = mixed.astype(BF)
        lse_out[rows, :] = lse
    top_out[...] = tops
    x1 = x + dot(mixed_out[...], full_ref[:, 3 * width : 4 * width])
    x1_out[...] = x1
    unit, _ = normalize(x1)
    n2 = (unit * norms[1:2] + norms[3:4]).astype(BF)
    lane = lane_of(tokens)
    logits = jnp.where(lane < experts, dot(n2, tail), -jnp.inf)
    probs = jnp.exp(logits - jnp.max(logits, axis=-1, keepdims=True))
    probs = probs / jnp.sum(probs, axis=-1, keepdims=True)
    probs_out[...] = probs
    first, second = cols_ref[:, 0:1], cols_ref[:, 1:2]
    picked = [
        jnp.sum(jnp.where(lane == chosen, probs, 0.0), axis=1, keepdims=True)
        for chosen in (first, second)
    ]
    total = jnp.where(first >= 0, picked[0] + picked[1], 1.0)
    gates = [one / total for one in picked]
    packed = jnp.zeros((tokens, LANES), F32)
    for at, column in enumerate((gates[0], gates[1], total, picked[0], picked[1])):
        packed = jnp.where(lane == at, column, packed)
    gates_out[...] = packed
    send_out[...] = dot(to_first[...] + to_second[...], n2).astype(BF)
    if last:
        send_gates_out[...] = (
            dot(to_first[...], two_lanes(gates[0])) + dot(to_second[...], two_lanes(gates[1]))
        ).astype(BF)


def expert_forward_kernel(last, *refs):
    refs = list(refs)
    if last:
        grad_refs, inner_out = (refs.pop(0), refs.pop(0)), refs.pop()
    rows_ref, win_ref, wout_ref, active_out, slope_out, out_ref = refs
    units = win_ref.shape[1] // 2
    factor = (2.0 / np.pi) ** 0.5
    rows = rows_ref[...]
    hidden = dot(rows, win_ref[:, :units])
    total = before = None
    for piece in range(2):
        at = slice(piece * units, (piece + 1) * units)
        later = dot(rows, win_ref[:, units:]) if piece == 0 else None
        square = hidden * hidden
        gate = 0.5 + 0.5 * jnp.tanh(hidden * (factor + (0.044715 * factor) * square))
        active = hidden * gate
        slope = active * (2 * factor + (6 * 0.044715 * factor) * square)
        slope_out[:, at] = (gate + slope * (1.0 - gate)).astype(BF)
        active = active.astype(BF)
        active_out[:, at] = active
        if piece == 1:
            total = dot(before, wout_ref[:units, :]) + dot(active, wout_ref[units:, :])
        before, hidden = active, later
    total = total.astype(BF)
    out_ref[...] = total
    if last:
        half = total.shape[1] // 2
        inner_out[...] = two_lanes(
            jnp.sum(
                total[:, :half].astype(F32) * grad_refs[0][...].astype(F32)
                + total[:, half:].astype(F32) * grad_refs[1][...].astype(F32),
                axis=1,
                keepdims=True,
            )
        )


def weight_spec(weight, layer_at):
    if weight.ndim == 4:
        return pl.BlockSpec((None, None) + weight.shape[2:], lambda i: (layer_at, 0, 0, 0))
    return pl.BlockSpec(weight.shape, lambda i: (0, 0))


def expert_forward(layer_at, grads, rows_in, weight_in, weight_out, after=()):
    last = len(grads) > 0
    slots, width = rows_in.shape
    hidden_units = weight_in.shape[-1]
    chunk = slots // 4
    return pl.pallas_call(
        functools.partial(behind, functools.partial(expert_forward_kernel, last), len(after)),
        grid=(4,),
        in_specs=[pl.BlockSpec(memory_space=pl.ANY)] * len(after)
        + [pl.BlockSpec((chunk, width // 2), lambda i: (i, 0))] * len(grads)
        + [
            pl.BlockSpec((chunk, width), lambda i: (i, 0)),
            weight_spec(weight_in, layer_at),
            weight_spec(weight_out, layer_at),
        ],
        out_specs=[
            pl.BlockSpec((chunk, hidden_units), lambda i: (i, 0)),
            pl.BlockSpec((chunk, hidden_units), lambda i: (i, 0)),
            pl.BlockSpec((chunk, width), lambda i: (i, 0)),
        ]
        + [pl.BlockSpec((chunk, LANES), lambda i: (i, 0))] * last,
        out_shape=[
            shape((slots, hidden_units), BF),
            shape((slots, hidden_units), BF),
            shape((slots, width), BF),
        ]
        + [shape((slots, LANES), BF)] * last,
        compiler_params=pltpu.CompilerParams(vmem_limit_bytes=VMEM_EX),
        cost_estimate=pl.CostEstimate(
            flops=4 * slots * width * hidden_units,
            bytes_accessed=slots * (hidden_units * 4 + width * 4) + 4 * width * hidden_units,
            transcendentals=slots * hidden_units,
        ),
    )(*after, *grads, rows_in, weight_in, weight_out)


def expert_backward_kernel(gated, *refs):
    refs = list(refs)
    grad_ref = refs.pop(0)
    if gated:
        second_ref, gates_ref, scaled = refs.pop(0), refs.pop(0), refs.pop()
        gates = from_lanes(gates_ref[...].astype(F32))
        half = grad_ref.shape[1]
        scaled[:, :half] = (gates * grad_ref[...].astype(F32)).astype(BF)
        scaled[:, half:] = (gates * second_ref[...].astype(F32)).astype(BF)
        grad_ref = scaled
    slope_ref, win_ref, wout_ref, hidden_out, out_ref = refs
    units = win_ref.shape[1] // PIECES
    for piece in range(PIECES):
        at = slice(piece * units, (piece + 1) * units)
        grad_active = dot_last(grad_ref[...], wout_ref[at, :])
        hidden_out[:, at] = (grad_active * slope_ref[:, at].astype(F32)).astype(BF)
    out_ref[...] = dot_last(hidden_out[...], win_ref[...]).astype(BF)


def expert_backward(layer_at, grads, gates, slope, weight_in, weight_out):
    slots, width = grads[0].shape[0], weight_in.shape[-2]
    hidden_units = weight_in.shape[-1]
    chunk = slots // 4
    gated = len(gates)
    rows_spec = lambda lanes: pl.BlockSpec((chunk, lanes), lambda i: (i, 0))
    return pl.pallas_call(
        functools.partial(expert_backward_kernel, gated),
        grid=(4,),
        in_specs=[rows_spec(one.shape[1]) for one in grads]
        + [rows_spec(LANES)] * gated
        + [
            rows_spec(hidden_units),
            weight_spec(weight_in, layer_at),
            weight_spec(weight_out, layer_at),
        ],
        out_specs=[rows_spec(hidden_units), rows_spec(width)] + [rows_spec(width)] * gated,
        out_shape=[shape((slots, hidden_units), BF), shape((slots, width), BF)]
        + [shape((slots, width), BF)] * gated,
        compiler_params=pltpu.CompilerParams(vmem_limit_bytes=VMEM_EX),
        cost_estimate=pl.CostEstimate(
            flops=4 * slots * width * hidden_units,
            bytes_accessed=slots * (hidden_units * 4 + width * 4) + 4 * width * hidden_units,
            transcendentals=0,
        ),
    )(*grads, *gates, slope, weight_in, weight_out)


def expert_weights_kernel(rows_ref, hidden_ref, active_ref, grad_ref, in_out, out_out):
    in_out[0] = dot_first(rows_ref[...], hidden_ref[...]).astype(BF)
    out_out[0] = dot_first(active_ref[...], grad_ref[...]).astype(BF)


def expert_weights(rows_in, grad_hidden, active, grad_rows, pieces):
    slots, width = rows_in.shape
    hidden_units = active.shape[1]
    block = hidden_units // pieces
    return pl.pallas_call(
        expert_weights_kernel,
        grid=(pieces,),
        in_specs=[
            pl.BlockSpec((slots, width), lambda i: (0, 0)),
            pl.BlockSpec((slots, block), lambda i: (0, i)),
            pl.BlockSpec((slots, block), lambda i: (0, i)),
            pl.BlockSpec((slots, width), lambda i: (0, 0)),
        ],
        out_specs=[
            pl.BlockSpec((1, width, block), lambda i: (i, 0, 0)),
            pl.BlockSpec((1, block, width), lambda i: (i, 0, 0)),
        ],
        out_shape=[shape((pieces, width, block), BF), shape((pieces, block, width), BF)],
        compiler_params=pltpu.CompilerParams(vmem_limit_bytes=VMEM_EX),
        cost_estimate=pl.CostEstimate(
            flops=4 * slots * width * hidden_units,
            bytes_accessed=slots * (hidden_units * 4 + width * 4) + 4 * width * hidden_units,
            transcendentals=0,
        ),
    )(rows_in, grad_hidden, active, grad_rows)


def dense_backward_kernel(experts, images, last, first_layer, *refs):
    refs = list(refs)
    take = lambda: refs.pop(0)
    g_ref, rows_ref, take_first, take_second = take(), take(), take(), take()
    if last:
        inner_ref = take()
    else:
        first_ref, second_ref = take(), take()
    probs_ref, gates_ref, cols_ref, x_ref, x1_ref = (take() for _ in range(5))
    full_ref, qkv_ref, mixed_ref, lse_ref = (take() for _ in range(4))
    if not first_layer:
        to_first, to_second, gates_below = take(), take(), take()
    g_out, weights_out = take(), take()
    if not first_layer:
        send_out = take()
    grad_qkv = take()
    tokens, width = g_ref.shape
    rows_of = tokens // images
    g = g_ref[...]
    gates = gates_ref[...]
    x1 = x1_ref[...]
    if last:
        inner = inner_ref[...]
        grad_gates = [from_lanes(dot(one[...], inner)) for one in (take_first, take_second)]
    else:
        grad_gates = [
            jnp.sum(g * one[...].astype(F32), axis=1, keepdims=True)
            for one in (first_ref, second_ref)
        ]
    weighted = grad_gates[0] * gates[:, 0:1] + grad_gates[1] * gates[:, 1:2]
    amounts = [
        (grad_gates[at] - weighted) / gates[:, 2:3] * gates[:, 3 + at : 4 + at]
        for at in range(TOP)
    ]
    lane = lane_of(tokens)
    chosen = [jnp.where(lane == cols_ref[:, at : at + 1], amounts[at], 0.0) for at in range(TOP)]
    grad_logits = (
        (chosen[0] + chosen[1]) - probs_ref[...] * (amounts[0] + amounts[1])
    ).astype(BF)
    tail = full_ref[:, 4 * width :]
    norms = norm_rows(tail, experts)
    rows = rows_ref[...]
    grad_n2 = dot(take_first[...] + take_second[...], rows) + dot_last(grad_logits, tail)
    unit2, inverse2 = normalize(x1)
    n2 = (unit2 * norms[1:2] + norms[3:4]).astype(BF)
    grad_x1 = g + norm_backward(grad_n2, unit2, inverse2, norms[1:2])
    grad_attn = grad_x1.astype(BF)
    grad_mixed = dot_last(grad_attn, full_ref[:, 3 * width : 4 * width]).astype(BF)
    masks = half_masks()
    key_at = lax.broadcasted_iota(jnp.int32, (rows_of, rows_of), 1)
    scale = HEAD_DIM**-0.5
    for image in range(images):
        rows = slice(image * rows_of, (image + 1) * rows_of)
        for pair in range(HEADS // 2):
            at = pair * LANES
            q = qkv_ref[rows, at : at + LANES]
            k = qkv_ref[rows, width + at : width + at + LANES]
            v = qkv_ref[rows, 2 * width + at : 2 * width + at + LANES]
            gm = grad_mixed[rows, at : at + LANES]
            sums = [None] * 3
            for half in range(2):
                head = 2 * pair + half
                mask = masks[half]
                scores = dot_last(q * mask, k) * scale
                weights = jnp.exp(scores - lse_ref[rows, head : head + 1])
                weights = jnp.where(key_at < SEQ, weights, 0.0)
                grad_weights = dot_last(gm * mask, v)
                inner = jnp.sum(grad_weights * weights, axis=-1, keepdims=True)
                grad_scores = (weights * (grad_weights - inner)).astype(BF)
                parts = (
                    dot(grad_scores, k * mask),
                    dot_first(grad_scores, q * mask),
                    dot_first(weights.astype(BF), gm * mask),
                )
                sums = [b if a is None else a + b for a, b in zip(sums, parts)]
            grad_qkv[rows, at : at + LANES] = (sums[0] * scale).astype(BF)
            grad_qkv[rows, width + at : width + at + LANES] = (sums[1] * scale).astype(BF)
            grad_qkv[rows, 2 * width + at : 2 * width + at + LANES] = sums[2].astype(BF)
    unit1, inverse1 = normalize(x_ref[...])
    n1 = (unit1 * norms[0:1] + norms[2:3]).astype(BF)
    grad_n1 = dot_last(grad_qkv[...], full_ref[:, : 3 * width])
    g_below = grad_x1 + norm_backward(grad_n1, unit1, inverse1, norms[0:1])
    g_out[...] = g_below
    if not first_layer:
        gates = gates_below[...]
        send_out[...] = (
            dot(to_first[...], (gates[:, 0:1] * g_below).astype(BF))
            + dot(to_second[...], (gates[:, 1:2] * g_below).astype(BF))
        ).astype(BF)
    weights_out[:, : 3 * width] = dot_first(n1, grad_qkv[...]).astype(BF)
    weights_out[:, 3 * width : 4 * width] = dot_first(mixed_ref[...], grad_attn).astype(BF)
    row = lax.broadcasted_iota(jnp.int32, (8, width), 0)
    norm_grads = jnp.zeros((8, width), F32)
    for at, total in enumerate((grad_n1 * unit1, grad_n2 * unit2, grad_n1, grad_n2)):
        norm_grads = jnp.where(row == at, jnp.sum(total, axis=0, keepdims=True), norm_grads)
    picks = (lane_of(8) == row_of(8) + experts).astype(F32).astype(BF)
    weights_out[:, 4 * width :] = (
        dot_first(n2, grad_logits) + dot_first(norm_grads.astype(BF), picks)
    ).astype(BF)


def combine_kernel(images, x1_ref, gates_ref, take_first, take_second, back_ref, out_ref):
    back = back_ref[...]
    gates = gates_ref[...]
    out = x1_ref[...] + (
        gates[:, 0:1] * dot(take_first[...], back) + gates[:, 1:2] * dot(take_second[...], back)
    )
    out_ref[...] = out


def pack_kernel(experts, qkv_ref, o_ref, router_ref, gains_ref, biases_ref, *out_refs):
    width = o_ref.shape[2]
    router_lanes = (lane_of(experts) == row_of(experts)).astype(F32).astype(BF)
    gains_lanes = (lane_of(2) == row_of(2) + experts).astype(F32).astype(BF)
    biases_lanes = (lane_of(2) == row_of(2) + experts + 2).astype(F32).astype(BF)
    for at, out_ref in enumerate(out_refs):
        out_ref[:, : 3 * width] = qkv_ref[at]
        out_ref[:, 3 * width : 4 * width] = o_ref[at]
        out_ref[:, 4 * width :] = (
            dot_first(router_ref[at], router_lanes)
            + dot_first(gains_ref[at], gains_lanes)
            + dot_first(biases_ref[at], biases_lanes)
        ).astype(BF)


def finish_kernel(experts, *refs):
    sums, outs = refs[:12], refs[12:]
    keep_ref, more_ref = sums[:2]
    qkv_out, o_out, router_out, gains_out, biases_out, second_out, in_out, wout_out = outs
    width = o_out.shape[2]
    picks = jnp.where(lane_of(8) == row_of(8) + experts, 1.0, 0.0)
    for at in range(LAYERS):
        dense = keep_ref[at].astype(F32) + more_ref[at].astype(F32)
        qkv_out[at] = dense[:, : 3 * width]
        o_out[at] = dense[:, 3 * width : 4 * width]
        tail = dense[:, 4 * width :]
        router_out[at] = tail[:, :experts]
        norms = lax.dot_general(
            picks, tail, (((1,), (1,)), ((), ())), precision=lax.Precision.HIGHEST
        )
        gains_out[at] = norms[0:2]
        biases_out[at] = norms[2:4]
        second_out[at : at + 1] = norms[3:4]
    for number, out_ref in enumerate((in_out, wout_out)):
        out_ref[0, 0] = sums[2 + number][...].astype(F32)
        for half in range(2):
            keep_ref, more_ref = sums[4 + 4 * number + 2 * half :][:2]
            rows = keep_ref.shape[0]
            at = slice(half * rows, (half + 1) * rows)
            out_ref[1, 0, at] = keep_ref[...].astype(F32) + more_ref[...].astype(F32)


def other(values, axis):
    return lax.ppermute(values, axis, [(0, 1), (1, 0)])


def across(values, core_axis, axis):
    if axis < core_axis:
        return lax.ppermute(values, (axis, core_axis), [(1, 3), (3, 1)])
    return lax.ppermute(values, (core_axis, axis), [(2, 3), (3, 2)])


def expert_sent(weight, split_at, dp_axes, ex_axes):
    row_axes = dp_axes[:-1]
    size = weight.shape[split_at] // 2 ** len(row_axes)
    place = lax.axis_index(row_axes) if row_axes else 0
    own = lax.dynamic_slice_in_dim(weight, place * size, size, split_at)
    return across(own, dp_axes[-1], ex_axes[0])


def expert_others(got, dp_axes):
    got = [got]
    for axis in dp_axes[:-1][::-1]:
        got = got + [across(one, dp_axes[-1], axis) for one in got]
    return got


def expert_joined(weight, got, split_at, dp_axes):
    row_axes = dp_axes[:-1]
    place = lax.axis_index(row_axes) if row_axes else 0
    first = lax.axis_index(dp_axes[-1]) == 0
    size = weight.shape[split_at] // len(got)
    blocks = []
    for at in range(len(got)):
        theirs = got[at]
        for p, one in enumerate(got):
            theirs = jnp.where(place == at ^ p, one, theirs)
        own = lax.slice_in_dim(weight, at * size, (at + 1) * size, axis=split_at)
        blocks.append(jnp.where(first, own, theirs))
    return jnp.concatenate(blocks, axis=split_at)


def returned_rows(pieces, dp_axes):
    row_axes = dp_axes[:-1]
    pieces = pieces.reshape((-1,) + pieces.shape[2:])
    pieces = lax.psum_scatter(pieces, row_axes, scatter_dimension=0, tiled=True)
    return pieces.reshape((2, -1) + pieces.shape[1:])


def returned_home(pieces, moved, core_axis):
    core = lax.axis_index(core_axis)
    mine = jnp.where(core == 0, pieces, moved)
    keep = lax.dynamic_index_in_dim(mine, core, 0, keepdims=False)
    send = lax.dynamic_index_in_dim(mine, 1 - core, 0, keepdims=False)
    return keep, other(send, core_axis)


def add_low(a, b):
    return (a.astype(F32) + b.astype(F32)).astype(BF)


def gather_step(whole, axis, milestone=None):
    theirs = other(whole, axis)
    if milestone is not None:
        theirs = tie(theirs, milestone)
    mine_first = lax.axis_index(axis) == 0
    return jnp.stack([jnp.where(mine_first, whole, theirs), jnp.where(mine_first, theirs, whole)])


def gathered(whole, axes, order):
    rows, columns = whole.shape[-2:]
    whole = whole.reshape((2,) * len(axes) + (rows, columns))
    places = tuple(order[::-1].index(axis) for axis in axes)
    whole = whole.transpose(places + (len(axes), len(axes) + 1))
    return whole.reshape(-1, columns)


def tie(values, milestone):
    return lax.optimization_barrier((values, milestone))[0]


def halves(values, left, axis, milestone=None):
    at = left.index(axis)
    mine = lax.axis_index(axis)
    keep = lax.dynamic_index_in_dim(values, mine, at, keepdims=False)
    theirs = other(lax.dynamic_index_in_dim(values, 1 - mine, at, keepdims=False), axis)
    if milestone is not None:
        theirs = tie(theirs, milestone)
    left.remove(axis)
    return keep, theirs


def halve(values, left, axis, milestone=None):
    return add_low(*halves(values, left, axis, milestone))


def body(
    dp_axes,
    ex_axes,
    x_in,
    norm_gains,
    norm_biases,
    w_qkv,
    w_o,
    w_router,
    w_in,
    w_out,
    routes,
    threshold,
    cotangent,
):
    axes = dp_axes + ex_axes
    group = dp_axes[-1:] + ex_axes[1:]
    order_out = ex_axes[::-1][1:] + ex_axes[-1:] + dp_axes
    order_in = dp_axes[-1:] + ex_axes[1:][::-1] + dp_axes[:-1][::-1] + ex_axes[:1]
    experts = 2 ** len(ex_axes)
    parts = 2 ** len(dp_axes)
    tokens, width = x_in.shape
    images = tokens // SEQ
    padded = up16(SEQ)
    capacity = -(-(4 * tokens // experts) // 8) * 8
    slots = experts * capacity
    total = images * padded

    def pad(values, fill=0):
        values = values.reshape((images, SEQ) + values.shape[1:])
        values = jnp.pad(
            values, ((0, 0), (0, padded - SEQ), (0, 0)), constant_values=fill
        )
        return values.reshape((total,) + values.shape[2:])

    def unpad(values):
        return values.reshape(images, padded, -1)[:, :SEQ].reshape(tokens, -1)

    shards = call(
        functools.partial(pack_kernel, experts),
        [shape((w_o.shape[1], 4 * width + LANES), BF)] * LAYERS,
        (w_qkv, w_o, w_router.transpose(0, 2, 1), norm_gains, norm_biases),
        1000,
    )
    def exchange(rows, at):
        over = group if MOVED[at] else ex_axes
        return lax.all_to_all(rows, over, split_axis=0, concat_axis=0, tiled=True)

    cols = [pad(routes[at], -1) for at in range(LAYERS)]
    half_away = lax.axis_index(ex_axes[0]) * (experts // 2)
    route_cols = jnp.stack(
        [
            pad((routes[at] + half_away) % experts if MOVED[at] else routes[at], -1)
            for at in range(LAYERS)
        ]
    )
    to_and_from = call(
        functools.partial(places_kernel, experts, capacity),
        [shape(s, BF) for s in ((total, slots),) * 2 + ((slots, total),) * 2] * LAYERS
        + [shape((slots, width // 2), BF)] * 2,
        (route_cols, route_cols.transpose(0, 2, 1), pad(cotangent)),
        LAYERS * 4 * total * total * LANES,
    )
    collect = [to_and_from[4 * at : 4 * at + 2] for at in range(LAYERS)]
    spread = [to_and_from[4 * at + 2 : 4 * at + 4] for at in range(LAYERS)]
    moved_at = LAYERS - 1
    whole = shards[0][None]
    for step, axis in enumerate(order_out):
        milestone = None if step < 2 else {2: (to_and_from, sent[0]), 3: sent[1]}.get(step)
        whole = gather_step(whole, axis, milestone)
        if step == 1:
            sent = [
                expert_sent(tie(one[moved_at, 0], whole), split_at, dp_axes, ex_axes)
                for one, split_at in ((w_in, 1), (w_out, 0))
            ]
    full = [gathered(whole, axes, order_out)]
    weights = [(w_in, w_out)] * LAYERS
    cot = pad(cotangent.astype(F32))
    current = pad(x_in.astype(F32))

    dense_flops = 2 * total * width * (4 * width) + 6 * total * slots * width
    kept = []
    tops = []
    back = gates = None
    for at in range(LAYERS):
        combine, last = at > 0, at == LAYERS - 1
        args = [current]
        outs = []
        if combine:
            args += [back, *collect[at - 1], gates]
            outs += [shape((total, width), F32), shape((total, width), BF), shape((total, width), BF)]
        args += [full[at], *spread[at], cols[at]]
        outs += [
            shape((total, width), F32),
            shape((total, 3 * width), BF),
            shape((total, width), BF),
            shape((total, LANES), F32),
            shape((total, LANES), F32),
            shape((total, LANES), F32),
            shape((slots, width), BF),
            shape((8, LANES), F32),
        ]
        if last:
            outs.append(shape((slots, LANES), BF))
        made = list(
            call(
                functools.partial(dense_forward_kernel, experts, images, combine, last),
                outs,
                args,
                dense_flops,
                after=weights[moved_at] if last else [],
            )
        )
        if combine:
            current, first, second = made[:3]
            made = made[3:]
            kept[-1]["routed"] = (first, second)
        x1, qkv, mixed, lse, probs, gates, send, top = made[:8]
        tops.append(top[0, :HEADS])
        rows = exchange(send if at == 0 else tie(send, cot_rows[1]), at)
        if at == 0:
            others = [expert_others(tie(one, send), dp_axes) for one in sent]
            ahead = [one for got in others for one in got]
            whole = tie(shards[1], whole)[None]
            for axis in order_out[:-1]:
                whole = gather_step(whole, axis)
            ahead.append(whole)
        if last:
            gate_rows = exchange(tie(made[8], rows), at)
            active, slope, out_rows, inner = expert_forward(at, cot_rows, rows, *weights[at])
        else:
            active, slope, out_rows = expert_forward(at, [], rows, *weights[at], ahead)
            cot_rows = [exchange(tie(to_and_from[-2], rows), LAYERS - 1)]
            back = exchange(tie(out_rows, cot_rows[0]), at)
            cot_rows.append(exchange(tie(to_and_from[-1], back), LAYERS - 1))
            full.append(
                gathered(gather_step(tie(whole, out_rows), order_out[-1]), axes, order_out)
            )
            weights[moved_at] = [
                expert_joined(one[moved_at, 0], tie(got, out_rows), split_at, dp_axes)
                for one, got, split_at in zip((w_in, w_out), others, (1, 0))
            ]
        kept.append(
            dict(
                x=current,
                x1=x1,
                qkv=qkv,
                mixed=mixed,
                lse=lse,
                probs=probs,
                gates=gates,
                rows=rows,
                active=active,
                slope=slope,
            )
        )
        current = x1
    tops = jnp.pad(jnp.concatenate(tops), (0, LANES - LAYERS * HEADS))
    upstream = cot
    expert_grads = [None] * LAYERS
    dense_grads = [None] * LAYERS
    for at in reversed(range(LAYERS)):
        own = kept[at]
        last, first_layer = at == LAYERS - 1, at == 0
        if last:
            inner = exchange(inner, at)
            grad_hidden, grad_back, grad_rows = expert_backward(
                at, cot_rows, [gate_rows], own["slope"], *weights[at]
            )
            grad_back = tie(grad_back, inner)
        else:
            grad_hidden, grad_back = expert_backward(
                at, [grad_rows], [], own["slope"], *weights[at]
            )
            grad_back = tie(grad_back, head_max)
        grad_back = exchange(grad_back, at)
        pieces = expert_weights(own["rows"], grad_hidden, own["active"], grad_rows, parts)
        if MOVED[at]:
            moved_pieces = [returned_rows(one, dp_axes) for one in pieces]
            moved_pieces = [half for one in moved_pieces for half in jnp.split(one, 2, axis=1)]
            out_rows = tie(out_rows, (grad_back, pieces))
        else:
            expert_grads[at] = [
                lax.psum_scatter(
                    one.reshape((-1,) + one.shape[2:]), dp_axes, scatter_dimension=0, tiled=True
                )
                for one in pieces
            ]
        if first_layer:
            moved_pieces = [tie(one, (grad_back, pieces)) for one in moved_pieces]
            crossed = [across(one, dp_axes[-1], ex_axes[0]) for one in moved_pieces]
        args = [upstream, grad_back, *collect[at]]
        if last:
            args.append(inner)
        else:
            args += own["routed"]
        args += [own["probs"], own["gates"], cols[at], own["x"], own["x1"]]
        args += [full[at], own["qkv"], own["mixed"], own["lse"]]
        outs = [shape((total, width), F32), shape((width, 4 * width + LANES), BF)]
        if not first_layer:
            args += [*spread[at - 1], kept[at - 1]["gates"]]
            outs.append(shape((slots, width), BF))
        made = list(
            call(
                functools.partial(dense_backward_kernel, experts, images, last, first_layer),
                outs,
                args,
                2 * dense_flops,
                [pltpu.VMEM((total, 3 * width), BF)],
                pieces,
            )
        )
        upstream, weight_grads = made[:2]
        if not first_layer:
            back = exchange(out_rows, at)
            grad_rows = exchange(tie(made[2], back), at - 1)
        weight_grads = weight_grads.reshape((2,) * len(axes) + (-1,) + weight_grads.shape[1:])
        if first_layer:
            first_left = list(axes)
            weight_grads = tie(weight_grads, crossed[0])
            weight_grads = halve(weight_grads, first_left, order_in[0])
            weight_grads = halve(weight_grads, first_left, order_in[1], crossed[1])
            both = jnp.stack([weight_grads, sums], axis=-3)
            both = halve(both, first_left, order_in[2], crossed[2])
            both = halve(both, first_left, order_in[3], crossed[3])
            for axis in order_in[4:-1]:
                both = halve(both, first_left, axis)
            dense = [
                one.reshape(LAYERS, -1, one.shape[-1])
                for one in halves(both, first_left, order_in[-1])
            ]
        else:
            left = list(axes)
            sums = halve(weight_grads, left, order_in[0])
            sums = halve(sums, left, order_in[1], grad_rows)
            [out_act] = call(
                functools.partial(combine_kernel, images),
                [shape((total, width), F32)],
                [own["x1"], own["gates"], *collect[at], back],
                4 * total * slots * width,
            )
            grad_rows = tie(grad_rows, (out_act, sums))
            everyone = 2 ** len(axes)
            tops = lax.all_to_all(
                jnp.broadcast_to(tie(tops, grad_rows), (everyone, LANES)),
                axes,
                split_axis=0,
                concat_axis=0,
                tiled=True,
            )
            head_max = jnp.max(tops, axis=0)[: LAYERS * HEADS].reshape(LAYERS, HEADS)
    home = [
        returned_home(one, tie(moved, both), dp_axes[-1])
        for one, moved in zip(moved_pieces, crossed)
    ]
    rows = w_o.shape[1]
    finished = call(
        functools.partial(finish_kernel, experts),
        [
            shape((LAYERS, rows, 3 * width), F32),
            shape((LAYERS, rows, width), F32),
            shape((LAYERS, rows, experts), F32),
            shape((LAYERS, 2, rows), F32),
            shape((LAYERS, 2, rows), F32),
            shape((LAYERS, rows), F32),
        ]
        + [shape((LAYERS, 1) + one.shape, F32) for one in expert_grads[0]],
        [*dense, *expert_grads[0], *(one for pair in home for one in pair)],
        1000,
    )
    grad_qkv, grad_o, grad_router, grad_gains, grad_biases, second, grad_in, grad_out = finished
    factor = jnp.sqrt(threshold / jnp.maximum(head_max, threshold))
    columns = jnp.repeat(factor, HEAD_DIM, axis=1)
    clipped_qk = (
        w_qkv[:, :, : 2 * width].astype(F32)
        * jnp.concatenate([columns, columns], axis=1)[:, None, :]
    )
    return (
        unpad(out_act),
        unpad(upstream),
        grad_gains,
        grad_biases,
        grad_qkv,
        grad_o,
        grad_router,
        grad_in,
        grad_out,
        head_max,
        clipped_qk,
        second,
    )


def solution(mesh):
    dp_bits = int(mesh.shape["dp"]).bit_length() - 1
    ex_bits = int(mesh.shape["expert"]).bit_length() - 1
    dp_axes = tuple(f"d{at}" for at in range(dp_bits))
    ex_axes = tuple(f"e{at}" for at in range(ex_bits))
    split = Mesh(mesh.devices.reshape((2,) * (dp_bits + ex_bits)), dp_axes + ex_axes)
    both = dp_axes + ex_axes
    in_specs = (
        P(both, None),
        P(None, None, both),
        P(None, None, both),
        P(None, both, None),
        P(None, both, None),
        P(None, both, None),
        P(None, ex_axes, None, None),
        P(None, ex_axes, None, None),
        P(None, both, None),
        P(),
        P(both, None),
    )
    out_specs = (
        P(both, None),
        P(both, None),
        P(None, None, both),
        P(None, None, both),
        P(None, both, None),
        P(None, both, None),
        P(None, both, None),
        P(None, ex_axes, None, dp_axes),
        P(None, ex_axes, dp_axes, None),
        P(),
        P(None, both, None),
        P(None, both),
    )
    return jax.shard_map(
        functools.partial(body, dp_axes, ex_axes),
        mesh=split,
        in_specs=in_specs,
        out_specs=out_specs,
        check_vma=False,
    )
```
